32 devices in a mesh: head: 2 (over x), clus: 16 (over z, y, core).
Axes of the slice: x: 2, y: 2, z: 4, core: 2. Of those that a mesh axis runs over, the one named last changes fastest.
Arguments:
- key_cache: bfloat16 [2, 16384, 1024], P('head', 'clus'), may hold values from -8 to 8
- value_cache: bfloat16 [2, 16384, 1024], P('head', 'clus'), may hold values from -6 to 6
- prompt_queries: bfloat16 [64, 8192], P(None, 'head'), may hold values from -64 to 64
- tile_cluster: int32 [8, 16, 2, 8, 1], P('head', 'clus'), may hold values from 0 to 15; in each aligned block of 16 rows (0 to 15, 16 to 31, ..., all dimensions but the last counted through in order) no two rows name the same one
- listed_clusters: int32 [8, 4, 4], P('head'), may hold values from 0 to 15, as said below
Outputs:
- attended: bfloat16 [64, 8192], P('clus', 'head')
The draws below stay inside these ranges and needn't reach their ends.
Inputs may be any that keep to these rules, and one draw needn't show every extreme that they name: `tile_cluster`: among the 16 tiles of one index of clus and one KV head (the aligned blocks of rows in the order head, clus, slab, tile), no cluster is named more than 1 times, and some block names one cluster exactly 1 times. `listed_clusters`: each row names 4 distinct clusters.
All inputs are finite; a program needn't handle non-finite values.
Results may differ from the reference program's by a relative error of at most 0.0085.
Values may be sent and summed in bfloat16 or wider, within the bound.
A program may use at most 64 MiB of HBM per device.

```python
import math
import jax
import jax.numpy as jnp
import numpy as np
from jax import lax

KVH = 8
DH = 128
GROUP = 8
TILE = 128
QUERIES = 64
QBLK = 16
TOKENS = 32768
SLABS = 2
OWNERS = 16
TPD = 8
TILES_DEV = 16
MOST = 1
LIST = 4
QBLOCKS = 4


def keys_base(key):
    full_shape = (SLABS, TOKENS // SLABS, KVH * DH)
    drawn = jax.random.normal(jax.random.fold_in(key, 11), full_shape, jnp.float32)
    return drawn


def draw_key_cache(key, part):
    return keys_base(key).astype(jnp.bfloat16)


def draw_prompt_queries(key, part):
    full_shape = (QUERIES, KVH, GROUP, DH)
    drawn = jax.random.normal(jax.random.fold_in(key, 21), full_shape, jnp.float32)
    return drawn.reshape(QUERIES, KVH * GROUP * DH).astype(jnp.bfloat16)


def draw_listed_clusters(key, part):
    subkeys = jax.random.split(jax.random.fold_in(key, 41), KVH * QBLOCKS)
    orders = jax.vmap(lambda subkey: jax.random.permutation(subkey, OWNERS))(subkeys)
    return orders[:, :LIST].reshape(KVH, QBLOCKS, LIST).astype(jnp.int32)


def level_of(stream_key, dims, shards, low, high):
    gain = 1.0
    for dim, shards_of in shards:
        heights = jax.random.uniform(jax.random.fold_in(jax.random.fold_in(stream_key, 6), dim), (shards_of,), jnp.float32, low / len(shards), high / len(shards))
        gain = gain * jnp.repeat(jnp.exp(heights), dims[dim] // shards_of).reshape((-1,) + (1,) * (len(dims) - 1 - dim))
    return gain


def assign_block(key, own, number, rows, amount, top, limit, slope):
    ranking = jax.random.permutation(key, amount)
    crowded, ordinary = portions_of(amount, rows * top, limit, slope, True), portions_of(amount, rows * top, limit, slope, False)
    places = jnp.arange(amount)

    def named(lengths, offset_by):
        used = int((lengths > 0).sum())
        fixed = max(1, used // 4)
        moved = fixed + (places - fixed + offset_by * (used - fixed)) % max(1, amount - fixed)
        return jnp.zeros((amount,), jnp.int32).at[ranking[jnp.where(places < fixed, places, moved)]].set(jnp.asarray(lengths, jnp.int32))

    lengths = jnp.where(number % 4 == 0, named(crowded, number // 4), named(ordinary, number - number // 4 - 1))
    mixed = jax.random.permutation(jax.random.fold_in(own, 3), amount)
    giver, sink = mixed[0:amount // 2 * 2:2], mixed[1:amount // 2 * 2:2]
    margin = jnp.minimum(lengths[giver] - 1, limit - lengths[sink]) // 2
    margin = jnp.where((giver == ranking[0]) | (sink == ranking[0]) | (lengths[sink] == 0), 0, jnp.maximum(margin, 0))
    moved = jax.random.randint(jax.random.fold_in(own, 4), (amount // 2,), 0, 1 << 20) % (margin + 1)
    lengths = lengths.at[giver].add(-moved).at[sink].add(moved)
    members = jnp.searchsorted(jnp.cumsum(lengths), jnp.arange(rows * top), side="right").astype(jnp.int32)
    table = members.reshape(top, rows).T
    table = table[jax.random.permutation(jax.random.fold_in(own, 1), rows)]
    offset_by = jax.random.randint(jax.random.fold_in(own, 2), (rows, 1), 0, top)
    return jnp.take_along_axis(table, (jnp.arange(top)[None, :] + offset_by) % top, axis=1)


def portions_of(count, total, bound, slope, full):
    weights = [(1 << 20) // math.isqrt(standing ** slope) + 1 for standing in range(1, count + 1)]
    largest = bound if full else min(bound, max(-(-total // count), total * weights[0] // sum(weights)))
    least = 1 if total - largest >= count - 1 else 0
    holding, surplus = [largest] + [least] * (count - 1), total - largest - least * (count - 1)
    while surplus > 0:
        movable = [i for i in range(1, count) if holding[i] < largest] or [i for i in range(1, count) if holding[i] < bound]
        whole, budget = sum([weights[i] for i in movable]), surplus
        for i in movable:
            extra = min(bound - holding[i], max(1, budget * weights[i] // whole), surplus)
            holding[i] = holding[i] + extra
            surplus = surplus - extra
    return np.array(holding)


def bell_draw(own_key, extent, width, most, pieces=(), held_as=jnp.bfloat16):
    values = jax.random.normal(own_key, extent, jnp.float32) * width
    if len(pieces) > 0:
        values = level_of(own_key, extent, pieces, -0.22, 0.18) * values
    return jnp.clip(values, min=-most, max=most).astype(held_as)


def setup_inputs(seed: int = 0) -> dict:
    splits = jax.random.split(jax.random.key(seed), 6)
    key_cache = draw_key_cache(jax.random.fold_in(splits[5], 71), 0)
    value_cache = bell_draw(splits[1], (SLABS, TOKENS // SLABS, KVH * DH), 1.0, 6.0, ((0, 2), (1, 16)))
    prompt_queries = draw_prompt_queries(jax.random.fold_in(splits[5], 71), 0)
    tile_cluster_keys = jax.random.split(jax.random.fold_in(splits[3], 1), KVH * OWNERS * SLABS * TPD // TILES_DEV)
    tile_cluster_turns = jax.random.permutation(jax.random.fold_in(splits[3], 3), KVH * OWNERS * SLABS * TPD // TILES_DEV)
    tile_cluster = jax.vmap(lambda own, number: assign_block(jax.random.fold_in(splits[3], 2), own, number, TILES_DEV, OWNERS, 1, MOST, 2))(tile_cluster_keys, tile_cluster_turns).reshape((KVH, OWNERS, SLABS, TPD, 1))
    listed_clusters = draw_listed_clusters(jax.random.fold_in(splits[5], 71), 0)
    return {"key_cache": key_cache, "value_cache": value_cache, "prompt_queries": prompt_queries, "tile_cluster": tile_cluster, "listed_clusters": listed_clusters}


floor_value = -1.0e30
highest = lax.Precision.HIGHEST


def reference(key_cache, value_cache, prompt_queries, tile_cluster, listed_clusters):
    tiles_all = SLABS * OWNERS * TPD
    key_tiles = key_cache.reshape(tiles_all, TILE, KVH, DH)
    value_tiles = value_cache.reshape(tiles_all, TILE, KVH, DH)
    query_heads = prompt_queries.reshape(QUERIES, KVH, GROUP, DH)
    cluster_ids = jnp.transpose(tile_cluster[..., 0], (0, 2, 1, 3)).reshape(KVH, tiles_all).astype(jnp.int32)
    column_ids = jnp.arange(OWNERS, dtype=jnp.int32)
    score_scale = DH ** -0.5

    def per_head(head_index):
        key_rows = lax.dynamic_index_in_dim(key_tiles, head_index, 2, keepdims=False)
        value_rows = lax.dynamic_index_in_dim(value_tiles, head_index, 2, keepdims=False)
        head_ids = lax.dynamic_index_in_dim(cluster_ids, head_index, 0, keepdims=False)
        member = (head_ids[:, None] == column_ids[None, :]).astype(jnp.float32)
        counts = TILE * jnp.sum(member, axis=0)
        key_sum = jnp.dot(member.T, jnp.sum(key_rows.astype(jnp.float32), axis=1), precision=highest)
        value_sum = jnp.dot(member.T, jnp.sum(value_rows.astype(jnp.float32), axis=1), precision=highest)
        key_mean = key_sum / jnp.maximum(counts, 1.0)[:, None]
        listed_head = lax.dynamic_index_in_dim(listed_clusters, head_index, 0, keepdims=False)
        listed_mask = jnp.max((listed_head[:, :, None] == column_ids[None, None, :]).astype(jnp.float32), axis=1)
        query_rows = lax.dynamic_index_in_dim(query_heads, head_index, 1, keepdims=False)
        query_rows = query_rows.reshape(QBLOCKS, QBLK * GROUP, DH)
        flat_keys = key_rows.reshape(tiles_all * TILE, DH)
        flat_values = value_rows.reshape(tiles_all * TILE, DH)

        def per_block(block_inputs):
            block_queries, block_listed = block_inputs
            key_mask = jnp.repeat(jnp.dot(member, block_listed, precision=highest), TILE) > 0.5
            scores = jnp.einsum("rd,kd->rk", block_queries, flat_keys, preferred_element_type=jnp.float32) * score_scale
            approx_score = jnp.dot(block_queries.astype(jnp.float32), key_mean.T, precision=highest) * score_scale
            approx_live = (block_listed < 0.5) & (counts > 0.5)
            row_top = jnp.maximum(
                jnp.max(jnp.where(key_mask[None, :], scores, floor_value), axis=1),
                jnp.max(jnp.where(approx_live[None, :], approx_score, floor_value), axis=1))
            weights = jnp.where(key_mask[None, :], jnp.exp(scores - row_top[:, None]), 0.0)
            probabilities = weights.astype(jnp.bfloat16)
            approx_weight = jnp.where(approx_live[None, :], jnp.exp(approx_score - row_top[:, None]), 0.0)
            row_total = jnp.sum(weights, axis=1) + jnp.dot(approx_weight, counts, precision=highest)
            numerator = jnp.dot(probabilities, flat_values, preferred_element_type=jnp.float32)
            numerator = numerator + jnp.dot(approx_weight, value_sum, precision=highest)
            return numerator / row_total[:, None]

        blocks_out = lax.map(per_block, (query_rows, listed_mask))
        return blocks_out.reshape(QUERIES, GROUP, DH)

    outputs = lax.map(per_head, jnp.arange(KVH, dtype=jnp.int32))
    return jnp.transpose(outputs, (1, 0, 2, 3)).reshape(QUERIES, KVH * GROUP * DH).astype(jnp.bfloat16)
```

```python
import functools
import math

import jax
import jax.numpy as jnp
from jax import lax
from jax.experimental import pallas as pl
from jax.experimental.pallas import tpu as pltpu
from jax.sharding import PartitionSpec as P

DH = 128
GROUP = 8
TILE = 128
QBLK = 16


floor_value = -1e30
highest = lax.Precision.HIGHEST


def combined_all(shard, axis, combine):
    everything = jax.tree.map(lambda part: lax.all_gather(part, axis), shard)
    leading = jax.tree.map(lambda part: part[0], everything)

    def turn(k, so_far):
        return combine(so_far, jax.tree.map(lambda part: part[k], everything))

    return lax.fori_loop(1, lax.axis_size(axis), turn, leading)


def block_partials(
    query_blocks, key_rows, value_rows, tile_mask, key_mean, value_sum, counts_mine, approx_on
):
    score_scale = key_rows.shape[-1] ** (-0.5)
    tile_rows = key_rows.shape[0] // tile_mask.shape[-1]

    def one_block(block_inputs):
        block_queries, mask_tiles, approx_flag = block_inputs
        key_mask = jnp.repeat(mask_tiles, tile_rows) > 0.5
        scores = (
            jnp.einsum("rd,kd->rk", block_queries, key_rows, preferred_element_type=jnp.float32)
            * score_scale
        )
        approx_score = (
            jnp.dot(block_queries.astype(jnp.float32), key_mean, precision=highest) * score_scale
        )
        approx_live = approx_flag > 0.5
        row_top = jnp.maximum(
            jnp.max(jnp.where(key_mask[None, :], scores, floor_value), axis=1),
            jnp.where(approx_live, approx_score, floor_value),
        )
        weights = jnp.where(key_mask[None, :], jnp.exp(scores - row_top[:, None]), 0.0)
        probabilities = weights.astype(jnp.bfloat16)
        approx_weight = jnp.where(approx_live, jnp.exp(approx_score - row_top), 0.0)
        row_total = jnp.sum(weights, axis=1) + counts_mine * approx_weight
        numerator = jnp.dot(probabilities, value_rows, preferred_element_type=jnp.float32)
        numerator = numerator + approx_weight[:, None] * value_sum[None, :]
        return (row_top, row_total, numerator)

    return lax.map(one_block, (query_blocks, tile_mask, approx_on))


def combine_parts(first_part, second_part):
    top_first, total_first, numer_first = first_part
    top_second, total_second, numer_second = second_part
    joined = jnp.maximum(top_first, top_second)
    factor_first = jnp.exp(top_first - joined)
    factor_second = jnp.exp(top_second - joined)
    return (
        joined,
        total_first * factor_first + total_second * factor_second,
        numer_first * factor_first[..., None] + numer_second * factor_second[..., None],
    )


def local(key_cache, value_cache, prompt_queries, tile_cluster, listed_clusters):
    owners = lax.axis_size("clus")
    owner_index = lax.axis_index("clus")
    moved_keys, moved_values = (
        lax.all_to_all(key_cache, "head", split_axis=2, concat_axis=0, tiled=True),
        lax.all_to_all(value_cache, "head", split_axis=2, concat_axis=0, tiled=True),
    )
    slab_count, slab_rows, feature_width = moved_keys.shape
    heads_dev = feature_width // DH
    tiles_dev = slab_count * slab_rows // TILE

    def to_tiles(moved):
        shaped = moved.reshape(slab_count, slab_rows // TILE, TILE, heads_dev, DH)
        return shaped.transpose(3, 0, 1, 2, 4).reshape(heads_dev, tiles_dev, TILE, DH)

    key_tiles = to_tiles(moved_keys)
    value_tiles = to_tiles(moved_values)
    cluster_ids = tile_cluster.reshape(heads_dev, tiles_dev)
    column_ids = jnp.arange(owners, dtype=jnp.int32)
    member = (cluster_ids[:, :, None] == column_ids[None, None, :]).astype(jnp.float32)
    listed_mask = jnp.max(
        (listed_clusters[:, :, :, None] == column_ids).astype(jnp.float32), axis=2
    )
    owner_hot = (column_ids == owner_index).astype(jnp.float32)
    mine_listed = jnp.einsum("hbc,c->hb", listed_mask, owner_hot, precision=highest)
    query_count = prompt_queries.shape[0]
    block_count = query_count // QBLK
    query_blocks = prompt_queries.reshape(query_count, heads_dev, GROUP, DH).transpose(1, 0, 2, 3)
    query_blocks = query_blocks.reshape(heads_dev, block_count, QBLK * GROUP, DH)
    key_rows = key_tiles.reshape(heads_dev, tiles_dev * TILE, DH)
    value_rows = value_tiles.reshape(heads_dev, tiles_dev * TILE, DH)
    unit_rows = jnp.ones((TILE,), jnp.bfloat16)
    tile_keys = jnp.einsum("htrd,r->htd", key_tiles, unit_rows, preferred_element_type=jnp.float32)
    tile_values = jnp.einsum(
        "htrd,r->htd", value_tiles, unit_rows, preferred_element_type=jnp.float32
    )
    local_keys = jnp.einsum("htc,htd->hcd", member, tile_keys, precision=highest)
    local_values = jnp.einsum("htc,htd->hcd", member, tile_values, precision=highest)
    local_counts = TILE * jnp.sum(member, axis=1)
    total_keys, total_values, total_counts = lax.psum(
        (local_keys, local_values, local_counts), "clus"
    )
    key_sum = jnp.einsum("hcd,c->hd", total_keys, owner_hot, precision=highest)
    value_sum = jnp.einsum("hcd,c->hd", total_values, owner_hot, precision=highest)
    counts_mine = jnp.einsum("hc,c->h", total_counts, owner_hot, precision=highest)
    tile_mask = jnp.einsum("hbc,htc->hbt", listed_mask, member, precision=highest)
    key_mean = key_sum / jnp.maximum(counts_mine, 1.0)[:, None]
    approx_on = (1.0 - mine_listed) * (counts_mine > 0.5).astype(jnp.float32)[:, None]
    row_top, row_total, numerator = jax.vmap(block_partials)(
        query_blocks, key_rows, value_rows, tile_mask, key_mean, value_sum, counts_mine, approx_on
    )
    row_top = row_top.reshape(heads_dev, query_count, GROUP)
    row_total = row_total.reshape(heads_dev, query_count, GROUP)
    numerator = numerator.reshape(heads_dev, query_count, GROUP, DH)
    share_rows = query_count // owners
    merged_top, merged_total, merged_numer = combined_all(
        (row_top, row_total, numerator), "clus", combine_parts
    )
    kept_total = lax.dynamic_slice_in_dim(merged_total, owner_index * share_rows, share_rows, 1)
    kept_numer = lax.dynamic_slice_in_dim(merged_numer, owner_index * share_rows, share_rows, 1)
    attended = kept_numer / kept_total[..., None]
    return (
        attended.transpose(1, 0, 2, 3)
        .reshape(share_rows, heads_dev * GROUP * DH)
        .astype(jnp.bfloat16)
    )


MESH = pl.DeviceIdType.MESH
dead = -1e30
lowest_top = -1e9
log2_scale = math.log2(math.e) * DH**-0.5
nt = (((1,), (1,)), ((), ()))


def fast_kernel(
    k_hbm, v_hbm, q_ref, bt_ref, a_ref, ab_ref, out_ref,
    kbuf, vbuf, qx, btx, ax, bias, o_buf, st_buf, o_rx, st_rx,
    ts_buf, ts_rx, cs_buf, cs_rx, red_buf, tot_rx, wt,
    loc_sem, kv_send, kv_recv, in_send, in_recv,
    o_send, o_recv, st_send, st_recv, ts_sem, cs_send, cs_recv, tot_send, tot_recv,
):
    x, i = lax.axis_index("head"), lax.axis_index("clus")
    clus = lax.axis_size("clus")
    chips = clus // 2
    c, w = lax.rem(i, 2), i // 2
    sib = i + 1 - 2 * c
    slot = x * chips + w
    rows = k_hbm.shape[0]
    tiles = rows // TILE
    count = float(clus * TILE)
    me = x * clus + i

    def pair_of(half, core):
        return 2 * (x if half == 0 else 1 - x) + core

    def kv_copies(half, remote):
        copies = []
        for hh in range(2):
            for n, (src, dst) in enumerate(((k_hbm, kbuf), (v_hbm, vbuf))):
                number = half * 4 + hh * 2 + n
                pair = pair_of(half, 1 - c if remote else c)
                column = pl.ds(pl.multiple_of((pair * 2 + hh) * DH, DH), DH)
                if remote:
                    copies.append(pltpu.make_async_remote_copy(
                        src_ref=src.at[:, column], dst_ref=dst.at[half, hh, pl.ds(rows, rows)],
                        send_sem=kv_send.at[number], recv_sem=kv_recv.at[number],
                        device_id=(x, sib), device_id_type=MESH))
                else:
                    copies.append(pltpu.make_async_copy(
                        src.at[:, column], dst.at[half, hh, pl.ds(0, rows)], loc_sem.at[number]))
        return copies

    def remote(src, dst, send_sem, recv_sem, device):
        return pltpu.make_async_remote_copy(
            src_ref=src, dst_ref=dst, send_sem=send_sem, recv_sem=recv_sem,
            device_id=device, device_id_type=MESH)

    own_kv = [kv_copies(0, False), kv_copies(1, False)]
    far_kv = [kv_copies(0, True), kv_copies(1, True)]
    for copy in own_kv[0] + own_kv[1]:
        copy.start()

    barrier = pltpu.get_barrier_semaphore()

    def greet(k, carry):
        other = lax.rem(me + k, 2 * clus)
        pl.semaphore_signal(
            barrier, inc=1, device_id=(other // clus, lax.rem(other, clus)), device_id_type=MESH)
        return carry

    lax.fori_loop(1, 2 * clus, greet, 0)
    pl.semaphore_wait(barrier, 2 * clus - 1)

    small = [
        remote(bt_ref.at[0, 1], btx.at[0], in_send.at[0], in_recv.at[0], (x, sib)),
        remote(bt_ref.at[1, 0], btx.at[1], in_send.at[1], in_recv.at[1], (1 - x, i)),
        remote(bt_ref.at[1, 1], btx.at[2], in_send.at[2], in_recv.at[2], (1 - x, sib)),
        remote(a_ref.at[1], ax, in_send.at[3], in_recv.at[3], (x, sib)),
        remote(q_ref.at[pl.ds(2 * c, 2)], qx, in_send.at[4], in_recv.at[4], (1 - x, i)),
    ]
    for copy in small[:3] + far_kv[0] + small[4:] + small[3:4] + far_kv[1]:
        copy.start()

    def spread(table):
        return jnp.concatenate(
            [jnp.broadcast_to(table[:, t : t + 1], (table.shape[0], TILE)) for t in range(tiles)],
            axis=1)

    def parts_for(half, b, j):
        dest = b * 4 + j
        device = ((x if half == 0 else 1 - x), dest)
        return dest, device, (
            (o_buf.at[half, dest], o_rx.at[c, slot], o_send.at[half, dest], o_recv.at[c, slot]),
            (st_buf.at[half, b], st_rx.at[c, slot], st_send.at[half, dest], st_recv.at[c, slot]),
        )

    square = lax.broadcasted_iota(jnp.int32, (128, 128), 0) == lax.broadcasted_iota(
        jnp.int32, (128, 128), 1)

    def as_row(column):
        return jnp.sum(jnp.where(square, column, 0.0), axis=0, keepdims=True)

    def attend(half, b, carry):
        stats = []
        for hh in range(2):
            span = pl.ds(pl.multiple_of(b * 128, 128), 128)
            queries = q_ref[2 * c + hh, span, :] if half == 0 else qx[hh, span, :]
            scores = lax.dot_general(
                queries, kbuf[half, hh], nt, preferred_element_type=jnp.float32)
            scores = scores * log2_scale + bias[half, pl.ds(hh * 4 + b, 1), :]
            top = jnp.maximum(jnp.max(scores, axis=1, keepdims=True), lowest_top)
            weights = jnp.exp2(scores - top)
            total = jnp.sum(weights, axis=1, keepdims=True)
            numer = jnp.dot(
                weights.astype(jnp.bfloat16), vbuf[half, hh], preferred_element_type=jnp.float32)
            numer = numer.astype(jnp.bfloat16)
            for j in range(4):
                o_buf[half, b * 4 + j, hh] = numer[32 * j : 32 * (j + 1)]
            stats += [as_row(top), as_row(total)]
        st_buf[half, b] = jnp.concatenate(stats + [jnp.zeros((4, 128), jnp.float32)], axis=0)
        for j in range(4):
            dest, device, parts = parts_for(half, b, j)

            @pl.when((dest != i) if half == 0 else (dest >= 0))
            def _():
                for src, dst, send_sem, recv_sem in parts:
                    remote(src, dst, send_sem, recv_sem, device).start()

            if half == 0:
                @pl.when(dest == i)
                def _():
                    for src, dst, send_sem, recv_sem in parts:
                        pltpu.make_async_copy(src, dst, recv_sem).start()
        return carry

    for copy in own_kv[0]:
        copy.wait()
    small[0].wait_recv()
    for copy in far_kv[0]:
        copy.wait_recv()
    bias[0] = jnp.concatenate([spread(bt_ref[0, 0]), spread(btx[0])], axis=1)
    lax.fori_loop(0, 4, functools.partial(attend, 0), 0)

    for copy in own_kv[1]:
        copy.wait()
    for copy in far_kv[1] + [small[1], small[2], small[3], small[4]]:
        copy.wait_recv()
    bias[1] = jnp.concatenate([spread(btx[1]), spread(btx[2])], axis=1)

    tile_rows = lax.broadcasted_iota(jnp.int32, (2 * tiles, 2 * rows), 0)
    tile_cols = lax.broadcasted_iota(jnp.int32, (2 * tiles, 2 * rows), 1) // TILE
    unit = jnp.where(tile_rows == tile_cols, 1.0, 0.0).astype(jnp.bfloat16)
    for half in (1, 0):
        for n, buf in enumerate((kbuf, vbuf)):
            for hh in range(2):
                sums = jnp.dot(unit, buf[half, hh], preferred_element_type=jnp.float32)
                ts_buf[half, n, hh] = sums.reshape(2, tiles, DH)
    ts_copy = remote(ts_buf.at[1], ts_rx, ts_sem.at[0], ts_sem.at[1], (1 - x, i))
    ts_copy.start()

    lax.fori_loop(0, 2, functools.partial(attend, 1), 0)

    ts_copy.wait_recv()
    all_sums = jnp.concatenate(
        [ts_buf[0].reshape(8, tiles, DH), ts_rx[...].reshape(8, tiles, DH)], axis=1
    ).reshape(16 * tiles, DH)
    clustered = jnp.dot(
        a_ref[0] + ax[...], all_sums, precision=highest, preferred_element_type=jnp.float32)
    cs_buf[...] = clustered.reshape(chips, 8, DH)
    cs_rx[w] = cs_buf[w]

    def cs_out(k):
        chip = lax.rem(w + k, chips)
        return remote(
            cs_buf.at[chip], cs_rx.at[w], cs_send.at[chip], cs_recv.at[w], (x, 2 * chip + c))

    def cs_in(k):
        chip = lax.rem(w + k, chips)
        return remote(
            cs_buf.at[chip], cs_rx.at[chip], cs_send.at[chip], cs_recv.at[chip], (x, 2 * chip + c))

    for k in range(1, chips):
        cs_out(k).start()

    lax.fori_loop(2, 4, functools.partial(attend, 1), 0)

    for k in range(1, chips):
        cs_in(k).wait_recv()
    reduced = jnp.sum(cs_rx[...], axis=0)
    red_buf[...] = reduced
    tot_rx[c, w] = reduced

    def tot_out(k):
        other = lax.rem(i + k, clus)
        return remote(
            red_buf, tot_rx.at[c, w], tot_send.at[other], tot_recv.at[i], (x, other))

    def tot_in(k):
        other = lax.rem(i + k, clus)
        return remote(
            red_buf, tot_rx.at[lax.rem(other, 2), other // 2], tot_send.at[other],
            tot_recv.at[other], (x, other))

    for k in range(1, clus):
        tot_out(k).start()
    for k in range(1, clus):
        tot_in(k).wait_recv()

    def arrive(n, carry):
        core, source = n // clus, lax.rem(n, clus)
        remote(o_buf.at[0, 0], o_rx.at[core, source], o_send.at[0, 0],
               o_recv.at[core, source], (x, sib)).wait_recv()
        remote(st_buf.at[0, 0], st_rx.at[core, source], st_send.at[0, 0],
               st_recv.at[core, source], (x, sib)).wait_recv()
        return carry

    lax.fori_loop(0, 2 * clus, arrive, 0)

    block, part = i // 4, lax.rem(i, 4)
    for h in range(4):
        p, hh = h // 2, h % 2
        totals = tot_rx[p].reshape(chips * 8, DH)
        queries = q_ref[h, pl.ds(pl.multiple_of(block * 128, 128), 128), :].astype(jnp.float32)
        approx = lax.dot_general(
            totals, queries, nt, precision=highest, preferred_element_type=jnp.float32)
        approx = approx * (log2_scale / count) + ab_ref[h]
        tops, sums = st_rx[p, :, 2 * hh, :], st_rx[p, :, 2 * hh + 1, :]
        top = jnp.maximum(
            jnp.max(tops, axis=0, keepdims=True), jnp.max(approx, axis=0, keepdims=True))
        factor = jnp.exp2(tops - top)
        approx_weight = jnp.exp2(approx - top)
        total = jnp.sum(factor * sums, axis=0, keepdims=True) + count * jnp.sum(
            approx_weight, axis=0, keepdims=True)
        inverse = 1.0 / total
        mixed = jnp.concatenate(
            [factor * inverse, jnp.zeros((48, 128), jnp.float32),
             pltpu.roll(approx_weight * inverse, 4, 0)], axis=0)
        wt[...] = mixed.T
        mine = wt[pl.ds(pl.multiple_of(part * 32, 32), 32), :]
        numer = jnp.dot(
            mine, jnp.concatenate([jnp.zeros((64, DH), jnp.float32), totals], axis=0),
            precision=highest, preferred_element_type=jnp.float32)
        for source in range(2 * chips):
            numer = numer + mine[:, source : source + 1] * o_rx[p, source, hh].astype(jnp.float32)
        out_ref[h] = numer.astype(jnp.bfloat16)

    for copy in small + far_kv[0] + far_kv[1] + [ts_copy]:
        copy.wait_send()
    for k in range(1, chips):
        cs_out(k).wait_send()
    for k in range(1, clus):
        tot_out(k).wait_send()

    def sent(dest, carry):
        for half in range(2):
            @pl.when((dest != i) if half == 0 else (dest >= 0))
            def _():
                _, device, parts = parts_for(half, dest // 4, lax.rem(dest, 4))
                for src, dst, send_sem, recv_sem in parts:
                    remote(src, dst, send_sem, recv_sem, device).wait_send()
        return carry

    lax.fori_loop(0, clus, sent, 0)


def fast_local(key_cache, value_cache, prompt_queries, tile_cluster, listed_clusters):
    clus = lax.axis_size("clus")
    x, i = lax.axis_index("head"), lax.axis_index("clus")
    c = lax.rem(i, 2)
    _, rows, width = key_cache.shape
    tiles = rows // TILE
    chips = clus // 2
    query_count = prompt_queries.shape[0]
    heads = prompt_queries.shape[1] // (GROUP * DH)
    blocks = query_count // QBLK
    queries = prompt_queries.reshape(query_count, heads, GROUP, DH).transpose(1, 0, 2, 3)
    queries = queries.reshape(heads, query_count * GROUP, DH)

    ids = tile_cluster.reshape(2, 2, 2, tiles)
    ids = jnp.where(x == 0, ids, ids[:, :, ::-1])
    ids = jnp.where(c == 0, ids, ids[::-1])
    listed = listed_clusters.reshape(2, 2, blocks, -1)
    listed_mine = jnp.where(c == 0, listed, listed[::-1])
    live = jnp.any(
        ids[:, :, :, None, :, None] == listed_mine[:, :, None, :, None, :], axis=-1)
    tables = jnp.where(live, 0.0, dead).transpose(2, 0, 1, 3, 4).reshape(2, 2, 2 * blocks, tiles)
    tables = jnp.pad(tables, ((0, 0), (0, 0), (0, 0), (0, 128 - tiles)))

    r = jnp.arange(8 * chips, dtype=jnp.int32)
    number, kv_r, hh_r = 2 * (r // 8) + r % 2, (r // 4) % 2, (r // 2) % 2
    k = jnp.arange(16 * tiles, dtype=jnp.int32)
    kv_k, hh_k, side_k = k // (8 * tiles), (k // (4 * tiles)) % 2, (k // (2 * tiles)) % 2
    same = (kv_r[:, None] == kv_k[None, :]) & (hh_r[:, None] == hh_k[None, :])
    named = jnp.broadcast_to(
        ids.reshape(2, 1, 2, 1, 2 * tiles), (2, 2, 2, 2, 2 * tiles)).reshape(2, 1, 16 * tiles)
    side = jnp.arange(2, dtype=jnp.int32)[:, None, None]
    member = (named == number[None, :, None]) & same[None] & (side_k[None, None, :] == side)
    member = member.astype(jnp.float32)

    listed_here = lax.dynamic_index_in_dim(
        listed_clusters, i * blocks // clus, 1, keepdims=False)
    skipped = jnp.any(listed_here[:, :, None] == number, axis=1)
    usable = (kv_r == 0)[None] & (hh_r[None] == (jnp.arange(heads) % 2)[:, None]) & ~skipped
    approx_bias = jnp.broadcast_to(
        jnp.where(usable, 0.0, dead)[:, :, None], (heads, 8 * chips, 128))

    dma = pltpu.SemaphoreType.DMA
    f32, bf16 = jnp.float32, jnp.bfloat16
    share = query_count * GROUP // clus
    vmem = pl.BlockSpec(memory_space=pltpu.VMEM)
    anywhere = pl.BlockSpec(memory_space=pl.ANY)
    out = pl.pallas_call(
        fast_kernel,
        out_shape=jax.ShapeDtypeStruct((heads, share, DH), bf16),
        in_specs=[anywhere, anywhere, vmem, vmem, vmem, vmem],
        out_specs=vmem,
        scratch_shapes=[
            pltpu.VMEM((2, 2, 2 * rows, DH), bf16),
            pltpu.VMEM((2, 2, 2 * rows, DH), bf16),
            pltpu.VMEM((2, query_count * GROUP, DH), bf16),
            pltpu.VMEM((3, 2 * blocks, 128), f32),
            pltpu.VMEM((8 * chips, 16 * tiles), f32),
            pltpu.VMEM((2, 2 * blocks, 2 * rows), f32),
            pltpu.VMEM((2, clus, 2, share, DH), bf16),
            pltpu.VMEM((2, blocks, 8, 128), f32),
            pltpu.VMEM((2, clus, 2, share, DH), bf16),
            pltpu.VMEM((2, clus, 8, 128), f32),
            pltpu.VMEM((2, 2, 2, 2, tiles, DH), f32),
            pltpu.VMEM((2, 2, 2, tiles, DH), f32),
            pltpu.VMEM((chips, 8, DH), f32),
            pltpu.VMEM((chips, 8, DH), f32),
            pltpu.VMEM((8, DH), f32),
            pltpu.VMEM((2, chips, 8, DH), f32),
            pltpu.VMEM((128, 128), f32),
            dma((8,)), dma((8,)), dma((8,)), dma((5,)), dma((5,)),
            dma((2, clus)), dma((2, clus)), dma((2, clus)), dma((2, clus)),
            dma((2,)), dma((chips,)), dma((chips,)), dma((clus,)), dma((clus,)),
        ],
        compiler_params=pltpu.CompilerParams(
            collective_id=0, has_side_effects=True, vmem_limit_bytes=48 * 1024 * 1024),
    )(
        key_cache.reshape(rows, width), value_cache.reshape(rows, width),
        queries, tables, member, approx_bias,
    )
    out = out.reshape(heads, query_count // clus, GROUP, DH).transpose(1, 0, 2, 3)
    return out.reshape(query_count // clus, heads * GROUP * DH)


def solution(mesh):
    placed = (
        P("head", "clus", None),
        P("head", "clus", None),
        P(None, "head"),
        P("head", "clus", None, None, None),
        P("head", None, None),
    )
    fits = mesh.shape["head"] == 2 and mesh.shape["clus"] == 16
    return jax.shard_map(
        fast_local if fits else local,
        mesh=mesh,
        in_specs=placed,
        out_specs=P("clus", "head"),
        check_vma=False,
    )
```

```python
import functools
import math

import jax
import jax.numpy as jnp
from jax import lax
from jax.experimental import pallas as pl
from jax.experimental.pallas import tpu as pltpu
from jax.sharding import PartitionSpec as P

DH = 128
GROUP = 8
TILE = 128
QBLK = 16


floor_value = -1e30
highest = lax.Precision.HIGHEST


def combined_all(shard, axis, combine):
    everything = jax.tree.map(lambda part: lax.all_gather(part, axis), shard)
    leading = jax.tree.map(lambda part: part[0], everything)

    def turn(k, so_far):
        return combine(so_far, jax.tree.map(lambda part: part[k], everything))

    return lax.fori_loop(1, lax.axis_size(axis), turn, leading)


def block_partials(
    query_blocks, key_rows, value_rows, tile_mask, key_mean, value_sum, counts_mine, approx_on
):
    score_scale = key_rows.shape[-1] ** (-0.5)
    tile_rows = key_rows.shape[0] // tile_mask.shape[-1]

    def one_block(block_inputs):
        block_queries, mask_tiles, approx_flag = block_inputs
        key_mask = jnp.repeat(mask_tiles, tile_rows) > 0.5
        scores = (
            jnp.einsum("rd,kd->rk", block_queries, key_rows, preferred_element_type=jnp.float32)
            * score_scale
        )
        approx_score = (
            jnp.dot(block_queries.astype(jnp.float32), key_mean, precision=highest) * score_scale
        )
        approx_live = approx_flag > 0.5
        row_top = jnp.maximum(
            jnp.max(jnp.where(key_mask[None, :], scores, floor_value), axis=1),
            jnp.where(approx_live, approx_score, floor_value),
        )
        weights = jnp.where(key_mask[None, :], jnp.exp(scores - row_top[:, None]), 0.0)
        probabilities = weights.astype(jnp.bfloat16)
        approx_weight = jnp.where(approx_live, jnp.exp(approx_score - row_top), 0.0)
        row_total = jnp.sum(weights, axis=1) + counts_mine * approx_weight
        numerator = jnp.dot(probabilities, value_rows, preferred_element_type=jnp.float32)
        numerator = numerator + approx_weight[:, None] * value_sum[None, :]
        return (row_top, row_total, numerator)

    return lax.map(one_block, (query_blocks, tile_mask, approx_on))


def combine_parts(first_part, second_part):
    top_first, total_first, numer_first = first_part
    top_second, total_second, numer_second = second_part
    joined = jnp.maximum(top_first, top_second)
    factor_first = jnp.exp(top_first - joined)
    factor_second = jnp.exp(top_second - joined)
    return (
        joined,
        total_first * factor_first + total_second * factor_second,
        numer_first * factor_first[..., None] + numer_second * factor_second[..., None],
    )


def local(key_cache, value_cache, prompt_queries, tile_cluster, listed_clusters):
    owners = lax.axis_size("clus")
    owner_index = lax.axis_index("clus")
    moved_keys, moved_values = (
        lax.all_to_all(key_cache, "head", split_axis=2, concat_axis=0, tiled=True),
        lax.all_to_all(value_cache, "head", split_axis=2, concat_axis=0, tiled=True),
    )
    slab_count, slab_rows, feature_width = moved_keys.shape
    heads_dev = feature_width // DH
    tiles_dev = slab_count * slab_rows // TILE

    def to_tiles(moved):
        shaped = moved.reshape(slab_count, slab_rows // TILE, TILE, heads_dev, DH)
        return shaped.transpose(3, 0, 1, 2, 4).reshape(heads_dev, tiles_dev, TILE, DH)

    key_tiles = to_tiles(moved_keys)
    value_tiles = to_tiles(moved_values)
    cluster_ids = tile_cluster.reshape(heads_dev, tiles_dev)
    column_ids = jnp.arange(owners, dtype=jnp.int32)
    member = (cluster_ids[:, :, None] == column_ids[None, None, :]).astype(jnp.float32)
    listed_mask = jnp.max(
        (listed_clusters[:, :, :, None] == column_ids).astype(jnp.float32), axis=2
    )
    owner_hot = (column_ids == owner_index).astype(jnp.float32)
    mine_listed = jnp.einsum("hbc,c->hb", listed_mask, owner_hot, precision=highest)
    query_count = prompt_queries.shape[0]
    block_count = query_count // QBLK
    query_blocks = prompt_queries.reshape(query_count, heads_dev, GROUP, DH).transpose(1, 0, 2, 3)
    query_blocks = query_blocks.reshape(heads_dev, block_count, QBLK * GROUP, DH)
    key_rows = key_tiles.reshape(heads_dev, tiles_dev * TILE, DH)
    value_rows = value_tiles.reshape(heads_dev, tiles_dev * TILE, DH)
    unit_rows = jnp.ones((TILE,), jnp.bfloat16)
    tile_keys = jnp.einsum("htrd,r->htd", key_tiles, unit_rows, preferred_element_type=jnp.float32)
    tile_values = jnp.einsum(
        "htrd,r->htd", value_tiles, unit_rows, preferred_element_type=jnp.float32
    )
    local_keys = jnp.einsum("htc,htd->hcd", member, tile_keys, precision=highest)
    local_values = jnp.einsum("htc,htd->hcd", member, tile_values, precision=highest)
    local_counts = TILE * jnp.sum(member, axis=1)
    total_keys, total_values, total_counts = lax.psum(
        (local_keys, local_values, local_counts), "clus"
    )
    key_sum = jnp.einsum("hcd,c->hd", total_keys, owner_hot, precision=highest)
    value_sum = jnp.einsum("hcd,c->hd", total_values, owner_hot, precision=highest)
    counts_mine = jnp.einsum("hc,c->h", total_counts, owner_hot, precision=highest)
    tile_mask = jnp.einsum("hbc,htc->hbt", listed_mask, member, precision=highest)
    key_mean = key_sum / jnp.maximum(counts_mine, 1.0)[:, None]
    approx_on = (1.0 - mine_listed) * (counts_mine > 0.5).astype(jnp.float32)[:, None]
    row_top, row_total, numerator = jax.vmap(block_partials)(
        query_blocks, key_rows, value_rows, tile_mask, key_mean, value_sum, counts_mine, approx_on
    )
    row_top = row_top.reshape(heads_dev, query_count, GROUP)
    row_total = row_total.reshape(heads_dev, query_count, GROUP)
    numerator = numerator.reshape(heads_dev, query_count, GROUP, DH)
    share_rows = query_count // owners
    merged_top, merged_total, merged_numer = combined_all(
        (row_top, row_total, numerator), "clus", combine_parts
    )
    kept_total = lax.dynamic_slice_in_dim(merged_total, owner_index * share_rows, share_rows, 1)
    kept_numer = lax.dynamic_slice_in_dim(merged_numer, owner_index * share_rows, share_rows, 1)
    attended = kept_numer / kept_total[..., None]
    return (
        attended.transpose(1, 0, 2, 3)
        .reshape(share_rows, heads_dev * GROUP * DH)
        .astype(jnp.bfloat16)
    )


MESH = pl.DeviceIdType.MESH
dead = -1e30
lowest_top = -1e9
log2_scale = math.log2(math.e) * DH**-0.5
nt = (((1,), (1,)), ((), ()))


def fast_kernel(
    k_hbm, v_hbm, q_ref, bt_ref, a_ref, ab_ref, out_ref,
    kbuf, vbuf, qx, qall, btx, ax, bias, o_buf, st_buf, o_rx, st_rx,
    ts_buf, ts_rx, cs_buf, cs_rx, red_buf, tot_rx, wt, hot_ref,
    loc_sem, kv_send, kv_recv, in_send, in_recv,
    o_send, o_recv, st_send, st_recv, ts_sem, cs_send, cs_recv, tot_send, tot_recv,
):
    x, i = lax.axis_index("head"), lax.axis_index("clus")
    clus = lax.axis_size("clus")
    chips = clus // 2
    c, w = lax.rem(i, 2), i // 2
    sib = i + 1 - 2 * c
    slot = x * chips + w
    rows = k_hbm.shape[0]
    tiles = rows // TILE
    count = float(clus * TILE)
    me = x * clus + i
    wide = GROUP * DH
    span = 2 * QBLK * GROUP

    def pair_of(half, core):
        return 2 * (x if half == 0 else 1 - x) + core

    def kv_copies(half, remote):
        copies = []
        for hh in range(2):
            for n, (src, dst) in enumerate(((k_hbm, kbuf), (v_hbm, vbuf))):
                number = half * 4 + hh * 2 + n
                pair = pair_of(half, 1 - c if remote else c)
                column = pl.ds(pl.multiple_of((pair * 2 + hh) * DH, DH), DH)
                if remote:
                    copies.append(pltpu.make_async_remote_copy(
                        src_ref=src.at[:, column], dst_ref=dst.at[half, hh, pl.ds(rows, rows)],
                        send_sem=kv_send.at[number], recv_sem=kv_recv.at[number],
                        device_id=(x, sib), device_id_type=MESH))
                else:
                    copies.append(pltpu.make_async_copy(
                        src.at[:, column], dst.at[half, hh, pl.ds(0, rows)], loc_sem.at[number]))
        return copies

    def remote(src, dst, send_sem, recv_sem, device):
        return pltpu.make_async_remote_copy(
            src_ref=src, dst_ref=dst, send_sem=send_sem, recv_sem=recv_sem,
            device_id=device, device_id_type=MESH)

    own_kv = [kv_copies(0, False), kv_copies(1, False)]
    far_kv = [kv_copies(0, True), kv_copies(1, True)]
    for copy in own_kv[0] + own_kv[1]:
        copy.start()

    barrier = pltpu.get_barrier_semaphore()

    def greet(k, carry):
        other = lax.rem(me + k, 2 * clus)
        pl.semaphore_signal(
            barrier, inc=1, device_id=(other // clus, lax.rem(other, clus)), device_id_type=MESH)
        return carry

    lax.fori_loop(1, 2 * clus, greet, 0)
    pl.semaphore_wait(barrier, 2 * clus - 1)

    small = [
        remote(bt_ref.at[0, 1], btx.at[0], in_send.at[0], in_recv.at[0], (x, sib)),
        remote(bt_ref.at[1, 0], btx.at[1], in_send.at[1], in_recv.at[1], (1 - x, i)),
        remote(bt_ref.at[1, 1], btx.at[2], in_send.at[2], in_recv.at[2], (1 - x, sib)),
        remote(a_ref.at[1], ax, in_send.at[3], in_recv.at[3], (x, sib)),
        remote(q_ref.at[:, pl.ds(pl.multiple_of(c * 2 * wide, 128), 2 * wide)], qx,
               in_send.at[4], in_recv.at[4], (1 - x, i)),
    ]
    for copy in small[:3] + far_kv[0] + small[4:] + small[3:4] + far_kv[1]:
        copy.start()

    def regroup(rows_in):
        count_in = rows_in.shape[0]
        split = rows_in.astype(jnp.float32).reshape(count_in, GROUP, DH)
        return split.reshape(count_in * GROUP, DH).astype(jnp.bfloat16)

    def parts_for(half, dest):
        device = (x + half * (1 - 2 * x), dest)
        return device, (
            (o_buf.at[half, dest], o_rx.at[c, slot], o_send.at[half, dest], o_recv.at[c, slot]),
            (st_buf.at[half, dest // 4], st_rx.at[c, slot], st_send.at[half, dest],
             st_recv.at[c, slot]),
        )

    square = lax.broadcasted_iota(jnp.int32, (128, 128), 0) == lax.broadcasted_iota(
        jnp.int32, (128, 128), 1)

    def as_row(column):
        return jnp.sum(jnp.where(square, column, 0.0), axis=0, keepdims=True)

    key_tile = lax.broadcasted_iota(jnp.int32, (2 * rows, 128), 0) // TILE
    hot = key_tile == lax.broadcasted_iota(jnp.int32, (2 * rows, 128), 1)
    hot_ref[...] = jnp.where(hot, 1.0, 0.0).astype(jnp.bfloat16)
    st_buf[...] = jnp.zeros_like(st_buf)

    def attend(half, pair, hh):
        start = pl.multiple_of(pair * span, span)
        masks = [
            jnp.broadcast_to(bias[half, pl.ds(hh * 4 + pair * 2 + n, 1), :], (128, 128))
            for n in range(2)
        ]
        masks = jnp.concatenate(masks, axis=0).astype(jnp.bfloat16)
        queries = jnp.concatenate([qall[half, hh, pl.ds(start, span), :], masks], axis=1)
        keys = jnp.concatenate([kbuf[half, hh], hot_ref[...]], axis=1)
        scores = lax.dot_general(queries, keys, nt, preferred_element_type=jnp.float32)
        top = jnp.maximum(jnp.max(scores, axis=1, keepdims=True), lowest_top) * log2_scale
        weights = jnp.exp2(scores * log2_scale - top).astype(jnp.bfloat16)
        values = jnp.concatenate(
            [vbuf[half, hh], jnp.ones((2 * rows, 128), jnp.bfloat16)], axis=1)
        numer = jnp.dot(weights, values, preferred_element_type=jnp.float32)
        for n in range(2):
            block = pair * 2 + n
            part = slice(128 * n, 128 * (n + 1))
            st_buf[half, block, pl.ds(hh * 2, 1), :] = as_row(top[part])
            st_buf[half, block, pl.ds(hh * 2 + 1, 1), :] = as_row(numer[part, DH:])
            for j in range(4):
                first = 128 * n + 32 * j
                o_buf[half, block * 4 + j, hh] = numer[first : first + 32, :DH].astype(
                    jnp.bfloat16)

    def ship(half, dest):
        device, parts = parts_for(half, dest)
        here = (half == 0) & (dest == i)

        @pl.when(jnp.logical_not(here))
        def _():
            for src, dst, send_sem, recv_sem in parts:
                remote(src, dst, send_sem, recv_sem, device).start()

        @pl.when(here)
        def _():
            for src, dst, send_sem, recv_sem in parts:
                pltpu.make_async_copy(src, dst, recv_sem).start()

    def place_queries(half, source, first):
        def block_of(n, carry):
            hh, block = n // 4, lax.rem(n, 4)
            for head in range(2):
                @pl.when(hh == head)
                def _():
                    columns = pl.ds(pl.multiple_of(first + head * wide, 128), wide)
                    taken = source[pl.ds(pl.multiple_of(block * QBLK, QBLK), QBLK), columns]
                    qall[half, head, pl.ds(pl.multiple_of(block * 128, 128), 128), :] = regroup(
                        taken)
            return carry

        lax.fori_loop(0, 8, block_of, 0)

    def first_half():
        for copy in own_kv[0]:
            copy.wait()
        place_queries(0, q_ref, c * 2 * wide)
        small[0].wait_recv()
        for copy in far_kv[0]:
            copy.wait_recv()
        bias[0] = bt_ref[0, 0] + btx[0]

    def tile_sums():
        for copy in own_kv[1]:
            copy.wait()
        for copy in far_kv[1]:
            copy.wait_recv()

        def add_up(n, carry):
            half, hh = n // 2, lax.rem(n, 2)
            for m, buf in enumerate((kbuf, vbuf)):
                for side in range(2):
                    part = buf[half, hh, side * rows : (side + 1) * rows]
                    ts_buf[half, m, hh, side] = jnp.sum(
                        part.astype(jnp.float32).reshape(tiles, TILE, DH), axis=1)
            return carry

        lax.fori_loop(0, 4, add_up, 0)
        ts_copy.start()

    def second_half():
        for copy in [small[1], small[2], small[4]]:
            copy.wait_recv()
        place_queries(1, qx, 0)
        bias[1] = btx[1] + btx[2]

    ts_copy = remote(ts_buf.at[1], ts_rx, ts_sem.at[0], ts_sem.at[1], (1 - x, i))

    def cluster_sums():
        small[3].wait_recv()
        ts_copy.wait_recv()
        all_sums = jnp.concatenate(
            [ts_buf[0].reshape(8, tiles, DH), ts_rx[...].reshape(8, tiles, DH)], axis=1
        ).reshape(16 * tiles, DH)
        clustered = jnp.dot(
            a_ref[0] + ax[...], all_sums, precision=highest, preferred_element_type=jnp.float32)
        cs_buf[...] = clustered.reshape(chips, 8, DH)
        cs_rx[w] = cs_buf[w]
        for k in range(1, chips):
            cs_out(k).start()

    def cs_out(k):
        chip = lax.rem(w + k, chips)
        return remote(
            cs_buf.at[chip], cs_rx.at[w], cs_send.at[chip], cs_recv.at[w], (x, 2 * chip + c))

    def cs_in(k):
        chip = lax.rem(w + k, chips)
        return remote(
            cs_buf.at[chip], cs_rx.at[chip], cs_send.at[chip], cs_recv.at[chip], (x, 2 * chip + c))

    def reduce_sums():
        for k in range(1, chips):
            cs_in(k).wait_recv()
        reduced = jnp.sum(cs_rx[...], axis=0)
        red_buf[...] = reduced
        tot_rx[c, w] = reduced
        for k in range(1, clus):
            tot_out(k).start()

    def tot_out(k):
        other = lax.rem(i + k, clus)
        return remote(
            red_buf, tot_rx.at[c, w], tot_send.at[other], tot_recv.at[i], (x, other))

    def tot_in(k):
        other = lax.rem(i + k, clus)
        return remote(
            red_buf, tot_rx.at[lax.rem(other, 2), other // 2], tot_send.at[other],
            tot_recv.at[other], (x, other))

    hooks = ((first_half,), (tile_sums,), (second_half, cluster_sums), (reduce_sums,))

    def step(n, carry):
        half, pair = n // 2, lax.rem(n, 2)
        for number, hook in enumerate(hooks):
            @pl.when(n == number)
            def _():
                for work in hook:
                    work()

        def one_head(hh, inner):
            attend(half, pair, hh)
            return inner

        lax.fori_loop(0, 2, one_head, 0)

        def one_dest(k, inner):
            ship(half, pair * 8 + k)
            return inner

        lax.fori_loop(0, 8, one_dest, 0)
        return carry

    lax.fori_loop(0, 4, step, 0)
    for k in range(1, clus):
        tot_in(k).wait_recv()

    def arrive(n, carry):
        core, source = n // clus, lax.rem(n, clus)
        remote(o_buf.at[0, 0], o_rx.at[core, source], o_send.at[0, 0],
               o_recv.at[core, source], (x, sib)).wait_recv()
        remote(st_buf.at[0, 0], st_rx.at[core, source], st_send.at[0, 0],
               st_recv.at[core, source], (x, sib)).wait_recv()
        return carry

    lax.fori_loop(0, 2 * clus, arrive, 0)

    block, part = i // 4, lax.rem(i, 4)
    for h in range(4):
        p, hh = h // 2, h % 2
        totals = tot_rx[p].reshape(chips * 8, DH)
        taken = q_ref[pl.ds(pl.multiple_of(block * QBLK, QBLK), QBLK), h * wide : (h + 1) * wide]
        queries = regroup(taken).astype(jnp.float32)
        approx = lax.dot_general(
            totals, queries, nt, precision=highest, preferred_element_type=jnp.float32)
        approx = approx * (log2_scale / count) + ab_ref[h]
        tops, sums = st_rx[p, :, 2 * hh, :], st_rx[p, :, 2 * hh + 1, :]
        top = jnp.maximum(
            jnp.max(tops, axis=0, keepdims=True), jnp.max(approx, axis=0, keepdims=True))
        factor = jnp.exp2(tops - top)
        approx_weight = jnp.exp2(approx - top)
        total = jnp.sum(factor * sums, axis=0, keepdims=True) + count * jnp.sum(
            approx_weight, axis=0, keepdims=True)
        inverse = 1.0 / total
        mixed = jnp.concatenate(
            [factor * inverse, jnp.zeros((48, 128), jnp.float32),
             pltpu.roll(approx_weight * inverse, 4, 0)], axis=0)
        wt[...] = mixed.T
        mine = wt[pl.ds(pl.multiple_of(part * 32, 32), 32), :]
        numer = jnp.dot(
            mine, jnp.concatenate([jnp.zeros((64, DH), jnp.float32), totals], axis=0),
            precision=highest, preferred_element_type=jnp.float32)
        for source in range(2 * chips):
            numer = numer + mine[:, source : source + 1] * o_rx[p, source, hh].astype(jnp.float32)
        out_ref[:, h * wide : (h + 1) * wide] = numer.reshape(32 // GROUP, GROUP, DH).reshape(
            32 // GROUP, wide).astype(jnp.bfloat16)

    for copy in small + far_kv[0] + far_kv[1] + [ts_copy]:
        copy.wait_send()
    for k in range(1, chips):
        cs_out(k).wait_send()
    for k in range(1, clus):
        tot_out(k).wait_send()

    def sent(dest, carry):
        for half in range(2):
            @pl.when((dest != i) if half == 0 else (dest >= 0))
            def _():
                device, parts = parts_for(half, dest)
                for src, dst, send_sem, recv_sem in parts:
                    remote(src, dst, send_sem, recv_sem, device).wait_send()
        return carry

    lax.fori_loop(0, clus, sent, 0)


def fast_local(key_cache, value_cache, prompt_queries, tile_cluster, listed_clusters):
    clus = lax.axis_size("clus")
    x, i = lax.axis_index("head"), lax.axis_index("clus")
    c = lax.rem(i, 2)
    _, rows, width = key_cache.shape
    tiles = rows // TILE
    chips = clus // 2
    query_count = prompt_queries.shape[0]
    heads = prompt_queries.shape[1] // (GROUP * DH)
    blocks = query_count // QBLK

    ids = tile_cluster.reshape(2, 2, 2, tiles)
    ids = jnp.where(x == 0, ids, ids[:, :, ::-1])
    ids = jnp.where(c == 0, ids, ids[::-1])
    listed = listed_clusters.reshape(2, 2, blocks, -1)
    listed_mine = jnp.where(c == 0, listed, listed[::-1])
    live = jnp.any(
        ids[:, :, :, None, :, None] == listed_mine[:, :, None, :, None, :], axis=-1)
    tables = jnp.where(live, 0.0, dead).transpose(2, 0, 1, 3, 4).reshape(2, 2, 2 * blocks, tiles)
    shifted = [jnp.pad(tables[:, side], ((0, 0), (0, 0), (side * tiles, 128 - (1 + side) * tiles)))
               for side in range(2)]
    tables = jnp.stack(shifted, axis=1)

    r = jnp.arange(8 * chips, dtype=jnp.int32)
    number, kv_r, hh_r = 2 * (r // 8) + r % 2, (r // 4) % 2, (r // 2) % 2
    k = jnp.arange(16 * tiles, dtype=jnp.int32)
    kv_k, hh_k, side_k = k // (8 * tiles), (k // (4 * tiles)) % 2, (k // (2 * tiles)) % 2
    same = (kv_r[:, None] == kv_k[None, :]) & (hh_r[:, None] == hh_k[None, :])
    named = jnp.broadcast_to(
        ids.reshape(2, 1, 2, 1, 2 * tiles), (2, 2, 2, 2, 2 * tiles)).reshape(2, 1, 16 * tiles)
    side = jnp.arange(2, dtype=jnp.int32)[:, None, None]
    member = (named == number[None, :, None]) & same[None] & (side_k[None, None, :] == side)
    member = member.astype(jnp.float32)

    listed_here = lax.dynamic_index_in_dim(
        listed_clusters, i * blocks // clus, 1, keepdims=False)
    skipped = jnp.any(listed_here[:, :, None] == number, axis=1)
    usable = (kv_r == 0)[None] & (hh_r[None] == (jnp.arange(heads) % 2)[:, None]) & ~skipped
    approx_bias = jnp.broadcast_to(
        jnp.where(usable, 0.0, dead)[:, :, None], (heads, 8 * chips, 128))

    dma = pltpu.SemaphoreType.DMA
    f32, bf16 = jnp.float32, jnp.bfloat16
    share = query_count * GROUP // clus
    vmem = pl.BlockSpec(memory_space=pltpu.VMEM)
    anywhere = pl.BlockSpec(memory_space=pl.ANY)
    return pl.pallas_call(
        fast_kernel,
        out_shape=jax.ShapeDtypeStruct((query_count // clus, heads * GROUP * DH), bf16),
        in_specs=[anywhere, anywhere, vmem, vmem, vmem, vmem],
        out_specs=vmem,
        scratch_shapes=[
            pltpu.VMEM((2, 2, 2 * rows, DH), bf16),
            pltpu.VMEM((2, 2, 2 * rows, DH), bf16),
            pltpu.VMEM((query_count, 2 * GROUP * DH), bf16),
            pltpu.VMEM((2, 2, query_count * GROUP, DH), bf16),
            pltpu.VMEM((3, 2 * blocks, 128), f32),
            pltpu.VMEM((8 * chips, 16 * tiles), f32),
            pltpu.VMEM((2, 2 * blocks, 128), f32),
            pltpu.VMEM((2, clus, 2, share, DH), bf16),
            pltpu.VMEM((2, blocks, 8, 128), f32),
            pltpu.VMEM((2, clus, 2, share, DH), bf16),
            pltpu.VMEM((2, clus, 8, 128), f32),
            pltpu.VMEM((2, 2, 2, 2, tiles, DH), f32),
            pltpu.VMEM((2, 2, 2, tiles, DH), f32),
            pltpu.VMEM((chips, 8, DH), f32),
            pltpu.VMEM((chips, 8, DH), f32),
            pltpu.VMEM((8, DH), f32),
            pltpu.VMEM((2, chips, 8, DH), f32),
            pltpu.VMEM((128, 128), f32),
            pltpu.VMEM((2 * rows, 128), bf16),
            dma((8,)), dma((8,)), dma((8,)), dma((5,)), dma((5,)),
            dma((2, clus)), dma((2, clus)), dma((2, clus)), dma((2, clus)),
            dma((2,)), dma((chips,)), dma((chips,)), dma((clus,)), dma((clus,)),
        ],
        compiler_params=pltpu.CompilerParams(
            collective_id=0, has_side_effects=True, vmem_limit_bytes=48 * 1024 * 1024),
    )(
        key_cache.reshape(rows, width), value_cache.reshape(rows, width),
        prompt_queries, tables, member, approx_bias,
    )


def solution(mesh):
    placed = (
        P("head", "clus", None),
        P("head", "clus", None),
        P(None, "head"),
        P("head", "clus", None, None, None),
        P("head", None, None),
    )
    fits = mesh.shape["head"] == 2 and mesh.shape["clus"] == 16
    return jax.shard_map(
        fast_local if fits else local,
        mesh=mesh,
        in_specs=placed,
        out_specs=P("clus", "head"),
        check_vma=False,
    )
```

```python
import functools
import math

import jax
import jax.numpy as jnp
from jax import lax
from jax.experimental import pallas as pl
from jax.experimental.pallas import tpu as pltpu
from jax.sharding import PartitionSpec as P

DH = 128
GROUP = 8
TILE = 128
QBLK = 16


floor_value = -1e30
highest = lax.Precision.HIGHEST


def combined_all(shard, axis, combine):
    everything = jax.tree.map(lambda part: lax.all_gather(part, axis), shard)
    leading = jax.tree.map(lambda part: part[0], everything)

    def turn(k, so_far):
        return combine(so_far, jax.tree.map(lambda part: part[k], everything))

    return lax.fori_loop(1, lax.axis_size(axis), turn, leading)


def block_partials(
    query_blocks, key_rows, value_rows, tile_mask, key_mean, value_sum, counts_mine, approx_on
):
    score_scale = key_rows.shape[-1] ** (-0.5)
    tile_rows = key_rows.shape[0] // tile_mask.shape[-1]

    def one_block(block_inputs):
        block_queries, mask_tiles, approx_flag = block_inputs
        key_mask = jnp.repeat(mask_tiles, tile_rows) > 0.5
        scores = (
            jnp.einsum("rd,kd->rk", block_queries, key_rows, preferred_element_type=jnp.float32)
            * score_scale
        )
        approx_score = (
            jnp.dot(block_queries.astype(jnp.float32), key_mean, precision=highest) * score_scale
        )
        approx_live = approx_flag > 0.5
        row_top = jnp.maximum(
            jnp.max(jnp.where(key_mask[None, :], scores, floor_value), axis=1),
            jnp.where(approx_live, approx_score, floor_value),
        )
        weights = jnp.where(key_mask[None, :], jnp.exp(scores - row_top[:, None]), 0.0)
        probabilities = weights.astype(jnp.bfloat16)
        approx_weight = jnp.where(approx_live, jnp.exp(approx_score - row_top), 0.0)
        row_total = jnp.sum(weights, axis=1) + counts_mine * approx_weight
        numerator = jnp.dot(probabilities, value_rows, preferred_element_type=jnp.float32)
        numerator = numerator + approx_weight[:, None] * value_sum[None, :]
        return (row_top, row_total, numerator)

    return lax.map(one_block, (query_blocks, tile_mask, approx_on))


def combine_parts(first_part, second_part):
    top_first, total_first, numer_first = first_part
    top_second, total_second, numer_second = second_part
    joined = jnp.maximum(top_first, top_second)
    factor_first = jnp.exp(top_first - joined)
    factor_second = jnp.exp(top_second - joined)
    return (
        joined,
        total_first * factor_first + total_second * factor_second,
        numer_first * factor_first[..., None] + numer_second * factor_second[..., None],
    )


def local(key_cache, value_cache, prompt_queries, tile_cluster, listed_clusters):
    owners = lax.axis_size("clus")
    owner_index = lax.axis_index("clus")
    moved_keys, moved_values = (
        lax.all_to_all(key_cache, "head", split_axis=2, concat_axis=0, tiled=True),
        lax.all_to_all(value_cache, "head", split_axis=2, concat_axis=0, tiled=True),
    )
    slab_count, slab_rows, feature_width = moved_keys.shape
    heads_dev = feature_width // DH
    tiles_dev = slab_count * slab_rows // TILE

    def to_tiles(moved):
        shaped = moved.reshape(slab_count, slab_rows // TILE, TILE, heads_dev, DH)
        return shaped.transpose(3, 0, 1, 2, 4).reshape(heads_dev, tiles_dev, TILE, DH)

    key_tiles = to_tiles(moved_keys)
    value_tiles = to_tiles(moved_values)
    cluster_ids = tile_cluster.reshape(heads_dev, tiles_dev)
    column_ids = jnp.arange(owners, dtype=jnp.int32)
    member = (cluster_ids[:, :, None] == column_ids[None, None, :]).astype(jnp.float32)
    listed_mask = jnp.max(
        (listed_clusters[:, :, :, None] == column_ids).astype(jnp.float32), axis=2
    )
    owner_hot = (column_ids == owner_index).astype(jnp.float32)
    mine_listed = jnp.einsum("hbc,c->hb", listed_mask, owner_hot, precision=highest)
    query_count = prompt_queries.shape[0]
    block_count = query_count // QBLK
    query_blocks = prompt_queries.reshape(query_count, heads_dev, GROUP, DH).transpose(1, 0, 2, 3)
    query_blocks = query_blocks.reshape(heads_dev, block_count, QBLK * GROUP, DH)
    key_rows = key_tiles.reshape(heads_dev, tiles_dev * TILE, DH)
    value_rows = value_tiles.reshape(heads_dev, tiles_dev * TILE, DH)
    unit_rows = jnp.ones((TILE,), jnp.bfloat16)
    tile_keys = jnp.einsum("htrd,r->htd", key_tiles, unit_rows, preferred_element_type=jnp.float32)
    tile_values = jnp.einsum(
        "htrd,r->htd", value_tiles, unit_rows, preferred_element_type=jnp.float32
    )
    local_keys = jnp.einsum("htc,htd->hcd", member, tile_keys, precision=highest)
    local_values = jnp.einsum("htc,htd->hcd", member, tile_values, precision=highest)
    local_counts = TILE * jnp.sum(member, axis=1)
    total_keys, total_values, total_counts = lax.psum(
        (local_keys, local_values, local_counts), "clus"
    )
    key_sum = jnp.einsum("hcd,c->hd", total_keys, owner_hot, precision=highest)
    value_sum = jnp.einsum("hcd,c->hd", total_values, owner_hot, precision=highest)
    counts_mine = jnp.einsum("hc,c->h", total_counts, owner_hot, precision=highest)
    tile_mask = jnp.einsum("hbc,htc->hbt", listed_mask, member, precision=highest)
    key_mean = key_sum / jnp.maximum(counts_mine, 1.0)[:, None]
    approx_on = (1.0 - mine_listed) * (counts_mine > 0.5).astype(jnp.float32)[:, None]
    row_top, row_total, numerator = jax.vmap(block_partials)(
        query_blocks, key_rows, value_rows, tile_mask, key_mean, value_sum, counts_mine, approx_on
    )
    row_top = row_top.reshape(heads_dev, query_count, GROUP)
    row_total = row_total.reshape(heads_dev, query_count, GROUP)
    numerator = numerator.reshape(heads_dev, query_count, GROUP, DH)
    share_rows = query_count // owners
    merged_top, merged_total, merged_numer = combined_all(
        (row_top, row_total, numerator), "clus", combine_parts
    )
    kept_total = lax.dynamic_slice_in_dim(merged_total, owner_index * share_rows, share_rows, 1)
    kept_numer = lax.dynamic_slice_in_dim(merged_numer, owner_index * share_rows, share_rows, 1)
    attended = kept_numer / kept_total[..., None]
    return (
        attended.transpose(1, 0, 2, 3)
        .reshape(share_rows, heads_dev * GROUP * DH)
        .astype(jnp.bfloat16)
    )


MESH = pl.DeviceIdType.MESH
dead = -1e30
lowest_top = -1e9
log2_scale = math.log2(math.e) * DH**-0.5
nt = (((1,), (1,)), ((), ()))


def fast_kernel(
    k_hbm, v_hbm, q_ref, ids_ref, listed_ref, out_ref,
    kbuf, vbuf, kout, vout, qx, qall, bt, btx, bias, o_buf, st_buf, o_rx, st_rx,
    ts_buf, ts_rx, cs_buf, cs_rx, red_buf, tot_rx, wt, hot_ref,
    loc_sem, kv_send, kv_recv, in_send, in_recv,
    o_send, o_recv, st_send, st_recv, ts_sem, cs_send, cs_recv, tot_send, tot_recv,
):
    x, i = lax.axis_index("head"), lax.axis_index("clus")
    clus = lax.axis_size("clus")
    chips = clus // 2
    c, w = lax.rem(i, 2), i // 2
    sib = i + 1 - 2 * c
    slot = x * chips + w
    rows = k_hbm.shape[0]
    tiles = rows // TILE
    count = float(clus * TILE)
    me = x * clus + i
    wide = GROUP * DH
    span = 2 * QBLK * GROUP
    far = jnp.where(i < chips, 1, 0)
    listing = listed_ref.shape[2]

    def pair_of(half, core):
        return 2 * (x if half == 0 else 1 - x) + core

    def kv_copies(half, kind):
        copies = []
        for hh in range(2):
            for n, (src, dst, out) in enumerate(((k_hbm, kbuf, kout), (v_hbm, vbuf, vout))):
                number = half * 4 + hh * 2 + n
                pair = pair_of(half, c if kind == 0 else 1 - c)
                column = pl.ds(pl.multiple_of((pair * 2 + hh) * DH, DH), DH)
                if kind == 0:
                    copies.append(pltpu.make_async_copy(
                        src.at[:, column], dst.at[half, hh, pl.ds(0, rows)], loc_sem.at[0, number]))
                elif kind == 1:
                    copies.append(pltpu.make_async_copy(
                        src.at[:, column], out.at[half, hh], loc_sem.at[1, number]))
                else:
                    copies.append(pltpu.make_async_remote_copy(
                        src_ref=out.at[half, hh], dst_ref=dst.at[half, hh, pl.ds(rows, rows)],
                        send_sem=kv_send.at[number], recv_sem=kv_recv.at[number],
                        device_id=(x, sib), device_id_type=MESH))
        return copies

    def remote(src, dst, send_sem, recv_sem, device):
        return pltpu.make_async_remote_copy(
            src_ref=src, dst_ref=dst, send_sem=send_sem, recv_sem=recv_sem,
            device_id=device, device_id_type=MESH)

    own_kv = [kv_copies(0, 0), kv_copies(1, 0)]
    out_kv = [kv_copies(0, 1), kv_copies(1, 1)]
    far_kv = [kv_copies(0, 2), kv_copies(1, 2)]
    for copy in out_kv[0] + out_kv[1] + own_kv[0] + own_kv[1]:
        copy.start()

    barrier = pltpu.get_barrier_semaphore()

    def greet(k, carry):
        other = lax.rem(me + k, 2 * clus)
        pl.semaphore_signal(
            barrier, inc=1, device_id=(other // clus, lax.rem(other, clus)), device_id_type=MESH)
        return carry

    lax.fori_loop(1, 2 * clus, greet, 0)

    lane8 = lax.broadcasted_iota(jnp.int32, (8, 128), 1)
    sub8 = lax.broadcasted_iota(jnp.int32, (8, 128), 0)
    for turn in range(2):
        pair = c if turn == 0 else 1 - c
        named = []
        for l in range(listing):
            table = jnp.zeros((8, 128), jnp.int32)
            for hh in range(2):
                for b in range(4):
                    table = jnp.where(sub8 == hh * 4 + b, listed_ref[2 * pair + hh, b, l], table)
            named.append(table)
        first = turn * tiles
        for side in range(2):
            slab = x if side == 0 else 1 - x
            held = jnp.full((8, 128), -1, jnp.int32)
            for hh in range(2):
                for t in range(tiles):
                    here = (lane8 == first + t) & (sub8 // 4 == hh)
                    held = jnp.where(here, ids_ref[2 * pair + hh, 0, slab, t, 0], held)
            live = (lane8 < first) | (lane8 >= first + tiles)
            for table in named:
                live = live | (held == table)
            bt[side, turn] = jnp.where(live, 0.0, dead)

    key_tile = lax.broadcasted_iota(jnp.int32, (2 * rows, 128), 0) // TILE
    hot = key_tile == lax.broadcasted_iota(jnp.int32, (2 * rows, 128), 1)
    hot_ref[...] = jnp.where(hot, 1.0, 0.0).astype(jnp.bfloat16)

    def regroup(rows_in):
        count_in = rows_in.shape[0]
        split = rows_in.astype(jnp.float32).reshape(count_in, GROUP, DH)
        return split.reshape(count_in * GROUP, DH).astype(jnp.bfloat16)

    def place_queries(half, source, first):
        def block_of(n, carry):
            hh, block = n // 4, lax.rem(n, 4)
            for head in range(2):
                @pl.when(hh == head)
                def _():
                    columns = pl.ds(pl.multiple_of(first + head * wide, 128), wide)
                    taken = source[pl.ds(pl.multiple_of(block * QBLK, QBLK), QBLK), columns]
                    qall[half, head, pl.ds(pl.multiple_of(block * 128, 128), 128), :] = regroup(
                        taken)
            return carry

        lax.fori_loop(0, 8, block_of, 0)

    place_queries(0, q_ref, c * 2 * wide)
    pl.semaphore_wait(barrier, 2 * clus - 1)
    for copy in out_kv[0] + out_kv[1]:
        copy.wait()

    small = [
        remote(bt.at[0, 1], btx.at[0], in_send.at[0], in_recv.at[0], (x, sib)),
        remote(bt.at[1, 0], btx.at[1], in_send.at[1], in_recv.at[1], (1 - x, i)),
        remote(bt.at[1, 1], btx.at[2], in_send.at[2], in_recv.at[2], (1 - x, sib)),
        remote(q_ref.at[:, pl.ds(pl.multiple_of(c * 2 * wide, 128), 2 * wide)], qx,
               in_send.at[3], in_recv.at[3], (1 - x, i)),
    ]
    for copy in small + far_kv[0] + far_kv[1]:
        copy.start()

    for copy in own_kv[0] + own_kv[1]:
        copy.wait()

    def add_up(n, carry):
        half, hh = n // 2, lax.rem(n, 2)
        for m, (buf, out) in enumerate(((kbuf, kout), (vbuf, vout))):
            for part, core in ((buf[half, hh, :rows], c), (out[half, hh], 1 - c)):
                ts_buf[half, m, 2 * core + hh] = jnp.sum(
                    part.astype(jnp.float32).reshape(tiles, TILE, DH), axis=1)
        return carry

    lax.fori_loop(0, 4, add_up, 0)
    ts_copy = remote(ts_buf.at[1], ts_rx, ts_sem.at[0], ts_sem.at[1], (1 - x, i))
    ts_copy.start()

    def parts_for(half, dest):
        device = (x + half * (1 - 2 * x), dest)
        return device, (
            (o_buf.at[half, dest], o_rx.at[c, slot], o_send.at[half, dest], o_recv.at[c, slot]),
            (st_buf.at[half, dest // 4], st_rx.at[c, slot], st_send.at[half, dest],
             st_recv.at[c, slot]),
        )

    square = lax.broadcasted_iota(jnp.int32, (128, 128), 0) == lax.broadcasted_iota(
        jnp.int32, (128, 128), 1)

    def as_row(column):
        return jnp.sum(jnp.where(square, column, 0.0), axis=0, keepdims=True)

    def attend(half, pair, hh):
        start = pl.multiple_of(pair * span, span)
        masks = [
            jnp.broadcast_to(bias[half, pl.ds(hh * 4 + pair * 2 + n, 1), :], (128, 128))
            for n in range(2)
        ]
        masks = jnp.concatenate(masks, axis=0).astype(jnp.bfloat16)
        queries = jnp.concatenate([qall[half, hh, pl.ds(start, span), :], masks], axis=1)
        keys = jnp.concatenate([kbuf[half, hh], hot_ref[...]], axis=1)
        scores = lax.dot_general(queries, keys, nt, preferred_element_type=jnp.float32)
        top = jnp.maximum(jnp.max(scores, axis=1, keepdims=True), lowest_top) * log2_scale
        weights = jnp.exp2(scores * log2_scale - top).astype(jnp.bfloat16)
        values = jnp.concatenate(
            [vbuf[half, hh], jnp.ones((2 * rows, 128), jnp.bfloat16)], axis=1)
        numer = jnp.dot(weights, values, preferred_element_type=jnp.float32)
        for n in range(2):
            block = pair * 2 + n
            part = slice(128 * n, 128 * (n + 1))
            st_buf[half, block, pl.ds(hh * 2, 1), :] = as_row(top[part])
            st_buf[half, block, pl.ds(hh * 2 + 1, 1), :] = as_row(numer[part, DH:])
            for j in range(4):
                first = 128 * n + 32 * j
                o_buf[half, block * 4 + j, hh] = numer[first : first + 32, :DH].astype(
                    jnp.bfloat16)

    def ship(half, dest):
        device, parts = parts_for(half, dest)
        here = (half == 0) & (dest == i)

        @pl.when(jnp.logical_not(here))
        def _():
            for src, dst, send_sem, recv_sem in parts:
                remote(src, dst, send_sem, recv_sem, device).start()

        @pl.when(here)
        def _():
            for src, dst, send_sem, recv_sem in parts:
                pltpu.make_async_copy(src, dst, recv_sem).start()

    def first_half():
        small[0].wait_recv()
        for copy in far_kv[0]:
            copy.wait_recv()
        bias[0] = bt[0, 0] + btx[0]

    def second_half():
        for copy in small[1:]:
            copy.wait_recv()
        for copy in far_kv[1]:
            copy.wait_recv()
        place_queries(1, qx, 0)
        bias[1] = btx[1] + btx[2]

    line = lax.broadcasted_iota(jnp.int32, (128, 128), 0)

    def cluster_sums():
        lane = lax.rem(lane8, 8 * tiles)
        held = jnp.zeros((8, 128), jnp.int32)
        for h in range(4):
            for side in range(2):
                slab = x if side == 0 else 1 - x
                for t in range(tiles):
                    held = jnp.where(
                        lane == (h * 2 + side) * tiles + t, ids_ref[h, 0, slab, t, 0], held)
        held = jnp.concatenate([held] * 16, axis=0)
        column = lax.broadcasted_iota(jnp.int32, (128, 128), 1)
        belongs = (held == line // 8) & (lax.rem(line, 8) == column // (2 * tiles))
        ts_copy.wait_recv()
        all_sums = jnp.concatenate(
            [ts_buf[0].reshape(8, tiles, DH), ts_rx[...].reshape(8, tiles, DH)], axis=1
        ).reshape(16 * tiles, DH)
        clustered = jnp.dot(
            jnp.where(belongs, 1.0, 0.0), all_sums, precision=highest,
            preferred_element_type=jnp.float32)
        cs_buf[...] = clustered.reshape(clus, 8, DH)
        cs_rx[i] = cs_buf[i]
        lax.fori_loop(1, clus, start_cs, 0)

    def cs_copy(k, out):
        other = lax.rem(i + k, clus)
        return remote(
            cs_buf.at[other], cs_rx.at[i if out else other], cs_send.at[other],
            cs_recv.at[i if out else other], (x, other))

    def start_cs(k, carry):
        cs_copy(k, True).start()
        return carry

    def tot_copy(k, out):
        other = lax.rem(i + k, clus)
        return remote(
            red_buf, tot_rx.at[i if out else other], tot_send.at[other],
            tot_recv.at[i if out else other], (x, other))

    def start_tot(k, carry):
        tot_copy(k, True).start()
        return carry

    def wait_cs(k, carry):
        cs_copy(k, False).wait_recv()
        return carry

    def wait_tot(k, carry):
        tot_copy(k, False).wait_recv()
        return carry

    def reduce_sums():
        lax.fori_loop(1, clus, wait_cs, 0)
        reduced = jnp.sum(cs_rx[...], axis=0)
        red_buf[...] = reduced
        tot_rx[i] = reduced
        lax.fori_loop(1, clus, start_tot, 0)

    hooks = ((first_half,), (cluster_sums,), (reduce_sums, second_half))

    def step(n, carry):
        half, pair = n // 2, lax.rem(n + far, 2)
        for number, hook in enumerate(hooks):
            @pl.when(n == number)
            def _():
                for work in hook:
                    work()

        def one_head(hh, inner):
            attend(half, pair, hh)
            return inner

        lax.fori_loop(0, 2, one_head, 0)

        def one_dest(k, inner):
            ship(half, pair * 8 + lax.rem(k + i, 8))
            return inner

        lax.fori_loop(0, 8, one_dest, 0)
        return carry

    lax.fori_loop(0, 4, step, 0)
    lax.fori_loop(1, clus, wait_tot, 0)
    block, part = i // 4, lax.rem(i, 4)
    share = pl.ds(pl.multiple_of(part * 32, 32), 32)
    totals = tot_rx[...].reshape(clus * 8, DH)
    approx_parts = []
    for h in range(4):
        taken = q_ref[pl.ds(pl.multiple_of(block * QBLK, QBLK), QBLK), h * wide : (h + 1) * wide]
        queries = regroup(taken).astype(jnp.float32)
        approx = lax.dot_general(
            totals, queries, nt, precision=highest, preferred_element_type=jnp.float32)
        usable = lax.rem(line, 8) == h
        for l in range(listing):
            usable = usable & (line // 8 != listed_ref[h, block, l])
        approx = jnp.where(usable, approx * (log2_scale / count), dead)
        top = jnp.max(approx, axis=0, keepdims=True)
        approx_weight = jnp.where(usable, jnp.exp2(approx - top), 0.0)
        total = count * jnp.sum(approx_weight, axis=0, keepdims=True)
        wt[h] = pltpu.roll(approx_weight, 4, 0).T
        numer = jnp.dot(
            wt[h, share, :], totals, precision=highest, preferred_element_type=jnp.float32)
        approx_parts.append((top, total, numer))

    def arrive(n, carry):
        core, source = n // clus, lax.rem(n, clus)
        remote(o_buf.at[0, 0], o_rx.at[core, source], o_send.at[0, 0],
               o_recv.at[core, source], (x, sib)).wait_recv()
        remote(st_buf.at[0, 0], st_rx.at[core, source], st_send.at[0, 0],
               st_recv.at[core, source], (x, sib)).wait_recv()
        return carry

    lax.fori_loop(0, 2 * clus, arrive, 0)

    for h in range(4):
        p, hh = h // 2, h % 2
        tops, sums = st_rx[p, :, 2 * hh, :], st_rx[p, :, 2 * hh + 1, :]
        approx_top, approx_total, _ = approx_parts[h]
        top = jnp.maximum(jnp.max(tops, axis=0, keepdims=True), approx_top)
        factor = jnp.exp2(tops - top)
        approx_factor = jnp.exp2(approx_top - top)
        total = jnp.sum(factor * sums, axis=0, keepdims=True) + approx_factor * approx_total
        inverse = 1.0 / total
        mixed = jnp.concatenate(
            [factor * inverse, jnp.broadcast_to(approx_factor * inverse, (8, 128)),
             jnp.zeros((104, 128), jnp.float32)], axis=0)
        wt[4 + h] = mixed.T
    for h in range(4):
        p, hh = h // 2, h % 2
        mine = wt[4 + h, share, :]
        numer = mine[:, 2 * chips : 2 * chips + 1] * approx_parts[h][2]
        for source in range(2 * chips):
            numer = numer + mine[:, source : source + 1] * o_rx[p, source, hh].astype(jnp.float32)
        out_ref[:, h * wide : (h + 1) * wide] = numer.reshape(32 // GROUP, GROUP, DH).reshape(
            32 // GROUP, wide).astype(jnp.bfloat16)

    for copy in small + far_kv[0] + far_kv[1] + [ts_copy]:
        copy.wait_send()

    def drain(k, carry):
        cs_copy(k, True).wait_send()
        tot_copy(k, True).wait_send()
        return carry

    lax.fori_loop(1, clus, drain, 0)

    def sent(dest, carry):
        for half in range(2):
            @pl.when((dest != i) if half == 0 else (dest >= 0))
            def _():
                device, parts = parts_for(half, dest)
                for src, dst, send_sem, recv_sem in parts:
                    remote(src, dst, send_sem, recv_sem, device).wait_send()
        return carry

    lax.fori_loop(0, clus, sent, 0)


def fast_local(key_cache, value_cache, prompt_queries, tile_cluster, listed_clusters):
    clus = lax.axis_size("clus")
    _, rows, width = key_cache.shape
    tiles = rows // TILE
    query_count = prompt_queries.shape[0]
    heads = prompt_queries.shape[1] // (GROUP * DH)
    blocks = query_count // QBLK
    dma = pltpu.SemaphoreType.DMA
    f32, bf16 = jnp.float32, jnp.bfloat16
    share = query_count * GROUP // clus
    vmem = pl.BlockSpec(memory_space=pltpu.VMEM)
    smem = pl.BlockSpec(memory_space=pltpu.SMEM)
    hbm = pl.BlockSpec(memory_space=pltpu.HBM)
    return pl.pallas_call(
        fast_kernel,
        out_shape=jax.ShapeDtypeStruct((query_count // clus, heads * GROUP * DH), bf16),
        in_specs=[hbm, hbm, vmem, smem, smem],
        out_specs=vmem,
        scratch_shapes=[
            pltpu.VMEM((2, 2, 2 * rows, DH), bf16),
            pltpu.VMEM((2, 2, 2 * rows, DH), bf16),
            pltpu.VMEM((2, 2, rows, DH), bf16),
            pltpu.VMEM((2, 2, rows, DH), bf16),
            pltpu.VMEM((query_count, 2 * GROUP * DH), bf16),
            pltpu.VMEM((2, 2, query_count * GROUP, DH), bf16),
            pltpu.VMEM((2, 2, 2 * blocks, 128), f32),
            pltpu.VMEM((3, 2 * blocks, 128), f32),
            pltpu.VMEM((2, 2 * blocks, 128), f32),
            pltpu.VMEM((2, clus, 2, share, DH), bf16),
            pltpu.VMEM((2, blocks, 4, 128), f32),
            pltpu.VMEM((2, clus, 2, share, DH), bf16),
            pltpu.VMEM((2, clus, 4, 128), f32),
            pltpu.VMEM((2, 2, heads, tiles, DH), f32),
            pltpu.VMEM((2, heads, tiles, DH), f32),
            pltpu.VMEM((clus, 8, DH), f32),
            pltpu.VMEM((clus, 8, DH), f32),
            pltpu.VMEM((8, DH), f32),
            pltpu.VMEM((clus, 8, DH), f32),
            pltpu.VMEM((8, 128, 128), f32),
            pltpu.VMEM((2 * rows, 128), bf16),
            dma((2, 8)), dma((8,)), dma((8,)), dma((4,)), dma((4,)),
            dma((2, clus)), dma((2, clus)), dma((2, clus)), dma((2, clus)),
            dma((2,)), dma((clus,)), dma((clus,)), dma((clus,)), dma((clus,)),
        ],
        compiler_params=pltpu.CompilerParams(
            collective_id=0, has_side_effects=True, vmem_limit_bytes=56 * 1024 * 1024),
    )(
        key_cache.reshape(rows, width), value_cache.reshape(rows, width),
        prompt_queries, tile_cluster, listed_clusters,
    )


def solution(mesh):
    placed = (
        P("head", "clus", None),
        P("head", "clus", None),
        P(None, "head"),
        P("head", "clus", None, None, None),
        P("head", None, None),
    )
    fits = mesh.shape["head"] == 2 and mesh.shape["clus"] == 16
    return jax.shard_map(
        fast_local if fits else local,
        mesh=mesh,
        in_specs=placed,
        out_specs=P("clus", "head"),
        check_vma=False,
    )
```

```python
import functools
import math

import jax
import jax.numpy as jnp
from jax import lax
from jax.experimental import pallas as pl
from jax.experimental.pallas import tpu as pltpu
from jax.sharding import PartitionSpec as P

DH = 128
GROUP = 8
TILE = 128
QBLK = 16


floor_value = -1e30
highest = lax.Precision.HIGHEST


def combined_all(shard, axis, combine):
    everything = jax.tree.map(lambda part: lax.all_gather(part, axis), shard)
    leading = jax.tree.map(lambda part: part[0], everything)

    def turn(k, so_far):
        return combine(so_far, jax.tree.map(lambda part: part[k], everything))

    return lax.fori_loop(1, lax.axis_size(axis), turn, leading)


def block_partials(
    query_blocks, key_rows, value_rows, tile_mask, key_mean, value_sum, counts_mine, approx_on
):
    score_scale = key_rows.shape[-1] ** (-0.5)
    tile_rows = key_rows.shape[0] // tile_mask.shape[-1]

    def one_block(block_inputs):
        block_queries, mask_tiles, approx_flag = block_inputs
        key_mask = jnp.repeat(mask_tiles, tile_rows) > 0.5
        scores = (
            jnp.einsum("rd,kd->rk", block_queries, key_rows, preferred_element_type=jnp.float32)
            * score_scale
        )
        approx_score = (
            jnp.dot(block_queries.astype(jnp.float32), key_mean, precision=highest) * score_scale
        )
        approx_live = approx_flag > 0.5
        row_top = jnp.maximum(
            jnp.max(jnp.where(key_mask[None, :], scores, floor_value), axis=1),
            jnp.where(approx_live, approx_score, floor_value),
        )
        weights = jnp.where(key_mask[None, :], jnp.exp(scores - row_top[:, None]), 0.0)
        probabilities = weights.astype(jnp.bfloat16)
        approx_weight = jnp.where(approx_live, jnp.exp(approx_score - row_top), 0.0)
        row_total = jnp.sum(weights, axis=1) + counts_mine * approx_weight
        numerator = jnp.dot(probabilities, value_rows, preferred_element_type=jnp.float32)
        numerator = numerator + approx_weight[:, None] * value_sum[None, :]
        return (row_top, row_total, numerator)

    return lax.map(one_block, (query_blocks, tile_mask, approx_on))


def combine_parts(first_part, second_part):
    top_first, total_first, numer_first = first_part
    top_second, total_second, numer_second = second_part
    joined = jnp.maximum(top_first, top_second)
    factor_first = jnp.exp(top_first - joined)
    factor_second = jnp.exp(top_second - joined)
    return (
        joined,
        total_first * factor_first + total_second * factor_second,
        numer_first * factor_first[..., None] + numer_second * factor_second[..., None],
    )


def local(key_cache, value_cache, prompt_queries, tile_cluster, listed_clusters):
    owners = lax.axis_size("clus")
    owner_index = lax.axis_index("clus")
    moved_keys, moved_values = (
        lax.all_to_all(key_cache, "head", split_axis=2, concat_axis=0, tiled=True),
        lax.all_to_all(value_cache, "head", split_axis=2, concat_axis=0, tiled=True),
    )
    slab_count, slab_rows, feature_width = moved_keys.shape
    heads_dev = feature_width // DH
    tiles_dev = slab_count * slab_rows // TILE

    def to_tiles(moved):
        shaped = moved.reshape(slab_count, slab_rows // TILE, TILE, heads_dev, DH)
        return shaped.transpose(3, 0, 1, 2, 4).reshape(heads_dev, tiles_dev, TILE, DH)

    key_tiles = to_tiles(moved_keys)
    value_tiles = to_tiles(moved_values)
    cluster_ids = tile_cluster.reshape(heads_dev, tiles_dev)
    column_ids = jnp.arange(owners, dtype=jnp.int32)
    member = (cluster_ids[:, :, None] == column_ids[None, None, :]).astype(jnp.float32)
    listed_mask = jnp.max(
        (listed_clusters[:, :, :, None] == column_ids).astype(jnp.float32), axis=2
    )
    owner_hot = (column_ids == owner_index).astype(jnp.float32)
    mine_listed = jnp.einsum("hbc,c->hb", listed_mask, owner_hot, precision=highest)
    query_count = prompt_queries.shape[0]
    block_count = query_count // QBLK
    query_blocks = prompt_queries.reshape(query_count, heads_dev, GROUP, DH).transpose(1, 0, 2, 3)
    query_blocks = query_blocks.reshape(heads_dev, block_count, QBLK * GROUP, DH)
    key_rows = key_tiles.reshape(heads_dev, tiles_dev * TILE, DH)
    value_rows = value_tiles.reshape(heads_dev, tiles_dev * TILE, DH)
    unit_rows = jnp.ones((TILE,), jnp.bfloat16)
    tile_keys = jnp.einsum("htrd,r->htd", key_tiles, unit_rows, preferred_element_type=jnp.float32)
    tile_values = jnp.einsum(
        "htrd,r->htd", value_tiles, unit_rows, preferred_element_type=jnp.float32
    )
    local_keys = jnp.einsum("htc,htd->hcd", member, tile_keys, precision=highest)
    local_values = jnp.einsum("htc,htd->hcd", member, tile_values, precision=highest)
    local_counts = TILE * jnp.sum(member, axis=1)
    total_keys, total_values, total_counts = lax.psum(
        (local_keys, local_values, local_counts), "clus"
    )
    key_sum = jnp.einsum("hcd,c->hd", total_keys, owner_hot, precision=highest)
    value_sum = jnp.einsum("hcd,c->hd", total_values, owner_hot, precision=highest)
    counts_mine = jnp.einsum("hc,c->h", total_counts, owner_hot, precision=highest)
    tile_mask = jnp.einsum("hbc,htc->hbt", listed_mask, member, precision=highest)
    key_mean = key_sum / jnp.maximum(counts_mine, 1.0)[:, None]
    approx_on = (1.0 - mine_listed) * (counts_mine > 0.5).astype(jnp.float32)[:, None]
    row_top, row_total, numerator = jax.vmap(block_partials)(
        query_blocks, key_rows, value_rows, tile_mask, key_mean, value_sum, counts_mine, approx_on
    )
    row_top = row_top.reshape(heads_dev, query_count, GROUP)
    row_total = row_total.reshape(heads_dev, query_count, GROUP)
    numerator = numerator.reshape(heads_dev, query_count, GROUP, DH)
    share_rows = query_count // owners
    merged_top, merged_total, merged_numer = combined_all(
        (row_top, row_total, numerator), "clus", combine_parts
    )
    kept_total = lax.dynamic_slice_in_dim(merged_total, owner_index * share_rows, share_rows, 1)
    kept_numer = lax.dynamic_slice_in_dim(merged_numer, owner_index * share_rows, share_rows, 1)
    attended = kept_numer / kept_total[..., None]
    return (
        attended.transpose(1, 0, 2, 3)
        .reshape(share_rows, heads_dev * GROUP * DH)
        .astype(jnp.bfloat16)
    )


MESH = pl.DeviceIdType.MESH
dead = -1e30
lowest_top = -1e9
log2_scale = math.log2(math.e) * DH**-0.5
nt = (((1,), (1,)), ((), ()))


def fast_kernel(
    k_hbm, v_hbm, q_ref, ids_ref, listed_ref, out_ref,
    kbuf, vbuf, kout, vout, kturn, qx, qall, bt, btx, bias, o_buf, o_rx,
    ts_buf, ts_rx, cs_buf, cs_rx, red_buf, tot_rx, wt, hot_ref,
    loc_sem, kv_send, kv_recv, in_send, in_recv,
    o_send, o_recv, ts_sem, cs_send, cs_recv, tot_send, tot_recv,
):
    x, i = lax.axis_index("head"), lax.axis_index("clus")
    clus = lax.axis_size("clus")
    chips = clus // 2
    c, w = lax.rem(i, 2), i // 2
    sib = i + 1 - 2 * c
    slot = x * chips + w
    rows = k_hbm.shape[0]
    tiles = rows // TILE
    count = float(clus * TILE)
    wide = GROUP * DH
    span = 2 * QBLK * GROUP
    far = jnp.where(i < chips, 1, 0)
    listing = listed_ref.shape[2]

    def pair_of(half, core):
        return 2 * (x if half == 0 else 1 - x) + core

    def kv_copies(half, kind):
        copies = []
        for hh in range(2):
            for n, (src, dst, out) in enumerate(((k_hbm, kbuf, kout), (v_hbm, vbuf, vout))):
                number = half * 4 + hh * 2 + n
                pair = pair_of(half, c if kind == 0 else 1 - c)
                column = pl.ds(pl.multiple_of((pair * 2 + hh) * DH, DH), DH)
                if kind == 0:
                    copies.append(pltpu.make_async_copy(
                        src.at[:, column], dst.at[half, hh, pl.ds(0, rows)], loc_sem.at[0, number]))
                elif kind == 1:
                    copies.append(pltpu.make_async_copy(
                        src.at[:, column], out.at[half, hh], loc_sem.at[1, number]))
                else:
                    copies.append(pltpu.make_async_remote_copy(
                        src_ref=out.at[half, hh], dst_ref=dst.at[half, hh, pl.ds(rows, rows)],
                        send_sem=kv_send.at[number], recv_sem=kv_recv.at[number],
                        device_id=(x, sib), device_id_type=MESH))
        return copies

    def remote(src, dst, send_sem, recv_sem, device):
        return pltpu.make_async_remote_copy(
            src_ref=src, dst_ref=dst, send_sem=send_sem, recv_sem=recv_sem,
            device_id=device, device_id_type=MESH)

    own_kv = [kv_copies(0, 0), kv_copies(1, 0)]
    out_kv = [kv_copies(0, 1), kv_copies(1, 1)]
    far_kv = [kv_copies(0, 2), kv_copies(1, 2)]
    for copy in out_kv[0] + out_kv[1] + own_kv[0] + own_kv[1]:
        copy.start()

    barrier = pltpu.get_barrier_semaphore()

    def ahead(k):
        return jnp.where(i + k >= clus, i + k - clus, i + k)

    def greet(side, k):
        pl.semaphore_signal(barrier, inc=1, device_id=(side, ahead(k)), device_id_type=MESH)

    for k in range(clus):
        greet(1 - x, k)
        if k > 0:
            greet(x, k)

    lane8 = lax.broadcasted_iota(jnp.int32, (8, 128), 1)
    sub8 = lax.broadcasted_iota(jnp.int32, (8, 128), 0)
    for turn in range(2):
        pair = c if turn == 0 else 1 - c
        named = []
        for l in range(listing):
            table = jnp.zeros((8, 128), jnp.int32)
            for hh in range(2):
                for b in range(4):
                    table = jnp.where(sub8 == hh * 4 + b, listed_ref[2 * pair + hh, b, l], table)
            named.append(table)
        first = turn * tiles
        for side in range(2):
            slab = x if side == 0 else 1 - x
            held = jnp.full((8, 128), -1, jnp.int32)
            for hh in range(2):
                for t in range(tiles):
                    here = (lane8 == first + t) & (sub8 // 4 == hh)
                    held = jnp.where(here, ids_ref[2 * (2 * pair + hh) + slab, t], held)
            live = (lane8 < first) | (lane8 >= first + tiles)
            for table in named:
                live = live | (held == table)
            bt[side, turn] = jnp.where(live, 0.0, dead)

    key_tile = lax.broadcasted_iota(jnp.int32, (128, 2 * rows), 1) // TILE
    hot = key_tile == lax.broadcasted_iota(jnp.int32, (128, 2 * rows), 0)
    hot_ref[...] = jnp.where(hot, 1.0, 0.0).astype(jnp.bfloat16)

    def turn_keys(half, side):
        def turn(n, carry):
            hh, first = n // 2, pl.multiple_of(side * rows + lax.rem(n, 2) * (rows // 2), 128)
            for head in range(2):
                @pl.when(hh == head)
                def _():
                    part = kbuf[half, head, pl.ds(first, rows // 2), :]
                    kturn[half, head, :, pl.ds(first, rows // 2)] = part.T
            return carry

        lax.fori_loop(0, 4, turn, 0)

    def regroup(rows_in):
        count_in = rows_in.shape[0]
        split = rows_in.astype(jnp.float32).reshape(count_in, GROUP, DH)
        return split.reshape(count_in * GROUP, DH).astype(jnp.bfloat16)

    def place_queries(half, source, first):
        def block_of(n, carry):
            hh, block = n // 4, lax.rem(n, 4)
            for head in range(2):
                @pl.when(hh == head)
                def _():
                    columns = pl.ds(pl.multiple_of(first + head * wide, 128), wide)
                    taken = source[pl.ds(pl.multiple_of(block * QBLK, QBLK), QBLK), columns]
                    qall[half, head, pl.ds(pl.multiple_of(block * 128, 128), 128), :] = regroup(
                        taken)
            return carry

        lax.fori_loop(0, 8, block_of, 0)

    place_queries(0, q_ref, c * 2 * wide)
    pl.semaphore_wait(barrier, 2 * clus - 1)
    for copy in out_kv[0] + out_kv[1]:
        copy.wait()

    small = [
        remote(bt.at[0, 1], btx.at[0], in_send.at[0], in_recv.at[0], (x, sib)),
        remote(bt.at[1, 0], btx.at[1], in_send.at[1], in_recv.at[1], (1 - x, i)),
        remote(bt.at[1, 1], btx.at[2], in_send.at[2], in_recv.at[2], (1 - x, sib)),
        remote(q_ref.at[:, pl.ds(pl.multiple_of(c * 2 * wide, 128), 2 * wide)], qx,
               in_send.at[3], in_recv.at[3], (1 - x, i)),
    ]
    for copy in small + far_kv[0] + far_kv[1]:
        copy.start()

    for copy in own_kv[0] + own_kv[1]:
        copy.wait()

    def add_up(n, carry):
        half, hh = n // 2, lax.rem(n, 2)
        for m, (buf, out) in enumerate(((kbuf, kout), (vbuf, vout))):
            for part, core in ((buf[half, hh, :rows], c), (out[half, hh], 1 - c)):
                ts_buf[half, m, 2 * core + hh] = jnp.sum(
                    part.astype(jnp.float32).reshape(tiles, TILE, DH), axis=1)
        return carry

    lax.fori_loop(0, 4, add_up, 0)
    turn_keys(0, 0)
    ts_copy = remote(ts_buf.at[1], ts_rx, ts_sem.at[0], ts_sem.at[1], (1 - x, i))
    ts_copy.start()

    square = lax.broadcasted_iota(jnp.int32, (128, 128), 0) == lax.broadcasted_iota(
        jnp.int32, (128, 128), 1)

    def as_row(column):
        return jnp.sum(jnp.where(square, column, 0.0), axis=0, keepdims=True)

    sub16 = lax.broadcasted_iota(jnp.int32, (16, 128), 0)

    def attend(half, pair, hh, stats):
        start = pl.multiple_of(pair * span, span)
        masks = [
            jnp.broadcast_to(bias[half, pl.ds(hh * 4 + pair * 2 + n, 1), :], (128, 128))
            for n in range(2)
        ]
        masks = jnp.concatenate(masks, axis=0).astype(jnp.bfloat16)
        queries = jnp.concatenate([qall[half, hh, pl.ds(start, span), :], masks], axis=1)
        keys = jnp.concatenate([kturn[half, hh], hot_ref[...]], axis=0)
        scores = jnp.dot(queries, keys, preferred_element_type=jnp.float32)
        top = jnp.maximum(jnp.max(scores, axis=1, keepdims=True), lowest_top) * log2_scale
        top = top.astype(jnp.bfloat16).astype(jnp.float32)
        weights = jnp.exp2(scores * log2_scale - top).astype(jnp.bfloat16)
        values = jnp.concatenate(
            [vbuf[half, hh], jnp.ones((2 * rows, 128), jnp.bfloat16)], axis=1)
        numer = jnp.dot(weights, values, preferred_element_type=jnp.float32)
        after = []
        for n in range(2):
            part = slice(128 * n, 128 * (n + 1))
            total = as_row(numer[part, DH:])
            upper = total.astype(jnp.bfloat16).astype(jnp.float32)
            held = stats[n]
            for r, row in enumerate((as_row(top[part]), upper, total - upper)):
                held = jnp.where(sub16 == hh * 3 + r, row, held)
            after.append(held)
            for j in range(4):
                first = 128 * n + 32 * j
                place = pl.ds(pl.multiple_of(hh * 32, 32), 32)
                o_buf[half * clus + pair * 8 + n * 4 + j, place, :] = numer[
                    first : first + 32, :DH].astype(jnp.bfloat16)
        return tuple(after)

    def ship(half, dest):
        src = o_buf.at[half * clus + dest]
        here = (half == 0) & (dest == i)

        @pl.when(jnp.logical_not(here))
        def _():
            remote(src, o_rx.at[c, slot], o_send, o_recv, (x + half * (1 - 2 * x), dest)).start()

        @pl.when(here)
        def _():
            pltpu.make_async_copy(src, o_rx.at[c, slot], o_recv).start()

    def first_half():
        small[0].wait_recv()
        for copy in far_kv[0]:
            copy.wait_recv()
        turn_keys(0, 1)
        bias[0] = bt[0, 0] + btx[0]

    def second_half():
        for copy in small[1:]:
            copy.wait_recv()
        for copy in far_kv[1]:
            copy.wait_recv()
        place_queries(1, qx, 0)
        turn_keys(1, 0)
        turn_keys(1, 1)
        bias[1] = btx[1] + btx[2]

    line = lax.broadcasted_iota(jnp.int32, (128, 128), 0)

    def cluster_sums():
        lane = lax.rem(lane8, 8 * tiles)
        held = jnp.zeros((8, 128), jnp.int32)
        for h in range(4):
            for side in range(2):
                slab = x if side == 0 else 1 - x
                for t in range(tiles):
                    held = jnp.where(
                        lane == (h * 2 + side) * tiles + t, ids_ref[2 * h + slab, t], held)
        held = jnp.concatenate([held] * 16, axis=0)
        column = lax.broadcasted_iota(jnp.int32, (128, 128), 1)
        belongs = (held == line // 8) & (lax.rem(line, 8) == column // (2 * tiles))
        ts_copy.wait_recv()
        all_sums = jnp.concatenate(
            [ts_buf[0].reshape(8, tiles, DH), ts_rx[...].reshape(8, tiles, DH)], axis=1
        ).reshape(16 * tiles, DH)
        clustered = jnp.dot(
            jnp.where(belongs, 1.0, 0.0), all_sums, precision=highest,
            preferred_element_type=jnp.float32)
        cs_buf[...] = clustered.reshape(clus, 8, DH)
        cs_rx[i] = cs_buf[i]
        lax.fori_loop(1, clus, start_cs, 0)

    def cs_copy(k):
        other = lax.rem(i + k, clus)
        return remote(cs_buf.at[other], cs_rx.at[i], cs_send, cs_recv, (x, other))

    def start_cs(k, carry):
        cs_copy(k).start()
        return carry

    def tot_copy(k):
        return remote(red_buf, tot_rx.at[i], tot_send, tot_recv, (x, lax.rem(i + k, clus)))

    def start_tot(k, carry):
        tot_copy(k).start()
        return carry

    def take_all(buf, amount, sem):
        part = buf.at[pl.ds(0, amount)]
        pltpu.make_async_copy(part, part, sem).wait()

    def reduce_sums():
        take_all(cs_rx, clus - 1, cs_recv)
        reduced = jnp.sum(cs_rx[...], axis=0)
        red_buf[...] = reduced
        tot_rx[i] = reduced
        lax.fori_loop(1, clus, start_tot, 0)

    hooks = ((first_half,), (cluster_sums,), (reduce_sums, second_half))

    def step(n, carry):
        half, pair = n // 2, lax.rem(n + far, 2)
        for number, hook in enumerate(hooks):
            @pl.when(n == number)
            def _():
                for work in hook:
                    work()

        blank = jnp.zeros((16, 128), jnp.float32)
        stats = lax.fori_loop(
            0, 2, lambda hh, held: attend(half, pair, hh, held), (blank, blank))
        for n in range(2):
            packed = stats[n].astype(jnp.bfloat16)
            for j in range(4):
                o_buf[half * clus + pair * 8 + n * 4 + j, 64:80, :] = packed

        def one_dest(k, inner):
            ship(half, pair * 8 + lax.rem(k + i, 8))
            return inner

        lax.fori_loop(0, 8, one_dest, 0)
        return carry

    lax.fori_loop(0, 4, step, 0)
    take_all(tot_rx, clus - 1, tot_recv)
    block, part = i // 4, lax.rem(i, 4)
    share = pl.ds(pl.multiple_of(part * 32, 32), 32)
    totals = tot_rx[...].reshape(clus * 8, DH)
    approx_parts = []
    for h in range(4):
        taken = q_ref[pl.ds(pl.multiple_of(block * QBLK, QBLK), QBLK), h * wide : (h + 1) * wide]
        queries = regroup(taken).astype(jnp.float32)
        approx = lax.dot_general(
            totals, queries, nt, precision=highest, preferred_element_type=jnp.float32)
        usable = lax.rem(line, 8) == h
        for l in range(listing):
            usable = usable & (line // 8 != listed_ref[h, block, l])
        approx = jnp.where(usable, approx * (log2_scale / count), dead)
        top = jnp.max(approx, axis=0, keepdims=True)
        approx_weight = jnp.where(usable, jnp.exp2(approx - top), 0.0)
        total = count * jnp.sum(approx_weight, axis=0, keepdims=True)
        wt[h] = pltpu.roll(approx_weight, 4, 0).T
        numer = jnp.dot(
            wt[h, share, :], totals, precision=highest, preferred_element_type=jnp.float32)
        approx_parts.append((top, total, numer))

    take_all(o_rx, 2, o_recv)
    for h in range(4):
        p, hh = h // 2, h % 2
        held = o_rx[p, :, 64:80, :].astype(jnp.float32)
        tops, sums = held[:, 3 * hh, :], held[:, 3 * hh + 1, :] + held[:, 3 * hh + 2, :]
        approx_top, approx_total, _ = approx_parts[h]
        top = jnp.maximum(jnp.max(tops, axis=0, keepdims=True), approx_top)
        factor = jnp.exp2(tops - top)
        approx_factor = jnp.exp2(approx_top - top)
        total = jnp.sum(factor * sums, axis=0, keepdims=True) + approx_factor * approx_total
        inverse = 1.0 / total
        mixed = jnp.concatenate(
            [factor * inverse, jnp.broadcast_to(approx_factor * inverse, (8, 128)),
             jnp.zeros((104, 128), jnp.float32)], axis=0)
        wt[4 + h] = mixed.T
    for h in range(4):
        p, hh = h // 2, h % 2
        mine = wt[4 + h, share, :]
        numer = mine[:, 2 * chips : 2 * chips + 1] * approx_parts[h][2]
        for source in range(2 * chips):
            numer = numer + mine[:, source : source + 1] * o_rx[p, source, 32 * hh : 32 * (hh + 1), :].astype(jnp.float32)
        out_ref[h] = numer.astype(jnp.bfloat16)

    for copy in small + far_kv[0] + far_kv[1] + [ts_copy]:
        copy.wait_send()

    take_all(cs_buf, clus - 1, cs_send)
    take_all(tot_rx, clus - 1, tot_send)
    take_all(o_buf, 2 * clus - 1, o_send)


def fast_local(key_cache, value_cache, prompt_queries, tile_cluster, listed_clusters):
    clus = lax.axis_size("clus")
    _, rows, width = key_cache.shape
    tiles = rows // TILE
    query_count = prompt_queries.shape[0]
    heads = prompt_queries.shape[1] // (GROUP * DH)
    blocks = query_count // QBLK
    dma = pltpu.SemaphoreType.DMA
    f32, bf16 = jnp.float32, jnp.bfloat16
    share = query_count * GROUP // clus
    vmem = pl.BlockSpec(memory_space=pltpu.VMEM)
    smem = pl.BlockSpec(memory_space=pltpu.SMEM)
    hbm = pl.BlockSpec(memory_space=pltpu.HBM)
    out = pl.pallas_call(
        fast_kernel,
        out_shape=jax.ShapeDtypeStruct((heads, share, DH), bf16),
        in_specs=[hbm, hbm, vmem, smem, smem],
        out_specs=vmem,
        scratch_shapes=[
            pltpu.VMEM((2, 2, 2 * rows, DH), bf16),
            pltpu.VMEM((2, 2, 2 * rows, DH), bf16),
            pltpu.VMEM((2, 2, rows, DH), bf16),
            pltpu.VMEM((2, 2, rows, DH), bf16),
            pltpu.VMEM((2, 2, DH, 2 * rows), bf16),
            pltpu.VMEM((query_count, 2 * GROUP * DH), bf16),
            pltpu.VMEM((2, 2, query_count * GROUP, DH), bf16),
            pltpu.VMEM((2, 2, 2 * blocks, 128), f32),
            pltpu.VMEM((3, 2 * blocks, 128), f32),
            pltpu.VMEM((2, 2 * blocks, 128), f32),
            pltpu.VMEM((2 * clus, 2 * share + 16, DH), bf16),
            pltpu.VMEM((2, clus, 2 * share + 16, DH), bf16),
            pltpu.VMEM((2, 2, heads, tiles, DH), f32),
            pltpu.VMEM((2, heads, tiles, DH), f32),
            pltpu.VMEM((clus, 8, DH), f32),
            pltpu.VMEM((clus, 8, DH), f32),
            pltpu.VMEM((8, DH), f32),
            pltpu.VMEM((clus, 8, DH), f32),
            pltpu.VMEM((8, 128, 128), f32),
            pltpu.VMEM((128, 2 * rows), bf16),
            dma((2, 8)), dma((8,)), dma((8,)), dma((4,)), dma((4,)),
            dma, dma, dma((2,)), dma, dma, dma, dma,
        ],
        compiler_params=pltpu.CompilerParams(
            collective_id=0, has_side_effects=True, vmem_limit_bytes=56 * 1024 * 1024),
    )(
        key_cache.reshape(rows, width), value_cache.reshape(rows, width),
        prompt_queries, tile_cluster.reshape(2 * heads, tiles), listed_clusters,
    )
    out = out.reshape(heads, query_count // clus, GROUP, DH).transpose(1, 0, 2, 3)
    return out.reshape(query_count // clus, heads * GROUP * DH)


def solution(mesh):
    placed = (
        P("head", "clus", None),
        P("head", "clus", None),
        P(None, "head"),
        P("head", "clus", None, None, None),
        P("head", None, None),
    )
    fits = mesh.shape["head"] == 2 and mesh.shape["clus"] == 16
    return jax.shard_map(
        fast_local if fits else local,
        mesh=mesh,
        in_specs=placed,
        out_specs=P("clus", "head"),
        check_vma=False,
    )
```

```python
import functools
import math

import jax
import jax.numpy as jnp
from jax import lax
from jax.experimental import pallas as pl
from jax.experimental.pallas import tpu as pltpu
from jax.sharding import PartitionSpec as P

DH = 128
GROUP = 8
TILE = 128
QBLK = 16


floor_value = -1e30
highest = lax.Precision.HIGHEST


def combined_all(shard, axis, combine):
    everything = jax.tree.map(lambda part: lax.all_gather(part, axis), shard)
    leading = jax.tree.map(lambda part: part[0], everything)

    def turn(k, so_far):
        return combine(so_far, jax.tree.map(lambda part: part[k], everything))

    return lax.fori_loop(1, lax.axis_size(axis), turn, leading)


def block_partials(
    query_blocks, key_rows, value_rows, tile_mask, key_mean, value_sum, counts_mine, approx_on
):
    score_scale = key_rows.shape[-1] ** (-0.5)
    tile_rows = key_rows.shape[0] // tile_mask.shape[-1]

    def one_block(block_inputs):
        block_queries, mask_tiles, approx_flag = block_inputs
        key_mask = jnp.repeat(mask_tiles, tile_rows) > 0.5
        scores = (
            jnp.einsum("rd,kd->rk", block_queries, key_rows, preferred_element_type=jnp.float32)
            * score_scale
        )
        approx_score = (
            jnp.dot(block_queries.astype(jnp.float32), key_mean, precision=highest) * score_scale
        )
        approx_live = approx_flag > 0.5
        row_top = jnp.maximum(
            jnp.max(jnp.where(key_mask[None, :], scores, floor_value), axis=1),
            jnp.where(approx_live, approx_score, floor_value),
        )
        weights = jnp.where(key_mask[None, :], jnp.exp(scores - row_top[:, None]), 0.0)
        probabilities = weights.astype(jnp.bfloat16)
        approx_weight = jnp.where(approx_live, jnp.exp(approx_score - row_top), 0.0)
        row_total = jnp.sum(weights, axis=1) + counts_mine * approx_weight
        numerator = jnp.dot(probabilities, value_rows, preferred_element_type=jnp.float32)
        numerator = numerator + approx_weight[:, None] * value_sum[None, :]
        return (row_top, row_total, numerator)

    return lax.map(one_block, (query_blocks, tile_mask, approx_on))


def combine_parts(first_part, second_part):
    top_first, total_first, numer_first = first_part
    top_second, total_second, numer_second = second_part
    joined = jnp.maximum(top_first, top_second)
    factor_first = jnp.exp(top_first - joined)
    factor_second = jnp.exp(top_second - joined)
    return (
        joined,
        total_first * factor_first + total_second * factor_second,
        numer_first * factor_first[..., None] + numer_second * factor_second[..., None],
    )


def local(key_cache, value_cache, prompt_queries, tile_cluster, listed_clusters):
    owners = lax.axis_size("clus")
    owner_index = lax.axis_index("clus")
    moved_keys, moved_values = (
        lax.all_to_all(key_cache, "head", split_axis=2, concat_axis=0, tiled=True),
        lax.all_to_all(value_cache, "head", split_axis=2, concat_axis=0, tiled=True),
    )
    slab_count, slab_rows, feature_width = moved_keys.shape
    heads_dev = feature_width // DH
    tiles_dev = slab_count * slab_rows // TILE

    def to_tiles(moved):
        shaped = moved.reshape(slab_count, slab_rows // TILE, TILE, heads_dev, DH)
        return shaped.transpose(3, 0, 1, 2, 4).reshape(heads_dev, tiles_dev, TILE, DH)

    key_tiles = to_tiles(moved_keys)
    value_tiles = to_tiles(moved_values)
    cluster_ids = tile_cluster.reshape(heads_dev, tiles_dev)
    column_ids = jnp.arange(owners, dtype=jnp.int32)
    member = (cluster_ids[:, :, None] == column_ids[None, None, :]).astype(jnp.float32)
    listed_mask = jnp.max(
        (listed_clusters[:, :, :, None] == column_ids).astype(jnp.float32), axis=2
    )
    owner_hot = (column_ids == owner_index).astype(jnp.float32)
    mine_listed = jnp.einsum("hbc,c->hb", listed_mask, owner_hot, precision=highest)
    query_count = prompt_queries.shape[0]
    block_count = query_count // QBLK
    query_blocks = prompt_queries.reshape(query_count, heads_dev, GROUP, DH).transpose(1, 0, 2, 3)
    query_blocks = query_blocks.reshape(heads_dev, block_count, QBLK * GROUP, DH)
    key_rows = key_tiles.reshape(heads_dev, tiles_dev * TILE, DH)
    value_rows = value_tiles.reshape(heads_dev, tiles_dev * TILE, DH)
    unit_rows = jnp.ones((TILE,), jnp.bfloat16)
    tile_keys = jnp.einsum("htrd,r->htd", key_tiles, unit_rows, preferred_element_type=jnp.float32)
    tile_values = jnp.einsum(
        "htrd,r->htd", value_tiles, unit_rows, preferred_element_type=jnp.float32
    )
    local_keys = jnp.einsum("htc,htd->hcd", member, tile_keys, precision=highest)
    local_values = jnp.einsum("htc,htd->hcd", member, tile_values, precision=highest)
    local_counts = TILE * jnp.sum(member, axis=1)
    total_keys, total_values, total_counts = lax.psum(
        (local_keys, local_values, local_counts), "clus"
    )
    key_sum = jnp.einsum("hcd,c->hd", total_keys, owner_hot, precision=highest)
    value_sum = jnp.einsum("hcd,c->hd", total_values, owner_hot, precision=highest)
    counts_mine = jnp.einsum("hc,c->h", total_counts, owner_hot, precision=highest)
    tile_mask = jnp.einsum("hbc,htc->hbt", listed_mask, member, precision=highest)
    key_mean = key_sum / jnp.maximum(counts_mine, 1.0)[:, None]
    approx_on = (1.0 - mine_listed) * (counts_mine > 0.5).astype(jnp.float32)[:, None]
    row_top, row_total, numerator = jax.vmap(block_partials)(
        query_blocks, key_rows, value_rows, tile_mask, key_mean, value_sum, counts_mine, approx_on
    )
    row_top = row_top.reshape(heads_dev, query_count, GROUP)
    row_total = row_total.reshape(heads_dev, query_count, GROUP)
    numerator = numerator.reshape(heads_dev, query_count, GROUP, DH)
    share_rows = query_count // owners
    merged_top, merged_total, merged_numer = combined_all(
        (row_top, row_total, numerator), "clus", combine_parts
    )
    kept_total = lax.dynamic_slice_in_dim(merged_total, owner_index * share_rows, share_rows, 1)
    kept_numer = lax.dynamic_slice_in_dim(merged_numer, owner_index * share_rows, share_rows, 1)
    attended = kept_numer / kept_total[..., None]
    return (
        attended.transpose(1, 0, 2, 3)
        .reshape(share_rows, heads_dev * GROUP * DH)
        .astype(jnp.bfloat16)
    )


MESH = pl.DeviceIdType.MESH
dead = -1e30
lowest_top = -1e9
log2_scale = math.log2(math.e) * DH**-0.5
nt = (((1,), (1,)), ((), ()))


def fast_kernel(
    k_hbm, v_hbm, q_ref, ids_ref, listed_ref, out_ref,
    kbuf, vbuf, kout, vout, qx, qall, bt, btx, bias, o_buf, o_rx,
    ts_buf, ts_rx, cs_buf, cs_rx, red_buf, tot_rx, wt, hot_ref,
    loc_sem, kv_send, kv_recv, in_send, in_recv,
    o_send, o_recv, ts_sem, cs_send, cs_recv, tot_send, tot_recv,
):
    x, i = lax.axis_index("head"), lax.axis_index("clus")
    clus = lax.axis_size("clus")
    chips = clus // 2
    c, w = lax.rem(i, 2), i // 2
    sib = i + 1 - 2 * c
    slot = x * chips + w
    rows = k_hbm.shape[0]
    tiles = rows // TILE
    count = float(clus * TILE)
    wide = GROUP * DH
    span = 2 * QBLK * GROUP
    far = jnp.where(i < chips, 1, 0)
    listing = listed_ref.shape[2]

    def pair_of(half, core):
        return 2 * (x if half == 0 else 1 - x) + core

    def kv_copies(half, kind):
        copies = []
        for hh in range(2):
            for n, (src, dst, out) in enumerate(((k_hbm, kbuf, kout), (v_hbm, vbuf, vout))):
                number = half * 4 + hh * 2 + n
                pair = pair_of(half, c if kind == 0 else 1 - c)
                column = pl.ds(pl.multiple_of((pair * 2 + hh) * DH, DH), DH)
                if kind == 0:
                    copies.append(pltpu.make_async_copy(
                        src.at[:, column], dst.at[half, hh, pl.ds(0, rows)], loc_sem.at[0, number]))
                elif kind == 1:
                    copies.append(pltpu.make_async_copy(
                        src.at[:, column], out.at[half, hh], loc_sem.at[1, number]))
                else:
                    copies.append(pltpu.make_async_remote_copy(
                        src_ref=src.at[:, column], dst_ref=dst.at[half, hh, pl.ds(rows, rows)],
                        send_sem=kv_send.at[number], recv_sem=kv_recv.at[number],
                        device_id=(x, sib), device_id_type=MESH))
        return copies

    def remote(src, dst, send_sem, recv_sem, device):
        return pltpu.make_async_remote_copy(
            src_ref=src, dst_ref=dst, send_sem=send_sem, recv_sem=recv_sem,
            device_id=device, device_id_type=MESH)

    own_kv = [kv_copies(0, 0), kv_copies(1, 0)]
    out_kv = [kv_copies(0, 1), kv_copies(1, 1)]
    far_kv = [kv_copies(0, 2), kv_copies(1, 2)]
    for copy in own_kv[0] + own_kv[1] + out_kv[0] + out_kv[1]:
        copy.start()

    barrier = pltpu.get_barrier_semaphore()

    def ahead(k):
        return jnp.where(i + k >= clus, i + k - clus, i + k)

    def greet(side, k):
        pl.semaphore_signal(barrier, inc=1, device_id=(side, ahead(k)), device_id_type=MESH)

    for k in range(clus):
        greet(1 - x, k)
        if k > 0:
            greet(x, k)

    lane8 = lax.broadcasted_iota(jnp.int32, (8, 128), 1)
    sub8 = lax.broadcasted_iota(jnp.int32, (8, 128), 0)
    for turn in range(2):
        pair = c if turn == 0 else 1 - c
        named = []
        for l in range(listing):
            table = jnp.zeros((8, 128), jnp.int32)
            for hh in range(2):
                for b in range(4):
                    table = jnp.where(sub8 == hh * 4 + b, listed_ref[2 * pair + hh, b, l], table)
            named.append(table)
        first = turn * tiles
        for side in range(2):
            slab = x if side == 0 else 1 - x
            held = jnp.full((8, 128), -1, jnp.int32)
            for hh in range(2):
                for t in range(tiles):
                    here = (lane8 == first + t) & (sub8 // 4 == hh)
                    held = jnp.where(here, ids_ref[2 * (2 * pair + hh) + slab, t], held)
            live = (lane8 < first) | (lane8 >= first + tiles)
            for table in named:
                live = live | (held == table)
            bt[side, turn] = jnp.where(live, 0.0, dead)

    key_tile = lax.broadcasted_iota(jnp.int32, (2 * rows, 128), 0) // TILE
    hot = key_tile == lax.broadcasted_iota(jnp.int32, (2 * rows, 128), 1)
    hot_ref[...] = jnp.where(hot, 1.0, 0.0).astype(jnp.bfloat16)

    def regroup(rows_in):
        count_in = rows_in.shape[0]
        split = rows_in.astype(jnp.float32).reshape(count_in, GROUP, DH)
        return split.reshape(count_in * GROUP, DH).astype(jnp.bfloat16)

    def place_queries(half, source, first):
        def block_of(n, carry):
            hh, block = n // 4, lax.rem(n, 4)
            for head in range(2):
                @pl.when(hh == head)
                def _():
                    columns = pl.ds(pl.multiple_of(first + head * wide, 128), wide)
                    taken = source[pl.ds(pl.multiple_of(block * QBLK, QBLK), QBLK), columns]
                    qall[half, head, pl.ds(pl.multiple_of(block * 128, 128), 128), :] = regroup(
                        taken)
            return carry

        lax.fori_loop(0, 8, block_of, 0)

    place_queries(0, q_ref, c * 2 * wide)
    pl.semaphore_wait(barrier, 2 * clus - 1)

    small = [
        remote(bt.at[0, 1], btx.at[0], in_send.at[0], in_recv.at[0], (x, sib)),
        remote(bt.at[1, 0], btx.at[1], in_send.at[1], in_recv.at[1], (1 - x, i)),
        remote(bt.at[1, 1], btx.at[2], in_send.at[2], in_recv.at[2], (1 - x, sib)),
        remote(q_ref.at[:, pl.ds(pl.multiple_of(c * 2 * wide, 128), 2 * wide)], qx,
               in_send.at[3], in_recv.at[3], (1 - x, i)),
    ]
    for copy in small[:1] + small[3:] + far_kv[0] + small[1:3] + far_kv[1]:
        copy.start()

    ts_copy = remote(ts_buf.at[1], ts_rx, ts_sem.at[0], ts_sem.at[1], (1 - x, i))

    def tile_sums():
        for copy in own_kv[1] + out_kv[0] + out_kv[1]:
            copy.wait()

        def add_up(n, carry):
            half, hh = n // 2, lax.rem(n, 2)
            for m, (buf, out) in enumerate(((kbuf, kout), (vbuf, vout))):
                for part, core in ((buf[half, hh, :rows], c), (out[half, hh], 1 - c)):
                    ts_buf[half, m, 2 * core + hh] = jnp.sum(
                        part.astype(jnp.float32).reshape(tiles, TILE, DH), axis=1)
            return carry

        lax.fori_loop(0, 4, add_up, 0)
        ts_copy.start()

    square = lax.broadcasted_iota(jnp.int32, (128, 128), 0) == lax.broadcasted_iota(
        jnp.int32, (128, 128), 1)

    def as_row(column):
        return jnp.sum(jnp.where(square, column, 0.0), axis=0, keepdims=True)

    sub16 = lax.broadcasted_iota(jnp.int32, (16, 128), 0)

    def attend(half, pair, hh, stats):
        start = pl.multiple_of(pair * span, span)
        masks = [
            jnp.broadcast_to(bias[half, pl.ds(hh * 4 + pair * 2 + n, 1), :], (128, 128))
            for n in range(2)
        ]
        masks = jnp.concatenate(masks, axis=0).astype(jnp.bfloat16)
        queries = jnp.concatenate([qall[half, hh, pl.ds(start, span), :], masks], axis=1)
        keys = jnp.concatenate([kbuf[half, hh], hot_ref[...]], axis=1)
        scores = lax.dot_general(queries, keys, nt, preferred_element_type=jnp.float32)
        top = jnp.maximum(jnp.max(scores, axis=1, keepdims=True), lowest_top) * log2_scale
        top = top.astype(jnp.bfloat16).astype(jnp.float32)
        weights = jnp.exp2(scores * log2_scale - top).astype(jnp.bfloat16)
        values = jnp.concatenate(
            [vbuf[half, hh], jnp.ones((2 * rows, 128), jnp.bfloat16)], axis=1)
        numer = jnp.dot(weights, values, preferred_element_type=jnp.float32)
        after = []
        for n in range(2):
            part = slice(128 * n, 128 * (n + 1))
            total = as_row(numer[part, DH:])
            upper = total.astype(jnp.bfloat16).astype(jnp.float32)
            held = stats[n]
            for r, row in enumerate((as_row(top[part]), upper, total - upper)):
                held = jnp.where(sub16 == hh * 3 + r, row, held)
            after.append(held)
            for j in range(4):
                first = 128 * n + 32 * j
                place = pl.ds(hh * 32, 32)
                o_buf[half * clus + pair * 8 + n * 4 + j, place, :] = numer[
                    first : first + 32, :DH].astype(jnp.bfloat16)
        return tuple(after)

    def ship(half, dest):
        src = o_buf.at[half * clus + dest]
        here = (half == 0) & (dest == i)

        @pl.when(jnp.logical_not(here))
        def _():
            remote(src, o_rx.at[c, slot], o_send, o_recv, (x + half * (1 - 2 * x), dest)).start()

        @pl.when(here)
        def _():
            pltpu.make_async_copy(src, o_rx.at[c, slot], o_recv).start()

    def first_half():
        for copy in own_kv[0]:
            copy.wait()
        small[0].wait_recv()
        for copy in far_kv[0]:
            copy.wait_recv()
        bias[0] = bt[0, 0] + btx[0]

    def second_half():
        for copy in small[1:]:
            copy.wait_recv()
        for copy in far_kv[1]:
            copy.wait_recv()
        place_queries(1, qx, 0)
        bias[1] = btx[1] + btx[2]

    line = lax.broadcasted_iota(jnp.int32, (128, 128), 0)

    def cluster_sums():
        lane = lax.rem(lane8, 8 * tiles)
        held = jnp.zeros((8, 128), jnp.int32)
        for h in range(4):
            for side in range(2):
                slab = x if side == 0 else 1 - x
                for t in range(tiles):
                    held = jnp.where(
                        lane == (h * 2 + side) * tiles + t, ids_ref[2 * h + slab, t], held)
        held = jnp.concatenate([held] * 16, axis=0)
        column = lax.broadcasted_iota(jnp.int32, (128, 128), 1)
        belongs = (held == line // 8) & (lax.rem(line, 8) == column // (2 * tiles))
        ts_copy.wait_recv()
        all_sums = jnp.concatenate(
            [ts_buf[0].reshape(8, tiles, DH), ts_rx[...].reshape(8, tiles, DH)], axis=1
        ).reshape(16 * tiles, DH)
        clustered = jnp.dot(
            jnp.where(belongs, 1.0, 0.0), all_sums, precision=highest,
            preferred_element_type=jnp.float32)
        cs_buf[...] = clustered.reshape(clus, 8, DH)
        cs_rx[i] = cs_buf[i]
        lax.fori_loop(1, clus, start_cs, 0)

    def cs_copy(k):
        other = lax.rem(i + k, clus)
        return remote(cs_buf.at[other], cs_rx.at[i], cs_send, cs_recv, (x, other))

    def start_cs(k, carry):
        cs_copy(k).start()
        return carry

    def tot_copy(k):
        return remote(red_buf, tot_rx.at[i], tot_send, tot_recv, (x, lax.rem(i + k, clus)))

    def start_tot(k, carry):
        tot_copy(k).start()
        return carry

    def take_all(buf, amount, sem):
        part = buf.at[pl.ds(0, amount)]
        pltpu.make_async_copy(part, part, sem).wait()

    def reduce_sums():
        take_all(cs_rx, clus - 1, cs_recv)
        reduced = jnp.sum(cs_rx[...], axis=0)
        red_buf[...] = reduced
        tot_rx[i] = reduced
        lax.fori_loop(1, clus, start_tot, 0)

    hooks = ((first_half,), (tile_sums,), (second_half, cluster_sums), (reduce_sums,))

    def step(n, carry):
        half, pair = n // 2, lax.rem(n + far, 2)
        for number, hook in enumerate(hooks):
            @pl.when(n == number)
            def _():
                for work in hook:
                    work()

        blank = jnp.zeros((16, 128), jnp.float32)
        stats = (blank, blank)
        for hh in range(2):
            stats = attend(half, pair, hh, stats)
        for n in range(2):
            packed = stats[n].astype(jnp.bfloat16)
            for j in range(4):
                o_buf[half * clus + pair * 8 + n * 4 + j, 64:80, :] = packed

        def one_dest(k, inner):
            ship(half, pair * 8 + lax.rem(k + i, 8))
            return inner

        lax.fori_loop(0, 8, one_dest, 0)
        return carry

    lax.fori_loop(0, 4, step, 0)
    take_all(tot_rx, clus - 1, tot_recv)
    block, part = i // 4, lax.rem(i, 4)
    share = pl.ds(pl.multiple_of(part * 32, 32), 32)
    totals = tot_rx[...].reshape(clus * 8, DH)
    approx_parts = []
    for h in range(4):
        taken = q_ref[pl.ds(pl.multiple_of(block * QBLK, QBLK), QBLK), h * wide : (h + 1) * wide]
        queries = regroup(taken).astype(jnp.float32)
        approx = lax.dot_general(
            totals, queries, nt, precision=highest, preferred_element_type=jnp.float32)
        usable = lax.rem(line, 8) == h
        for l in range(listing):
            usable = usable & (line // 8 != listed_ref[h, block, l])
        approx = jnp.where(usable, approx * (log2_scale / count), dead)
        top = jnp.max(approx, axis=0, keepdims=True)
        approx_weight = jnp.where(usable, jnp.exp2(approx - top), 0.0)
        total = count * jnp.sum(approx_weight, axis=0, keepdims=True)
        wt[h] = pltpu.roll(approx_weight, 4, 0).T
        numer = jnp.dot(
            wt[h, share, :], totals, precision=highest, preferred_element_type=jnp.float32)
        approx_parts.append((top, total, numer))

    take_all(o_rx, 2, o_recv)
    for h in range(4):
        p, hh = h // 2, h % 2
        held = o_rx[p, :, 64:80, :].astype(jnp.float32)
        tops, sums = held[:, 3 * hh, :], held[:, 3 * hh + 1, :] + held[:, 3 * hh + 2, :]
        approx_top, approx_total, _ = approx_parts[h]
        top = jnp.maximum(jnp.max(tops, axis=0, keepdims=True), approx_top)
        factor = jnp.exp2(tops - top)
        approx_factor = jnp.exp2(approx_top - top)
        total = jnp.sum(factor * sums, axis=0, keepdims=True) + approx_factor * approx_total
        inverse = 1.0 / total
        mixed = jnp.concatenate(
            [factor * inverse, jnp.broadcast_to(approx_factor * inverse, (8, 128)),
             jnp.zeros((104, 128), jnp.float32)], axis=0)
        wt[4 + h] = mixed.T
    for h in range(4):
        p, hh = h // 2, h % 2
        mine = wt[4 + h, share, :]
        numer = mine[:, 2 * chips : 2 * chips + 1] * approx_parts[h][2]
        for source in range(2 * chips):
            numer = numer + mine[:, source : source + 1] * o_rx[p, source, 32 * hh : 32 * (hh + 1), :].astype(jnp.float32)
        out_ref[h] = numer.astype(jnp.bfloat16)

    for copy in small + far_kv[0] + far_kv[1] + [ts_copy]:
        copy.wait_send()

    take_all(cs_buf, clus - 1, cs_send)
    take_all(tot_rx, clus - 1, tot_send)
    take_all(o_buf, 2 * clus - 1, o_send)


def fast_local(key_cache, value_cache, prompt_queries, tile_cluster, listed_clusters):
    clus = lax.axis_size("clus")
    _, rows, width = key_cache.shape
    tiles = rows // TILE
    query_count = prompt_queries.shape[0]
    heads = prompt_queries.shape[1] // (GROUP * DH)
    blocks = query_count // QBLK
    dma = pltpu.SemaphoreType.DMA
    f32, bf16 = jnp.float32, jnp.bfloat16
    share = query_count * GROUP // clus
    vmem = pl.BlockSpec(memory_space=pltpu.VMEM)
    smem = pl.BlockSpec(memory_space=pltpu.SMEM)
    hbm = pl.BlockSpec(memory_space=pltpu.HBM)
    out = pl.pallas_call(
        fast_kernel,
        out_shape=jax.ShapeDtypeStruct((heads, share, DH), bf16),
        in_specs=[hbm, hbm, vmem, smem, smem],
        out_specs=vmem,
        scratch_shapes=[
            pltpu.VMEM((2, 2, 2 * rows, DH), bf16),
            pltpu.VMEM((2, 2, 2 * rows, DH), bf16),
            pltpu.VMEM((2, 2, rows, DH), bf16),
            pltpu.VMEM((2, 2, rows, DH), bf16),
            pltpu.VMEM((query_count, 2 * GROUP * DH), bf16),
            pltpu.VMEM((2, 2, query_count * GROUP, DH), bf16),
            pltpu.VMEM((2, 2, 2 * blocks, 128), f32),
            pltpu.VMEM((3, 2 * blocks, 128), f32),
            pltpu.VMEM((2, 2 * blocks, 128), f32),
            pltpu.VMEM((2 * clus, 2 * share + 16, DH), bf16),
            pltpu.VMEM((2, clus, 2 * share + 16, DH), bf16),
            pltpu.VMEM((2, 2, heads, tiles, DH), f32),
            pltpu.VMEM((2, heads, tiles, DH), f32),
            pltpu.VMEM((clus, 8, DH), f32),
            pltpu.VMEM((clus, 8, DH), f32),
            pltpu.VMEM((8, DH), f32),
            pltpu.VMEM((clus, 8, DH), f32),
            pltpu.VMEM((8, 128, 128), f32),
            pltpu.VMEM((2 * rows, 128), bf16),
            dma((2, 8)), dma((8,)), dma((8,)), dma((4,)), dma((4,)),
            dma, dma, dma((2,)), dma, dma, dma, dma,
        ],
        compiler_params=pltpu.CompilerParams(
            collective_id=0, has_side_effects=True, vmem_limit_bytes=56 * 1024 * 1024),
    )(
        key_cache.reshape(rows, width), value_cache.reshape(rows, width),
        prompt_queries, tile_cluster.reshape(2 * heads, tiles), listed_clusters,
    )
    out = out.reshape(heads, query_count // clus, GROUP, DH).transpose(1, 0, 2, 3)
    return out.reshape(query_count // clus, heads * GROUP * DH)


def solution(mesh):
    placed = (
        P("head", "clus", None),
        P("head", "clus", None),
        P(None, "head"),
        P("head", "clus", None, None, None),
        P("head", None, None),
    )
    fits = mesh.shape["head"] == 2 and mesh.shape["clus"] == 16
    return jax.shard_map(
        fast_local if fits else local,
        mesh=mesh,
        in_specs=placed,
        out_specs=P("clus", "head"),
        check_vma=False,
    )
```

```python
import functools
import math

import jax
import jax.numpy as jnp
from jax import lax
from jax.experimental import pallas as pl
from jax.experimental.pallas import tpu as pltpu
from jax.sharding import PartitionSpec as P

DH = 128
GROUP = 8
TILE = 128
QBLK = 16


floor_value = -1e30
highest = lax.Precision.HIGHEST


def combined_all(shard, axis, combine):
    everything = jax.tree.map(lambda part: lax.all_gather(part, axis), shard)
    leading = jax.tree.map(lambda part: part[0], everything)

    def turn(k, so_far):
        return combine(so_far, jax.tree.map(lambda part: part[k], everything))

    return lax.fori_loop(1, lax.axis_size(axis), turn, leading)


def block_partials(
    query_blocks, key_rows, value_rows, tile_mask, key_mean, value_sum, counts_mine, approx_on
):
    score_scale = key_rows.shape[-1] ** (-0.5)
    tile_rows = key_rows.shape[0] // tile_mask.shape[-1]

    def one_block(block_inputs):
        block_queries, mask_tiles, approx_flag = block_inputs
        key_mask = jnp.repeat(mask_tiles, tile_rows) > 0.5
        scores = (
            jnp.einsum("rd,kd->rk", block_queries, key_rows, preferred_element_type=jnp.float32)
            * score_scale
        )
        approx_score = (
            jnp.dot(block_queries.astype(jnp.float32), key_mean, precision=highest) * score_scale
        )
        approx_live = approx_flag > 0.5
        row_top = jnp.maximum(
            jnp.max(jnp.where(key_mask[None, :], scores, floor_value), axis=1),
            jnp.where(approx_live, approx_score, floor_value),
        )
        weights = jnp.where(key_mask[None, :], jnp.exp(scores - row_top[:, None]), 0.0)
        probabilities = weights.astype(jnp.bfloat16)
        approx_weight = jnp.where(approx_live, jnp.exp(approx_score - row_top), 0.0)
        row_total = jnp.sum(weights, axis=1) + counts_mine * approx_weight
        numerator = jnp.dot(probabilities, value_rows, preferred_element_type=jnp.float32)
        numerator = numerator + approx_weight[:, None] * value_sum[None, :]
        return (row_top, row_total, numerator)

    return lax.map(one_block, (query_blocks, tile_mask, approx_on))


def combine_parts(first_part, second_part):
    top_first, total_first, numer_first = first_part
    top_second, total_second, numer_second = second_part
    joined = jnp.maximum(top_first, top_second)
    factor_first = jnp.exp(top_first - joined)
    factor_second = jnp.exp(top_second - joined)
    return (
        joined,
        total_first * factor_first + total_second * factor_second,
        numer_first * factor_first[..., None] + numer_second * factor_second[..., None],
    )


def local(key_cache, value_cache, prompt_queries, tile_cluster, listed_clusters):
    owners = lax.axis_size("clus")
    owner_index = lax.axis_index("clus")
    moved_keys, moved_values = (
        lax.all_to_all(key_cache, "head", split_axis=2, concat_axis=0, tiled=True),
        lax.all_to_all(value_cache, "head", split_axis=2, concat_axis=0, tiled=True),
    )
    slab_count, slab_rows, feature_width = moved_keys.shape
    heads_dev = feature_width // DH
    tiles_dev = slab_count * slab_rows // TILE

    def to_tiles(moved):
        shaped = moved.reshape(slab_count, slab_rows // TILE, TILE, heads_dev, DH)
        return shaped.transpose(3, 0, 1, 2, 4).reshape(heads_dev, tiles_dev, TILE, DH)

    key_tiles = to_tiles(moved_keys)
    value_tiles = to_tiles(moved_values)
    cluster_ids = tile_cluster.reshape(heads_dev, tiles_dev)
    column_ids = jnp.arange(owners, dtype=jnp.int32)
    member = (cluster_ids[:, :, None] == column_ids[None, None, :]).astype(jnp.float32)
    listed_mask = jnp.max(
        (listed_clusters[:, :, :, None] == column_ids).astype(jnp.float32), axis=2
    )
    owner_hot = (column_ids == owner_index).astype(jnp.float32)
    mine_listed = jnp.einsum("hbc,c->hb", listed_mask, owner_hot, precision=highest)
    query_count = prompt_queries.shape[0]
    block_count = query_count // QBLK
    query_blocks = prompt_queries.reshape(query_count, heads_dev, GROUP, DH).transpose(1, 0, 2, 3)
    query_blocks = query_blocks.reshape(heads_dev, block_count, QBLK * GROUP, DH)
    key_rows = key_tiles.reshape(heads_dev, tiles_dev * TILE, DH)
    value_rows = value_tiles.reshape(heads_dev, tiles_dev * TILE, DH)
    unit_rows = jnp.ones((TILE,), jnp.bfloat16)
    tile_keys = jnp.einsum("htrd,r->htd", key_tiles, unit_rows, preferred_element_type=jnp.float32)
    tile_values = jnp.einsum(
        "htrd,r->htd", value_tiles, unit_rows, preferred_element_type=jnp.float32
    )
    local_keys = jnp.einsum("htc,htd->hcd", member, tile_keys, precision=highest)
    local_values = jnp.einsum("htc,htd->hcd", member, tile_values, precision=highest)
    local_counts = TILE * jnp.sum(member, axis=1)
    total_keys, total_values, total_counts = lax.psum(
        (local_keys, local_values, local_counts), "clus"
    )
    key_sum = jnp.einsum("hcd,c->hd", total_keys, owner_hot, precision=highest)
    value_sum = jnp.einsum("hcd,c->hd", total_values, owner_hot, precision=highest)
    counts_mine = jnp.einsum("hc,c->h", total_counts, owner_hot, precision=highest)
    tile_mask = jnp.einsum("hbc,htc->hbt", listed_mask, member, precision=highest)
    key_mean = key_sum / jnp.maximum(counts_mine, 1.0)[:, None]
    approx_on = (1.0 - mine_listed) * (counts_mine > 0.5).astype(jnp.float32)[:, None]
    row_top, row_total, numerator = jax.vmap(block_partials)(
        query_blocks, key_rows, value_rows, tile_mask, key_mean, value_sum, counts_mine, approx_on
    )
    row_top = row_top.reshape(heads_dev, query_count, GROUP)
    row_total = row_total.reshape(heads_dev, query_count, GROUP)
    numerator = numerator.reshape(heads_dev, query_count, GROUP, DH)
    share_rows = query_count // owners
    merged_top, merged_total, merged_numer = combined_all(
        (row_top, row_total, numerator), "clus", combine_parts
    )
    kept_total = lax.dynamic_slice_in_dim(merged_total, owner_index * share_rows, share_rows, 1)
    kept_numer = lax.dynamic_slice_in_dim(merged_numer, owner_index * share_rows, share_rows, 1)
    attended = kept_numer / kept_total[..., None]
    return (
        attended.transpose(1, 0, 2, 3)
        .reshape(share_rows, heads_dev * GROUP * DH)
        .astype(jnp.bfloat16)
    )


MESH = pl.DeviceIdType.MESH
dead = -1e30
lowest_top = -1e9
log2_scale = math.log2(math.e) * DH**-0.5
nt = (((1,), (1,)), ((), ()))


def fast_kernel(
    k_hbm, v_hbm, q_ref, ids_ref, listed_ref, out_ref,
    kbuf, vbuf, kout, vout, qall, bt, btx, bias, o_buf, o_rx,
    ts_buf, ts_rx, cs_buf, cs_rx, red_buf, tot_rx, wt, hot_ref,
    loc_sem, kv_send, kv_recv, in_send, in_recv,
    o_send, o_recv, ts_sem, cs_send, cs_recv, tot_send, tot_recv,
):
    x, i = lax.axis_index("head"), lax.axis_index("clus")
    clus = lax.axis_size("clus")
    chips = clus // 2
    c, w = lax.rem(i, 2), i // 2
    sib = i + 1 - 2 * c
    slot = x * chips + w
    rows = k_hbm.shape[0]
    tiles = rows // TILE
    count = float(clus * TILE)
    wide = GROUP * DH
    span = 2 * QBLK * GROUP
    far = jnp.where(i < chips, 1, 0)
    listing = listed_ref.shape[2]

    def pair_of(half, core):
        return 2 * (x if half == 0 else 1 - x) + core

    def kv_copies(half, kind):
        copies = []
        for hh in range(2):
            for n, (src, dst, out) in enumerate(((k_hbm, kbuf, kout), (v_hbm, vbuf, vout))):
                number = half * 4 + hh * 2 + n
                pair = pair_of(half, c if kind == 0 else 1 - c)
                column = pl.ds(pl.multiple_of((pair * 2 + hh) * DH, DH), DH)
                if kind == 0:
                    copies.append(pltpu.make_async_copy(
                        src.at[:, column], dst.at[half, hh, pl.ds(0, rows)], loc_sem.at[0, number]))
                elif kind == 1:
                    copies.append(pltpu.make_async_copy(
                        src.at[:, column], out.at[half, hh], loc_sem.at[1, number]))
                else:
                    copies.append(pltpu.make_async_remote_copy(
                        src_ref=src.at[:, column], dst_ref=dst.at[half, hh, pl.ds(rows, rows)],
                        send_sem=kv_send.at[number], recv_sem=kv_recv.at[number],
                        device_id=(x, sib), device_id_type=MESH))
        return copies

    def remote(src, dst, send_sem, recv_sem, device):
        return pltpu.make_async_remote_copy(
            src_ref=src, dst_ref=dst, send_sem=send_sem, recv_sem=recv_sem,
            device_id=device, device_id_type=MESH)

    own_kv = [kv_copies(0, 0), kv_copies(1, 0)]
    out_kv = [kv_copies(0, 1), kv_copies(1, 1)]
    far_kv = [kv_copies(0, 2), kv_copies(1, 2)]
    for copy in own_kv[0] + own_kv[1] + out_kv[0] + out_kv[1]:
        copy.start()

    barrier = pltpu.get_barrier_semaphore()

    def ahead(k):
        return jnp.where(i + k >= clus, i + k - clus, i + k)

    def greet(side, k):
        pl.semaphore_signal(barrier, inc=1, device_id=(side, ahead(k)), device_id_type=MESH)

    for k in range(clus):
        greet(1 - x, k)
        if k > 0:
            greet(x, k)

    lane8 = lax.broadcasted_iota(jnp.int32, (8, 128), 1)
    sub8 = lax.broadcasted_iota(jnp.int32, (8, 128), 0)
    for turn in range(2):
        pair = c if turn == 0 else 1 - c
        named = []
        for l in range(listing):
            table = jnp.zeros((8, 128), jnp.int32)
            for hh in range(2):
                for b in range(4):
                    table = jnp.where(sub8 == hh * 4 + b, listed_ref[2 * pair + hh, b, l], table)
            named.append(table)
        first = turn * tiles
        for side in range(2):
            slab = x if side == 0 else 1 - x
            held = jnp.full((8, 128), -1, jnp.int32)
            for hh in range(2):
                for t in range(tiles):
                    here = (lane8 == first + t) & (sub8 // 4 == hh)
                    held = jnp.where(here, ids_ref[2 * (2 * pair + hh) + slab, t], held)
            live = (lane8 < first) | (lane8 >= first + tiles)
            for table in named:
                live = live | (held == table)
            bt[side, turn] = jnp.where(live, 0.0, dead)

    key_tile = lax.broadcasted_iota(jnp.int32, (2 * rows, 128), 0) // TILE
    hot = key_tile == lax.broadcasted_iota(jnp.int32, (2 * rows, 128), 1)
    hot_ref[...] = jnp.where(hot, 1.0, 0.0).astype(jnp.bfloat16)

    def regroup(rows_in):
        count_in = rows_in.shape[0]
        split = rows_in.astype(jnp.float32).reshape(count_in, GROUP, DH)
        return split.reshape(count_in * GROUP, DH).astype(jnp.bfloat16)

    def place_queries(first):
        def block_of(n, carry):
            hh, block = n // 4, lax.rem(n, 4)
            for head in range(2):
                @pl.when(hh == head)
                def _():
                    columns = pl.ds(pl.multiple_of(first + head * wide, 128), wide)
                    taken = q_ref[pl.ds(pl.multiple_of(block * QBLK, QBLK), QBLK), columns]
                    qall[0, head, pl.ds(pl.multiple_of(block * 128, 128), 128), :] = regroup(
                        taken)
            return carry

        lax.fori_loop(0, 8, block_of, 0)

    place_queries(c * 2 * wide)
    pl.semaphore_wait(barrier, 2 * clus - 1)

    small = [
        remote(bt.at[0, 1], btx.at[0], in_send.at[0], in_recv.at[0], (x, sib)),
        remote(bt.at[1, 0], btx.at[1], in_send.at[1], in_recv.at[1], (1 - x, i)),
        remote(bt.at[1, 1], btx.at[2], in_send.at[2], in_recv.at[2], (1 - x, sib)),
        remote(qall.at[0], qall.at[1], in_send.at[3], in_recv.at[3], (1 - x, i)),
    ]
    for copy in small[:1] + small[3:] + far_kv[0] + small[1:3] + far_kv[1]:
        copy.start()

    ts_copy = remote(ts_buf.at[1], ts_rx, ts_sem.at[0], ts_sem.at[1], (1 - x, i))

    def tile_sums():
        for copy in own_kv[0] + own_kv[1] + out_kv[0] + out_kv[1]:
            copy.wait()

        def add_up(n, carry):
            half, hh = n // 2, lax.rem(n, 2)
            for m, (buf, out) in enumerate(((kbuf, kout), (vbuf, vout))):
                for part, core in ((buf[half, hh, :rows], c), (out[half, hh], 1 - c)):
                    ts_buf[half, m, 2 * core + hh] = jnp.sum(
                        part.astype(jnp.float32).reshape(tiles, TILE, DH), axis=1)
            return carry

        lax.fori_loop(0, 4, add_up, 0)
        ts_copy.start()

    square = lax.broadcasted_iota(jnp.int32, (128, 128), 0) == lax.broadcasted_iota(
        jnp.int32, (128, 128), 1)

    def as_row(column):
        return jnp.sum(jnp.where(square, column, 0.0), axis=0, keepdims=True)

    sub16 = lax.broadcasted_iota(jnp.int32, (16, 128), 0)

    def attend(half, pair, hh, stats):
        start = pl.multiple_of(pair * span, span)
        masks = [
            jnp.broadcast_to(bias[half, pl.ds(hh * 4 + pair * 2 + n, 1), :], (128, 128))
            for n in range(2)
        ]
        masks = jnp.concatenate(masks, axis=0).astype(jnp.bfloat16)
        queries = jnp.concatenate([qall[half, hh, pl.ds(start, span), :], masks], axis=1)
        keys = jnp.concatenate([kbuf[half, hh], hot_ref[...]], axis=1)
        scores = lax.dot_general(queries, keys, nt, preferred_element_type=jnp.float32)
        top = jnp.maximum(jnp.max(scores, axis=1, keepdims=True), lowest_top) * log2_scale
        top = top.astype(jnp.bfloat16).astype(jnp.float32)
        weights = jnp.exp2(scores * log2_scale - top).astype(jnp.bfloat16)
        values = jnp.concatenate(
            [vbuf[half, hh], jnp.ones((2 * rows, 128), jnp.bfloat16)], axis=1)
        numer = jnp.dot(weights, values, preferred_element_type=jnp.float32)
        after = []
        for n in range(2):
            part = slice(128 * n, 128 * (n + 1))
            total = as_row(numer[part, DH:])
            upper = total.astype(jnp.bfloat16).astype(jnp.float32)
            held = stats[n]
            for r, row in enumerate((as_row(top[part]), upper, total - upper)):
                held = jnp.where(sub16 == hh * 3 + r, row, held)
            after.append(held)
            for j in range(4):
                first = 128 * n + 32 * j
                place = pl.ds(hh * 32, 32)
                o_buf[half * clus + pair * 8 + n * 4 + j, place, :] = numer[
                    first : first + 32, :DH].astype(jnp.bfloat16)
        return tuple(after)

    def ship(half, dest):
        src = o_buf.at[half * clus + dest]
        here = (half == 0) & (dest == i)

        @pl.when(jnp.logical_not(here))
        def _():
            remote(src, o_rx.at[c, slot], o_send, o_recv, (x + half * (1 - 2 * x), dest)).start()

        @pl.when(here)
        def _():
            pltpu.make_async_copy(src, o_rx.at[c, slot], o_recv).start()

    def first_half():
        small[0].wait_recv()
        for copy in far_kv[0]:
            copy.wait_recv()
        bias[0] = bt[0, 0] + btx[0]

    def second_half():
        for copy in small[1:]:
            copy.wait_recv()
        for copy in far_kv[1]:
            copy.wait_recv()
        bias[1] = btx[1] + btx[2]

    line = lax.broadcasted_iota(jnp.int32, (128, 128), 0)

    def cluster_sums():
        lane = lax.rem(lane8, 8 * tiles)
        held = jnp.zeros((8, 128), jnp.int32)
        for h in range(4):
            for side in range(2):
                slab = x if side == 0 else 1 - x
                for t in range(tiles):
                    held = jnp.where(
                        lane == (h * 2 + side) * tiles + t, ids_ref[2 * h + slab, t], held)
        held = jnp.concatenate([held] * 16, axis=0)
        column = lax.broadcasted_iota(jnp.int32, (128, 128), 1)
        belongs = (held == line // 8) & (lax.rem(line, 8) == column // (2 * tiles))
        ts_copy.wait_recv()
        all_sums = jnp.concatenate(
            [ts_buf[0].reshape(8, tiles, DH), ts_rx[...].reshape(8, tiles, DH)], axis=1
        ).reshape(16 * tiles, DH)
        clustered = jnp.dot(
            jnp.where(belongs, 1.0, 0.0), all_sums, precision=highest,
            preferred_element_type=jnp.float32)
        cs_buf[...] = clustered.reshape(clus, 8, DH)
        cs_rx[i] = cs_buf[i]
        lax.fori_loop(1, clus, start_cs, 0)

    def cs_copy(k):
        other = lax.rem(i + k, clus)
        return remote(cs_buf.at[other], cs_rx.at[i], cs_send, cs_recv, (x, other))

    def start_cs(k, carry):
        cs_copy(k).start()
        return carry

    def tot_copy(k):
        return remote(red_buf, tot_rx.at[i], tot_send, tot_recv, (x, lax.rem(i + k, clus)))

    def start_tot(k, carry):
        tot_copy(k).start()
        return carry

    def take_all(buf, amount, sem):
        part = buf.at[pl.ds(0, amount)]
        pltpu.make_async_copy(part, part, sem).wait()

    def reduce_sums():
        take_all(cs_rx, clus - 1, cs_recv)
        reduced = jnp.sum(cs_rx[...], axis=0)
        red_buf[...] = reduced
        tot_rx[i] = reduced
        lax.fori_loop(1, clus, start_tot, 0)

    hooks = ((0, first_half), (2, second_half))
    late_hooks = ((0, cluster_sums), (1, reduce_sums))
    tile_sums()

    def step(n, carry):
        half, pair = n // 2, lax.rem(n + far, 2)
        for number, work in hooks:
            pl.when(n == number)(work)

        blank = jnp.zeros((16, 128), jnp.float32)
        stats = (blank, blank)
        for hh in range(2):
            stats = attend(half, pair, hh, stats)
        for m in range(2):
            packed = stats[m].astype(jnp.bfloat16)
            for j in range(4):
                o_buf[half * clus + pair * 8 + m * 4 + j, 64:80, :] = packed

        for number, work in late_hooks:
            pl.when(n == number)(work)

        def one_dest(k, inner):
            ship(half, pair * 8 + lax.rem(k + i, 8))
            return inner

        lax.fori_loop(0, 8, one_dest, 0)
        return carry

    lax.fori_loop(0, 4, step, 0)
    take_all(tot_rx, clus - 1, tot_recv)
    block, part = i // 4, lax.rem(i, 4)
    share = pl.ds(pl.multiple_of(part * 32, 32), 32)
    totals = tot_rx[...].reshape(clus * 8, DH)
    approx_parts = []
    for h in range(4):
        taken = q_ref[pl.ds(pl.multiple_of(block * QBLK, QBLK), QBLK), h * wide : (h + 1) * wide]
        queries = regroup(taken).astype(jnp.float32)
        approx = lax.dot_general(
            totals, queries, nt, precision=highest, preferred_element_type=jnp.float32)
        usable = lax.rem(line, 8) == h
        for l in range(listing):
            usable = usable & (line // 8 != listed_ref[h, block, l])
        approx = jnp.where(usable, approx * (log2_scale / count), dead)
        top = jnp.max(approx, axis=0, keepdims=True)
        approx_weight = jnp.where(usable, jnp.exp2(approx - top), 0.0)
        total = count * jnp.sum(approx_weight, axis=0, keepdims=True)
        wt[h] = pltpu.roll(approx_weight, 4, 0).T
        numer = jnp.dot(
            wt[h, share, :], totals, precision=highest, preferred_element_type=jnp.float32)
        approx_parts.append((top, total, numer))

    take_all(o_rx, 2, o_recv)
    for h in range(4):
        p, hh = h // 2, h % 2
        held = o_rx[p, :, 64:80, :].astype(jnp.float32)
        tops, sums = held[:, 3 * hh, :], held[:, 3 * hh + 1, :] + held[:, 3 * hh + 2, :]
        approx_top, approx_total, _ = approx_parts[h]
        top = jnp.maximum(jnp.max(tops, axis=0, keepdims=True), approx_top)
        factor = jnp.exp2(tops - top)
        approx_factor = jnp.exp2(approx_top - top)
        total = jnp.sum(factor * sums, axis=0, keepdims=True) + approx_factor * approx_total
        inverse = 1.0 / total
        mixed = jnp.concatenate(
            [factor * inverse, jnp.broadcast_to(approx_factor * inverse, (8, 128)),
             jnp.zeros((104, 128), jnp.float32)], axis=0)
        wt[4 + h] = mixed.T
    for h in range(4):
        p, hh = h // 2, h % 2
        mine = wt[4 + h, share, :]
        numer = mine[:, 2 * chips : 2 * chips + 1] * approx_parts[h][2]
        for source in range(2 * chips):
            numer = numer + mine[:, source : source + 1] * o_rx[p, source, 32 * hh : 32 * (hh + 1), :].astype(jnp.float32)
        out_ref[h] = numer.astype(jnp.bfloat16)

    for copy in small + far_kv[0] + far_kv[1] + [ts_copy]:
        copy.wait_send()

    take_all(cs_buf, clus - 1, cs_send)
    take_all(tot_rx, clus - 1, tot_send)
    take_all(o_buf, 2 * clus - 1, o_send)


def fast_local(key_cache, value_cache, prompt_queries, tile_cluster, listed_clusters):
    clus = lax.axis_size("clus")
    _, rows, width = key_cache.shape
    tiles = rows // TILE
    query_count = prompt_queries.shape[0]
    heads = prompt_queries.shape[1] // (GROUP * DH)
    blocks = query_count // QBLK
    dma = pltpu.SemaphoreType.DMA
    f32, bf16 = jnp.float32, jnp.bfloat16
    share = query_count * GROUP // clus
    vmem = pl.BlockSpec(memory_space=pltpu.VMEM)
    smem = pl.BlockSpec(memory_space=pltpu.SMEM)
    hbm = pl.BlockSpec(memory_space=pltpu.HBM)
    out = pl.pallas_call(
        fast_kernel,
        out_shape=jax.ShapeDtypeStruct((heads, share, DH), bf16),
        in_specs=[hbm, hbm, vmem, smem, smem],
        out_specs=vmem,
        scratch_shapes=[
            pltpu.VMEM((2, 2, 2 * rows, DH), bf16),
            pltpu.VMEM((2, 2, 2 * rows, DH), bf16),
            pltpu.VMEM((2, 2, rows, DH), bf16),
            pltpu.VMEM((2, 2, rows, DH), bf16),
            pltpu.VMEM((2, 2, query_count * GROUP, DH), bf16),
            pltpu.VMEM((2, 2, 2 * blocks, 128), f32),
            pltpu.VMEM((3, 2 * blocks, 128), f32),
            pltpu.VMEM((2, 2 * blocks, 128), f32),
            pltpu.VMEM((2 * clus, 2 * share + 16, DH), bf16),
            pltpu.VMEM((2, clus, 2 * share + 16, DH), bf16),
            pltpu.VMEM((2, 2, heads, tiles, DH), f32),
            pltpu.VMEM((2, heads, tiles, DH), f32),
            pltpu.VMEM((clus, 8, DH), f32),
            pltpu.VMEM((clus, 8, DH), f32),
            pltpu.VMEM((8, DH), f32),
            pltpu.VMEM((clus, 8, DH), f32),
            pltpu.VMEM((8, 128, 128), f32),
            pltpu.VMEM((2 * rows, 128), bf16),
            dma((2, 8)), dma((8,)), dma((8,)), dma((4,)), dma((4,)),
            dma, dma, dma((2,)), dma, dma, dma, dma,
        ],
        compiler_params=pltpu.CompilerParams(
            collective_id=0, has_side_effects=True, vmem_limit_bytes=56 * 1024 * 1024),
    )(
        key_cache.reshape(rows, width), value_cache.reshape(rows, width),
        prompt_queries, tile_cluster.reshape(2 * heads, tiles), listed_clusters,
    )
    out = out.reshape(heads, query_count // clus, GROUP, DH).transpose(1, 0, 2, 3)
    return out.reshape(query_count // clus, heads * GROUP * DH)


def solution(mesh):
    placed = (
        P("head", "clus", None),
        P("head", "clus", None),
        P(None, "head"),
        P("head", "clus", None, None, None),
        P("head", None, None),
    )
    fits = mesh.shape["head"] == 2 and mesh.shape["clus"] == 16
    return jax.shard_map(
        fast_local if fits else local,
        mesh=mesh,
        in_specs=placed,
        out_specs=P("clus", "head"),
        check_vma=False,
    )
```

```python
import functools
import math

import jax
import jax.numpy as jnp
from jax import lax
from jax.experimental import pallas as pl
from jax.experimental.pallas import tpu as pltpu
from jax.sharding import PartitionSpec as P

DH = 128
GROUP = 8
TILE = 128
QBLK = 16


floor_value = -1e30
highest = lax.Precision.HIGHEST


def combined_all(shard, axis, combine):
    everything = jax.tree.map(lambda part: lax.all_gather(part, axis), shard)
    leading = jax.tree.map(lambda part: part[0], everything)

    def turn(k, so_far):
        return combine(so_far, jax.tree.map(lambda part: part[k], everything))

    return lax.fori_loop(1, lax.axis_size(axis), turn, leading)


def block_partials(
    query_blocks, key_rows, value_rows, tile_mask, key_mean, value_sum, counts_mine, approx_on
):
    score_scale = key_rows.shape[-1] ** (-0.5)
    tile_rows = key_rows.shape[0] // tile_mask.shape[-1]

    def one_block(block_inputs):
        block_queries, mask_tiles, approx_flag = block_inputs
        key_mask = jnp.repeat(mask_tiles, tile_rows) > 0.5
        scores = (
            jnp.einsum("rd,kd->rk", block_queries, key_rows, preferred_element_type=jnp.float32)
            * score_scale
        )
        approx_score = (
            jnp.dot(block_queries.astype(jnp.float32), key_mean, precision=highest) * score_scale
        )
        approx_live = approx_flag > 0.5
        row_top = jnp.maximum(
            jnp.max(jnp.where(key_mask[None, :], scores, floor_value), axis=1),
            jnp.where(approx_live, approx_score, floor_value),
        )
        weights = jnp.where(key_mask[None, :], jnp.exp(scores - row_top[:, None]), 0.0)
        probabilities = weights.astype(jnp.bfloat16)
        approx_weight = jnp.where(approx_live, jnp.exp(approx_score - row_top), 0.0)
        row_total = jnp.sum(weights, axis=1) + counts_mine * approx_weight
        numerator = jnp.dot(probabilities, value_rows, preferred_element_type=jnp.float32)
        numerator = numerator + approx_weight[:, None] * value_sum[None, :]
        return (row_top, row_total, numerator)

    return lax.map(one_block, (query_blocks, tile_mask, approx_on))


def combine_parts(first_part, second_part):
    top_first, total_first, numer_first = first_part
    top_second, total_second, numer_second = second_part
    joined = jnp.maximum(top_first, top_second)
    factor_first = jnp.exp(top_first - joined)
    factor_second = jnp.exp(top_second - joined)
    return (
        joined,
        total_first * factor_first + total_second * factor_second,
        numer_first * factor_first[..., None] + numer_second * factor_second[..., None],
    )


def local(key_cache, value_cache, prompt_queries, tile_cluster, listed_clusters):
    owners = lax.axis_size("clus")
    owner_index = lax.axis_index("clus")
    moved_keys, moved_values = (
        lax.all_to_all(key_cache, "head", split_axis=2, concat_axis=0, tiled=True),
        lax.all_to_all(value_cache, "head", split_axis=2, concat_axis=0, tiled=True),
    )
    slab_count, slab_rows, feature_width = moved_keys.shape
    heads_dev = feature_width // DH
    tiles_dev = slab_count * slab_rows // TILE

    def to_tiles(moved):
        shaped = moved.reshape(slab_count, slab_rows // TILE, TILE, heads_dev, DH)
        return shaped.transpose(3, 0, 1, 2, 4).reshape(heads_dev, tiles_dev, TILE, DH)

    key_tiles = to_tiles(moved_keys)
    value_tiles = to_tiles(moved_values)
    cluster_ids = tile_cluster.reshape(heads_dev, tiles_dev)
    column_ids = jnp.arange(owners, dtype=jnp.int32)
    member = (cluster_ids[:, :, None] == column_ids[None, None, :]).astype(jnp.float32)
    listed_mask = jnp.max(
        (listed_clusters[:, :, :, None] == column_ids).astype(jnp.float32), axis=2
    )
    owner_hot = (column_ids == owner_index).astype(jnp.float32)
    mine_listed = jnp.einsum("hbc,c->hb", listed_mask, owner_hot, precision=highest)
    query_count = prompt_queries.shape[0]
    block_count = query_count // QBLK
    query_blocks = prompt_queries.reshape(query_count, heads_dev, GROUP, DH).transpose(1, 0, 2, 3)
    query_blocks = query_blocks.reshape(heads_dev, block_count, QBLK * GROUP, DH)
    key_rows = key_tiles.reshape(heads_dev, tiles_dev * TILE, DH)
    value_rows = value_tiles.reshape(heads_dev, tiles_dev * TILE, DH)
    unit_rows = jnp.ones((TILE,), jnp.bfloat16)
    tile_keys = jnp.einsum("htrd,r->htd", key_tiles, unit_rows, preferred_element_type=jnp.float32)
    tile_values = jnp.einsum(
        "htrd,r->htd", value_tiles, unit_rows, preferred_element_type=jnp.float32
    )
    local_keys = jnp.einsum("htc,htd->hcd", member, tile_keys, precision=highest)
    local_values = jnp.einsum("htc,htd->hcd", member, tile_values, precision=highest)
    local_counts = TILE * jnp.sum(member, axis=1)
    total_keys, total_values, total_counts = lax.psum(
        (local_keys, local_values, local_counts), "clus"
    )
    key_sum = jnp.einsum("hcd,c->hd", total_keys, owner_hot, precision=highest)
    value_sum = jnp.einsum("hcd,c->hd", total_values, owner_hot, precision=highest)
    counts_mine = jnp.einsum("hc,c->h", total_counts, owner_hot, precision=highest)
    tile_mask = jnp.einsum("hbc,htc->hbt", listed_mask, member, precision=highest)
    key_mean = key_sum / jnp.maximum(counts_mine, 1.0)[:, None]
    approx_on = (1.0 - mine_listed) * (counts_mine > 0.5).astype(jnp.float32)[:, None]
    row_top, row_total, numerator = jax.vmap(block_partials)(
        query_blocks, key_rows, value_rows, tile_mask, key_mean, value_sum, counts_mine, approx_on
    )
    row_top = row_top.reshape(heads_dev, query_count, GROUP)
    row_total = row_total.reshape(heads_dev, query_count, GROUP)
    numerator = numerator.reshape(heads_dev, query_count, GROUP, DH)
    share_rows = query_count // owners
    merged_top, merged_total, merged_numer = combined_all(
        (row_top, row_total, numerator), "clus", combine_parts
    )
    kept_total = lax.dynamic_slice_in_dim(merged_total, owner_index * share_rows, share_rows, 1)
    kept_numer = lax.dynamic_slice_in_dim(merged_numer, owner_index * share_rows, share_rows, 1)
    attended = kept_numer / kept_total[..., None]
    return (
        attended.transpose(1, 0, 2, 3)
        .reshape(share_rows, heads_dev * GROUP * DH)
        .astype(jnp.bfloat16)
    )


MESH = pl.DeviceIdType.MESH
dead = -1e30
lowest_top = -1e9
log2_scale = math.log2(math.e) * DH**-0.5
nt = (((1,), (1,)), ((), ()))


def fast_kernel(
    k_hbm, v_hbm, q_ref, ids_ref, listed_ref, out_ref,
    kbuf, vbuf, kout, vout, qall, bt, btx, bias, o_buf, o_rx,
    ts_buf, ts_rx, cs_buf, cs_rx, red_buf, tot_rx, wt, hot_ref,
    loc_sem, kv_send, kv_recv, in_send, in_recv,
    o_send, o_recv, ts_sem, cs_send, cs_recv, tot_send, tot_recv,
):
    x, i = lax.axis_index("head"), lax.axis_index("clus")
    clus = lax.axis_size("clus")
    chips = clus // 2
    c, w = lax.rem(i, 2), i // 2
    sib = i + 1 - 2 * c
    slot = x * chips + w
    rows = k_hbm.shape[0]
    tiles = rows // TILE
    count = float(clus * TILE)
    wide = GROUP * DH
    span = 2 * QBLK * GROUP
    far = jnp.where(i < chips, 1, 0)
    listing = listed_ref.shape[2]

    def pair_of(half, core):
        return 2 * (x if half == 0 else 1 - x) + core

    def kv_copies(half, kind):
        copies = []
        for hh in range(2):
            for n, (src, dst, out) in enumerate(((k_hbm, kbuf, kout), (v_hbm, vbuf, vout))):
                number = half * 4 + hh * 2 + n
                pair = pair_of(half, c if kind == 0 else 1 - c)
                column = pl.ds(pl.multiple_of((pair * 2 + hh) * DH, DH), DH)
                if kind == 0:
                    copies.append(pltpu.make_async_copy(
                        src.at[:, column], dst.at[half, hh, pl.ds(0, rows)], loc_sem.at[0, number]))
                elif kind == 1:
                    copies.append(pltpu.make_async_copy(
                        src.at[:, column], out.at[half, hh], loc_sem.at[1, number]))
                else:
                    copies.append(pltpu.make_async_remote_copy(
                        src_ref=src.at[:, column], dst_ref=dst.at[half, hh, pl.ds(rows, rows)],
                        send_sem=kv_send.at[number], recv_sem=kv_recv.at[number],
                        device_id=(x, sib), device_id_type=MESH))
        return copies

    def remote(src, dst, send_sem, recv_sem, device):
        return pltpu.make_async_remote_copy(
            src_ref=src, dst_ref=dst, send_sem=send_sem, recv_sem=recv_sem,
            device_id=device, device_id_type=MESH)

    own_kv = [kv_copies(0, 0), kv_copies(1, 0)]
    out_kv = [kv_copies(0, 1), kv_copies(1, 1)]
    far_kv = [kv_copies(0, 2), kv_copies(1, 2)]
    for copy in own_kv[0] + own_kv[1] + out_kv[0] + out_kv[1]:
        copy.start()

    barrier = pltpu.get_barrier_semaphore()

    def ahead(k):
        return jnp.where(i + k >= clus, i + k - clus, i + k)

    def greet(side, k):
        pl.semaphore_signal(barrier, inc=1, device_id=(side, ahead(k)), device_id_type=MESH)

    for k in range(clus):
        greet(1 - x, k)
        if k > 0:
            greet(x, k)

    lane8 = lax.broadcasted_iota(jnp.int32, (8, 128), 1)
    sub8 = lax.broadcasted_iota(jnp.int32, (8, 128), 0)
    for turn in range(2):
        pair = c if turn == 0 else 1 - c
        named = []
        for l in range(listing):
            table = jnp.zeros((8, 128), jnp.int32)
            for hh in range(2):
                for b in range(4):
                    table = jnp.where(sub8 == hh * 4 + b, listed_ref[2 * pair + hh, b, l], table)
            named.append(table)
        first = turn * tiles
        for side in range(2):
            slab = x if side == 0 else 1 - x
            held = jnp.full((8, 128), -1, jnp.int32)
            for hh in range(2):
                for t in range(tiles):
                    here = (lane8 == first + t) & (sub8 // 4 == hh)
                    held = jnp.where(here, ids_ref[2 * (2 * pair + hh) + slab, t], held)
            live = (lane8 < first) | (lane8 >= first + tiles)
            for table in named:
                live = live | (held == table)
            bt[side, turn] = jnp.where(live, 0.0, dead)

    pl.semaphore_wait(barrier, 2 * clus - 1)
    small = [
        remote(bt.at[0, 1], btx.at[0], in_send.at[0], in_recv.at[0], (x, sib)),
        remote(bt.at[1, 0], btx.at[1], in_send.at[1], in_recv.at[1], (1 - x, i)),
        remote(bt.at[1, 1], btx.at[2], in_send.at[2], in_recv.at[2], (1 - x, sib)),
        remote(qall.at[0], qall.at[1], in_send.at[3], in_recv.at[3], (1 - x, i)),
    ]
    for copy in far_kv[0] + small[:3] + far_kv[1]:
        copy.start()

    key_tile = lax.broadcasted_iota(jnp.int32, (2 * rows, 128), 0) // TILE
    hot = key_tile == lax.broadcasted_iota(jnp.int32, (2 * rows, 128), 1)
    hot_ref[...] = jnp.where(hot, 1.0, 0.0).astype(jnp.bfloat16)

    def regroup(rows_in):
        count_in = rows_in.shape[0]
        split = rows_in.astype(jnp.float32).reshape(count_in, GROUP, DH)
        return split.reshape(count_in * GROUP, DH).astype(jnp.bfloat16)

    def place_queries(first):
        def block_of(n, carry):
            hh, block = n // 4, lax.rem(n, 4)
            for head in range(2):
                @pl.when(hh == head)
                def _():
                    columns = pl.ds(pl.multiple_of(first + head * wide, 128), wide)
                    taken = q_ref[pl.ds(pl.multiple_of(block * QBLK, QBLK), QBLK), columns]
                    qall[0, head, pl.ds(pl.multiple_of(block * 128, 128), 128), :] = regroup(
                        taken)
            return carry

        lax.fori_loop(0, 8, block_of, 0)

    place_queries(c * 2 * wide)

    small[3].start()

    ts_copy = remote(ts_buf.at[1], ts_rx, ts_sem.at[0], ts_sem.at[1], (1 - x, i))

    def tile_sums():
        for copy in own_kv[1] + out_kv[0] + out_kv[1]:
            copy.wait()

        def add_up(n, carry):
            half, hh = n // 2, lax.rem(n, 2)
            for m, (buf, out) in enumerate(((kbuf, kout), (vbuf, vout))):
                for part, core in ((buf[half, hh, :rows], c), (out[half, hh], 1 - c)):
                    ts_buf[half, m, 2 * core + hh] = jnp.sum(
                        part.astype(jnp.float32).reshape(tiles, TILE, DH), axis=1)
            return carry

        lax.fori_loop(0, 4, add_up, 0)
        ts_copy.start()

    square = lax.broadcasted_iota(jnp.int32, (128, 128), 0) == lax.broadcasted_iota(
        jnp.int32, (128, 128), 1)

    def as_row(column):
        return jnp.sum(jnp.where(square, column, 0.0), axis=0, keepdims=True)

    sub16 = lax.broadcasted_iota(jnp.int32, (16, 128), 0)

    def attend(half, pair, hh, stats):
        start = pl.multiple_of(pair * span, span)
        masks = [
            jnp.broadcast_to(bias[half, pl.ds(hh * 4 + pair * 2 + n, 1), :], (128, 128))
            for n in range(2)
        ]
        masks = jnp.concatenate(masks, axis=0).astype(jnp.bfloat16)
        queries = jnp.concatenate([qall[half, hh, pl.ds(start, span), :], masks], axis=1)
        keys = jnp.concatenate([kbuf[half, hh], hot_ref[...]], axis=1)
        scores = lax.dot_general(queries, keys, nt, preferred_element_type=jnp.float32)
        top = jnp.maximum(jnp.max(scores, axis=1, keepdims=True), lowest_top) * log2_scale
        top = top.astype(jnp.bfloat16).astype(jnp.float32)
        weights = jnp.exp2(scores * log2_scale - top).astype(jnp.bfloat16)
        values = jnp.concatenate(
            [vbuf[half, hh], jnp.ones((2 * rows, 128), jnp.bfloat16)], axis=1)
        numer = jnp.dot(weights, values, preferred_element_type=jnp.float32)
        after = []
        for n in range(2):
            part = slice(128 * n, 128 * (n + 1))
            total = as_row(numer[part, DH:])
            upper = total.astype(jnp.bfloat16).astype(jnp.float32)
            held = stats[n]
            for r, row in enumerate((as_row(top[part]), upper, total - upper)):
                held = jnp.where(sub16 == hh * 3 + r, row, held)
            after.append(held)
            for j in range(4):
                first = 128 * n + 32 * j
                place = pl.ds(hh * 32, 32)
                o_buf[half * clus + pair * 8 + n * 4 + j, place, :] = numer[
                    first : first + 32, :DH].astype(jnp.bfloat16)
        return tuple(after)

    def ship(half, dest):
        src = o_buf.at[half * clus + dest]
        here = (half == 0) & (dest == i)

        @pl.when(jnp.logical_not(here))
        def _():
            remote(src, o_rx.at[c, slot], o_send, o_recv, (x + half * (1 - 2 * x), dest)).start()

        @pl.when(here)
        def _():
            pltpu.make_async_copy(src, o_rx.at[c, slot], o_recv).start()

    def first_half():
        for copy in own_kv[0]:
            copy.wait()
        small[0].wait_recv()
        for copy in far_kv[0]:
            copy.wait_recv()
        bias[0] = bt[0, 0] + btx[0]

    def second_half():
        for copy in small[1:]:
            copy.wait_recv()
        for copy in far_kv[1]:
            copy.wait_recv()
        bias[1] = btx[1] + btx[2]

    line = lax.broadcasted_iota(jnp.int32, (128, 128), 0)

    def cluster_sums():
        lane = lax.rem(lane8, 8 * tiles)
        held = jnp.zeros((8, 128), jnp.int32)
        for h in range(4):
            for side in range(2):
                slab = x if side == 0 else 1 - x
                for t in range(tiles):
                    held = jnp.where(
                        lane == (h * 2 + side) * tiles + t, ids_ref[2 * h + slab, t], held)
        held = jnp.concatenate([held] * 16, axis=0)
        column = lax.broadcasted_iota(jnp.int32, (128, 128), 1)
        belongs = (held == line // 8) & (lax.rem(line, 8) == column // (2 * tiles))
        ts_copy.wait_recv()
        all_sums = jnp.concatenate(
            [ts_buf[0].reshape(8, tiles, DH), ts_rx[...].reshape(8, tiles, DH)], axis=1
        ).reshape(16 * tiles, DH)
        clustered = jnp.dot(
            jnp.where(belongs, 1.0, 0.0), all_sums, precision=highest,
            preferred_element_type=jnp.float32)
        cs_buf[...] = clustered.reshape(clus, 8, DH)
        cs_rx[i] = cs_buf[i]
        lax.fori_loop(1, clus, start_cs, 0)

    def cs_copy(k):
        other = lax.rem(i + k, clus)
        return remote(cs_buf.at[other], cs_rx.at[i], cs_send, cs_recv, (x, other))

    def start_cs(k, carry):
        cs_copy(k).start()
        return carry

    def tot_copy(k):
        return remote(red_buf, tot_rx.at[i], tot_send, tot_recv, (x, lax.rem(i + k, clus)))

    def start_tot(k, carry):
        tot_copy(k).start()
        return carry

    def take_all(buf, amount, sem):
        part = buf.at[pl.ds(0, amount)]
        pltpu.make_async_copy(part, part, sem).wait()

    def reduce_sums():
        take_all(cs_rx, clus - 1, cs_recv)
        reduced = jnp.sum(cs_rx[...], axis=0)
        red_buf[...] = reduced
        tot_rx[i] = reduced
        lax.fori_loop(1, clus, start_tot, 0)

    hooks = (
        (0, first_half), (1, tile_sums), (2, second_half), (2, cluster_sums), (3, reduce_sums))

    def step(n, carry):
        half, pair = n // 2, lax.rem(n + far, 2)
        for number, work in hooks:
            pl.when(n == number)(work)

        blank = jnp.zeros((16, 128), jnp.float32)
        stats = (blank, blank)
        for hh in range(2):
            stats = attend(half, pair, hh, stats)
        for m in range(2):
            packed = stats[m].astype(jnp.bfloat16)
            for j in range(4):
                o_buf[half * clus + pair * 8 + m * 4 + j, 64:80, :] = packed

        def one_dest(k, inner):
            ship(half, pair * 8 + lax.rem(k + i, 8))
            return inner

        lax.fori_loop(0, 8, one_dest, 0)
        return carry

    lax.fori_loop(0, 4, step, 0)
    take_all(tot_rx, clus - 1, tot_recv)
    block, part = i // 4, lax.rem(i, 4)
    share = pl.ds(pl.multiple_of(part * 32, 32), 32)
    totals = tot_rx[...].reshape(clus * 8, DH)
    approx_parts = []
    for h in range(4):
        taken = q_ref[pl.ds(pl.multiple_of(block * QBLK, QBLK), QBLK), h * wide : (h + 1) * wide]
        queries = regroup(taken).astype(jnp.float32)
        approx = lax.dot_general(
            totals, queries, nt, precision=highest, preferred_element_type=jnp.float32)
        usable = lax.rem(line, 8) == h
        for l in range(listing):
            usable = usable & (line // 8 != listed_ref[h, block, l])
        approx = jnp.where(usable, approx * (log2_scale / count), dead)
        top = jnp.max(approx, axis=0, keepdims=True)
        approx_weight = jnp.where(usable, jnp.exp2(approx - top), 0.0)
        total = count * jnp.sum(approx_weight, axis=0, keepdims=True)
        wt[h] = pltpu.roll(approx_weight, 4, 0).T
        numer = jnp.dot(
            wt[h, share, :], totals, precision=highest, preferred_element_type=jnp.float32)
        approx_parts.append((top, total, numer))

    take_all(o_rx, 2, o_recv)
    for h in range(4):
        p, hh = h // 2, h % 2
        held = o_rx[p, :, 64:80, :].astype(jnp.float32)
        tops, sums = held[:, 3 * hh, :], held[:, 3 * hh + 1, :] + held[:, 3 * hh + 2, :]
        approx_top, approx_total, _ = approx_parts[h]
        top = jnp.maximum(jnp.max(tops, axis=0, keepdims=True), approx_top)
        factor = jnp.exp2(tops - top)
        approx_factor = jnp.exp2(approx_top - top)
        total = jnp.sum(factor * sums, axis=0, keepdims=True) + approx_factor * approx_total
        inverse = 1.0 / total
        mixed = jnp.concatenate(
            [factor * inverse, jnp.broadcast_to(approx_factor * inverse, (8, 128)),
             jnp.zeros((104, 128), jnp.float32)], axis=0)
        wt[4 + h] = mixed.T
    for h in range(4):
        p, hh = h // 2, h % 2
        mine = wt[4 + h, share, :]
        numer = mine[:, 2 * chips : 2 * chips + 1] * approx_parts[h][2]
        for source in range(2 * chips):
            numer = numer + mine[:, source : source + 1] * o_rx[p, source, 32 * hh : 32 * (hh + 1), :].astype(jnp.float32)
        out_ref[h] = numer.astype(jnp.bfloat16)

    for copy in small + far_kv[0] + far_kv[1] + [ts_copy]:
        copy.wait_send()

    take_all(cs_buf, clus - 1, cs_send)
    take_all(tot_rx, clus - 1, tot_send)
    take_all(o_buf, 2 * clus - 1, o_send)


def fast_local(key_cache, value_cache, prompt_queries, tile_cluster, listed_clusters):
    clus = lax.axis_size("clus")
    _, rows, width = key_cache.shape
    tiles = rows // TILE
    query_count = prompt_queries.shape[0]
    heads = prompt_queries.shape[1] // (GROUP * DH)
    blocks = query_count // QBLK
    dma = pltpu.SemaphoreType.DMA
    f32, bf16 = jnp.float32, jnp.bfloat16
    share = query_count * GROUP // clus
    vmem = pl.BlockSpec(memory_space=pltpu.VMEM)
    smem = pl.BlockSpec(memory_space=pltpu.SMEM)
    hbm = pl.BlockSpec(memory_space=pltpu.HBM)
    out = pl.pallas_call(
        fast_kernel,
        out_shape=jax.ShapeDtypeStruct((heads, share, DH), bf16),
        in_specs=[hbm, hbm, vmem, smem, smem],
        out_specs=vmem,
        scratch_shapes=[
            pltpu.VMEM((2, 2, 2 * rows, DH), bf16),
            pltpu.VMEM((2, 2, 2 * rows, DH), bf16),
            pltpu.VMEM((2, 2, rows, DH), bf16),
            pltpu.VMEM((2, 2, rows, DH), bf16),
            pltpu.VMEM((2, 2, query_count * GROUP, DH), bf16),
            pltpu.VMEM((2, 2, 2 * blocks, 128), f32),
            pltpu.VMEM((3, 2 * blocks, 128), f32),
            pltpu.VMEM((2, 2 * blocks, 128), f32),
            pltpu.VMEM((2 * clus, 2 * share + 16, DH), bf16),
            pltpu.VMEM((2, clus, 2 * share + 16, DH), bf16),
            pltpu.VMEM((2, 2, heads, tiles, DH), f32),
            pltpu.VMEM((2, heads, tiles, DH), f32),
            pltpu.VMEM((clus, 8, DH), f32),
            pltpu.VMEM((clus, 8, DH), f32),
            pltpu.VMEM((8, DH), f32),
            pltpu.VMEM((clus, 8, DH), f32),
            pltpu.VMEM((8, 128, 128), f32),
            pltpu.VMEM((2 * rows, 128), bf16),
            dma((2, 8)), dma((8,)), dma((8,)), dma((4,)), dma((4,)),
            dma, dma, dma((2,)), dma, dma, dma, dma,
        ],
        compiler_params=pltpu.CompilerParams(
            collective_id=0, has_side_effects=True, vmem_limit_bytes=56 * 1024 * 1024),
    )(
        key_cache.reshape(rows, width), value_cache.reshape(rows, width),
        prompt_queries, tile_cluster.reshape(2 * heads, tiles), listed_clusters,
    )
    out = out.reshape(heads, query_count // clus, GROUP, DH).transpose(1, 0, 2, 3)
    return out.reshape(query_count // clus, heads * GROUP * DH)


def solution(mesh):
    placed = (
        P("head", "clus", None),
        P("head", "clus", None),
        P(None, "head"),
        P("head", "clus", None, None, None),
        P("head", None, None),
    )
    fits = mesh.shape["head"] == 2 and mesh.shape["clus"] == 16
    return jax.shard_map(
        fast_local if fits else local,
        mesh=mesh,
        in_specs=placed,
        out_specs=P("clus", "head"),
        check_vma=False,
    )
```

```python
import functools
import math

import jax
import jax.numpy as jnp
from jax import lax
from jax.experimental import pallas as pl
from jax.experimental.pallas import tpu as pltpu
from jax.sharding import PartitionSpec as P

DH = 128
GROUP = 8
TILE = 128
QBLK = 16


floor_value = -1e30
highest = lax.Precision.HIGHEST


def combined_all(shard, axis, combine):
    everything = jax.tree.map(lambda part: lax.all_gather(part, axis), shard)
    leading = jax.tree.map(lambda part: part[0], everything)

    def turn(k, so_far):
        return combine(so_far, jax.tree.map(lambda part: part[k], everything))

    return lax.fori_loop(1, lax.axis_size(axis), turn, leading)


def block_partials(
    query_blocks, key_rows, value_rows, tile_mask, key_mean, value_sum, counts_mine, approx_on
):
    score_scale = key_rows.shape[-1] ** (-0.5)
    tile_rows = key_rows.shape[0] // tile_mask.shape[-1]

    def one_block(block_inputs):
        block_queries, mask_tiles, approx_flag = block_inputs
        key_mask = jnp.repeat(mask_tiles, tile_rows) > 0.5
        scores = (
            jnp.einsum("rd,kd->rk", block_queries, key_rows, preferred_element_type=jnp.float32)
            * score_scale
        )
        approx_score = (
            jnp.dot(block_queries.astype(jnp.float32), key_mean, precision=highest) * score_scale
        )
        approx_live = approx_flag > 0.5
        row_top = jnp.maximum(
            jnp.max(jnp.where(key_mask[None, :], scores, floor_value), axis=1),
            jnp.where(approx_live, approx_score, floor_value),
        )
        weights = jnp.where(key_mask[None, :], jnp.exp(scores - row_top[:, None]), 0.0)
        probabilities = weights.astype(jnp.bfloat16)
        approx_weight = jnp.where(approx_live, jnp.exp(approx_score - row_top), 0.0)
        row_total = jnp.sum(weights, axis=1) + counts_mine * approx_weight
        numerator = jnp.dot(probabilities, value_rows, preferred_element_type=jnp.float32)
        numerator = numerator + approx_weight[:, None] * value_sum[None, :]
        return (row_top, row_total, numerator)

    return lax.map(one_block, (query_blocks, tile_mask, approx_on))


def combine_parts(first_part, second_part):
    top_first, total_first, numer_first = first_part
    top_second, total_second, numer_second = second_part
    joined = jnp.maximum(top_first, top_second)
    factor_first = jnp.exp(top_first - joined)
    factor_second = jnp.exp(top_second - joined)
    return (
        joined,
        total_first * factor_first + total_second * factor_second,
        numer_first * factor_first[..., None] + numer_second * factor_second[..., None],
    )


def local(key_cache, value_cache, prompt_queries, tile_cluster, listed_clusters):
    owners = lax.axis_size("clus")
    owner_index = lax.axis_index("clus")
    moved_keys, moved_values = (
        lax.all_to_all(key_cache, "head", split_axis=2, concat_axis=0, tiled=True),
        lax.all_to_all(value_cache, "head", split_axis=2, concat_axis=0, tiled=True),
    )
    slab_count, slab_rows, feature_width = moved_keys.shape
    heads_dev = feature_width // DH
    tiles_dev = slab_count * slab_rows // TILE

    def to_tiles(moved):
        shaped = moved.reshape(slab_count, slab_rows // TILE, TILE, heads_dev, DH)
        return shaped.transpose(3, 0, 1, 2, 4).reshape(heads_dev, tiles_dev, TILE, DH)

    key_tiles = to_tiles(moved_keys)
    value_tiles = to_tiles(moved_values)
    cluster_ids = tile_cluster.reshape(heads_dev, tiles_dev)
    column_ids = jnp.arange(owners, dtype=jnp.int32)
    member = (cluster_ids[:, :, None] == column_ids[None, None, :]).astype(jnp.float32)
    listed_mask = jnp.max(
        (listed_clusters[:, :, :, None] == column_ids).astype(jnp.float32), axis=2
    )
    owner_hot = (column_ids == owner_index).astype(jnp.float32)
    mine_listed = jnp.einsum("hbc,c->hb", listed_mask, owner_hot, precision=highest)
    query_count = prompt_queries.shape[0]
    block_count = query_count // QBLK
    query_blocks = prompt_queries.reshape(query_count, heads_dev, GROUP, DH).transpose(1, 0, 2, 3)
    query_blocks = query_blocks.reshape(heads_dev, block_count, QBLK * GROUP, DH)
    key_rows = key_tiles.reshape(heads_dev, tiles_dev * TILE, DH)
    value_rows = value_tiles.reshape(heads_dev, tiles_dev * TILE, DH)
    unit_rows = jnp.ones((TILE,), jnp.bfloat16)
    tile_keys = jnp.einsum("htrd,r->htd", key_tiles, unit_rows, preferred_element_type=jnp.float32)
    tile_values = jnp.einsum(
        "htrd,r->htd", value_tiles, unit_rows, preferred_element_type=jnp.float32
    )
    local_keys = jnp.einsum("htc,htd->hcd", member, tile_keys, precision=highest)
    local_values = jnp.einsum("htc,htd->hcd", member, tile_values, precision=highest)
    local_counts = TILE * jnp.sum(member, axis=1)
    total_keys, total_values, total_counts = lax.psum(
        (local_keys, local_values, local_counts), "clus"
    )
    key_sum = jnp.einsum("hcd,c->hd", total_keys, owner_hot, precision=highest)
    value_sum = jnp.einsum("hcd,c->hd", total_values, owner_hot, precision=highest)
    counts_mine = jnp.einsum("hc,c->h", total_counts, owner_hot, precision=highest)
    tile_mask = jnp.einsum("hbc,htc->hbt", listed_mask, member, precision=highest)
    key_mean = key_sum / jnp.maximum(counts_mine, 1.0)[:, None]
    approx_on = (1.0 - mine_listed) * (counts_mine > 0.5).astype(jnp.float32)[:, None]
    row_top, row_total, numerator = jax.vmap(block_partials)(
        query_blocks, key_rows, value_rows, tile_mask, key_mean, value_sum, counts_mine, approx_on
    )
    row_top = row_top.reshape(heads_dev, query_count, GROUP)
    row_total = row_total.reshape(heads_dev, query_count, GROUP)
    numerator = numerator.reshape(heads_dev, query_count, GROUP, DH)
    share_rows = query_count // owners
    merged_top, merged_total, merged_numer = combined_all(
        (row_top, row_total, numerator), "clus", combine_parts
    )
    kept_total = lax.dynamic_slice_in_dim(merged_total, owner_index * share_rows, share_rows, 1)
    kept_numer = lax.dynamic_slice_in_dim(merged_numer, owner_index * share_rows, share_rows, 1)
    attended = kept_numer / kept_total[..., None]
    return (
        attended.transpose(1, 0, 2, 3)
        .reshape(share_rows, heads_dev * GROUP * DH)
        .astype(jnp.bfloat16)
    )


MESH = pl.DeviceIdType.MESH
dead = -1e30
lowest_top = -1e9
log2_scale = math.log2(math.e) * DH**-0.5
nt = (((1,), (1,)), ((), ()))


def fast_kernel(
    k_hbm, v_hbm, q_ref, ids_ref, listed_ref, out_ref,
    kbuf, vbuf, kout, vout, qall, bt, btx, bias, o_buf, o_rx,
    ts_buf, ts_rx, cs_buf, cs_rx, red_buf, tot_rx, wt, hot_ref,
    loc_sem, kv_send, kv_recv, in_send, in_recv,
    o_send, o_recv, ts_sem, cs_send, cs_recv, tot_send, tot_recv,
):
    x, i = lax.axis_index("head"), lax.axis_index("clus")
    clus = lax.axis_size("clus")
    chips = clus // 2
    c, w = lax.rem(i, 2), i // 2
    sib = i + 1 - 2 * c
    slot = x * chips + w
    rows = k_hbm.shape[0]
    tiles = rows // TILE
    count = float(clus * TILE)
    wide = GROUP * DH
    span = 2 * QBLK * GROUP
    far = jnp.where(i < chips, 1, 0)
    listing = listed_ref.shape[2]

    def pair_of(half, core):
        return 2 * (x if half == 0 else 1 - x) + core

    def kv_copies(half, kind):
        copies = []
        for hh in range(2):
            for n, (src, dst, out) in enumerate(((k_hbm, kbuf, kout), (v_hbm, vbuf, vout))):
                number = half * 4 + hh * 2 + n
                pair = pair_of(half, c if kind == 0 else 1 - c)
                column = pl.ds(pl.multiple_of((pair * 2 + hh) * DH, DH), DH)
                if kind == 0:
                    copies.append(pltpu.make_async_copy(
                        src.at[:, column], dst.at[half, hh, pl.ds(0, rows)], loc_sem.at[0, number]))
                elif kind == 1:
                    copies.append(pltpu.make_async_copy(
                        src.at[:, column], out.at[half, hh], loc_sem.at[1, number]))
                else:
                    copies.append(pltpu.make_async_remote_copy(
                        src_ref=src.at[:, column], dst_ref=dst.at[half, hh, pl.ds(rows, rows)],
                        send_sem=kv_send.at[number], recv_sem=kv_recv.at[number],
                        device_id=(x, sib), device_id_type=MESH))
        return copies

    def remote(src, dst, send_sem, recv_sem, device):
        return pltpu.make_async_remote_copy(
            src_ref=src, dst_ref=dst, send_sem=send_sem, recv_sem=recv_sem,
            device_id=device, device_id_type=MESH)

    own_kv = [kv_copies(0, 0), kv_copies(1, 0)]
    out_kv = [kv_copies(0, 1), kv_copies(1, 1)]
    far_kv = [kv_copies(0, 2), kv_copies(1, 2)]
    for copy in own_kv[0] + own_kv[1] + out_kv[0] + out_kv[1]:
        copy.start()

    barrier = pltpu.get_barrier_semaphore()

    def ahead(k):
        return jnp.where(i + k >= clus, i + k - clus, i + k)

    def greet(side, k):
        pl.semaphore_signal(barrier, inc=1, device_id=(side, ahead(k)), device_id_type=MESH)

    for k in range(clus):
        greet(1 - x, k)
        if k > 0:
            greet(x, k)

    lane8 = lax.broadcasted_iota(jnp.int32, (8, 128), 1)
    sub8 = lax.broadcasted_iota(jnp.int32, (8, 128), 0)
    for turn in range(2):
        pair = c if turn == 0 else 1 - c
        named = []
        for l in range(listing):
            table = jnp.zeros((8, 128), jnp.int32)
            for hh in range(2):
                for b in range(4):
                    table = jnp.where(sub8 == hh * 4 + b, listed_ref[2 * pair + hh, b, l], table)
            named.append(table)
        first = turn * tiles
        for side in range(2):
            slab = x if side == 0 else 1 - x
            held = jnp.full((8, 128), -1, jnp.int32)
            for hh in range(2):
                for t in range(tiles):
                    here = (lane8 == first + t) & (sub8 // 4 == hh)
                    held = jnp.where(here, ids_ref[2 * (2 * pair + hh) + slab, t], held)
            live = (lane8 < first) | (lane8 >= first + tiles)
            for table in named:
                live = live | (held == table)
            bt[side, turn] = jnp.where(live, 0.0, dead)

    pl.semaphore_wait(barrier, 2 * clus - 1)
    small = [
        remote(bt.at[0, 1], btx.at[0], in_send.at[0], in_recv.at[0], (x, sib)),
        remote(bt.at[1, 0], btx.at[1], in_send.at[1], in_recv.at[1], (1 - x, i)),
        remote(bt.at[1, 1], btx.at[2], in_send.at[2], in_recv.at[2], (1 - x, sib)),
        remote(qall.at[0], qall.at[1], in_send.at[3], in_recv.at[3], (1 - x, i)),
    ]
    for copy in far_kv[0] + small[:3] + far_kv[1]:
        copy.start()

    key_tile = lax.broadcasted_iota(jnp.int32, (2 * rows, 128), 0) // TILE
    hot = key_tile == lax.broadcasted_iota(jnp.int32, (2 * rows, 128), 1)
    hot_ref[...] = jnp.where(hot, 1.0, 0.0).astype(jnp.bfloat16)

    def regroup(rows_in):
        count_in = rows_in.shape[0]
        split = rows_in.astype(jnp.float32).reshape(count_in, GROUP, DH)
        return split.reshape(count_in * GROUP, DH).astype(jnp.bfloat16)

    def place_queries(first):
        def block_of(n, carry):
            hh, block = n // 4, lax.rem(n, 4)
            for head in range(2):
                @pl.when(hh == head)
                def _():
                    columns = pl.ds(pl.multiple_of(first + head * wide, 128), wide)
                    taken = q_ref[pl.ds(pl.multiple_of(block * QBLK, QBLK), QBLK), columns]
                    qall[0, head, pl.ds(pl.multiple_of(block * 128, 128), 128), :] = regroup(
                        taken)
            return carry

        lax.fori_loop(0, 8, block_of, 0)

    place_queries(c * 2 * wide)

    small[3].start()

    ts_copy = remote(ts_buf.at[1], ts_rx, ts_sem.at[0], ts_sem.at[1], (1 - x, i))

    def tile_sums():
        for copy in own_kv[1] + out_kv[0] + out_kv[1]:
            copy.wait()

        def add_up(n, carry):
            half, hh = n // 2, lax.rem(n, 2)
            for m, (buf, out) in enumerate(((kbuf, kout), (vbuf, vout))):
                for part, core in ((buf[half, hh, :rows], c), (out[half, hh], 1 - c)):
                    ts_buf[half, m, 2 * core + hh] = jnp.sum(
                        part.astype(jnp.float32).reshape(tiles, TILE, DH), axis=1)
            return carry

        lax.fori_loop(0, 4, add_up, 0)
        ts_copy.start()

    square = lax.broadcasted_iota(jnp.int32, (128, 128), 0) == lax.broadcasted_iota(
        jnp.int32, (128, 128), 1)

    def as_row(column):
        return jnp.sum(jnp.where(square, column, 0.0), axis=0, keepdims=True)

    sub16 = lax.broadcasted_iota(jnp.int32, (16, 128), 0)

    def attend(half, pair, hh, stats):
        start = pl.multiple_of(pair * span, span)
        masks = [
            jnp.broadcast_to(bias[half, pl.ds(hh * 4 + pair * 2 + n, 1), :], (128, 128))
            for n in range(2)
        ]
        masks = jnp.concatenate(masks, axis=0).astype(jnp.bfloat16)
        queries = jnp.concatenate([qall[half, hh, pl.ds(start, span), :], masks], axis=1)
        keys = jnp.concatenate([kbuf[half, hh], hot_ref[...]], axis=1)
        scores = lax.dot_general(queries, keys, nt, preferred_element_type=jnp.float32)
        top = jnp.maximum(jnp.max(scores, axis=1, keepdims=True), lowest_top) * log2_scale
        top = top.astype(jnp.bfloat16).astype(jnp.float32)
        weights = jnp.exp2(scores * log2_scale - top).astype(jnp.bfloat16)
        values = jnp.concatenate(
            [vbuf[half, hh], jnp.ones((2 * rows, 128), jnp.bfloat16)], axis=1)
        numer = jnp.dot(weights, values, preferred_element_type=jnp.float32)
        after = []
        for n in range(2):
            part = slice(128 * n, 128 * (n + 1))
            total = as_row(numer[part, DH:])
            upper = total.astype(jnp.bfloat16).astype(jnp.float32)
            held = stats[n]
            for r, row in enumerate((as_row(top[part]), upper, total - upper)):
                held = jnp.where(sub16 == hh * 3 + r, row, held)
            after.append(held)
            for j in range(4):
                first = 128 * n + 32 * j
                place = pl.ds(hh * 32, 32)
                o_buf[half * clus + pair * 8 + n * 4 + j, place, :] = numer[
                    first : first + 32, :DH].astype(jnp.bfloat16)
        return tuple(after)

    def ship(half, dest):
        src = o_buf.at[half * clus + dest]
        here = (half == 0) & (dest == i)

        @pl.when(jnp.logical_not(here))
        def _():
            remote(src, o_rx.at[c, slot], o_send, o_recv, (x + half * (1 - 2 * x), dest)).start()

        @pl.when(here)
        def _():
            pltpu.make_async_copy(src, o_rx.at[c, slot], o_recv).start()

    def first_half():
        for copy in own_kv[0]:
            copy.wait()
        small[0].wait_recv()
        for copy in far_kv[0]:
            copy.wait_recv()
        bias[0] = bt[0, 0] + btx[0]

    def second_half():
        for copy in small[1:]:
            copy.wait_recv()
        for copy in far_kv[1]:
            copy.wait_recv()
        bias[1] = btx[1] + btx[2]

    line = lax.broadcasted_iota(jnp.int32, (128, 128), 0)

    def cluster_sums():
        lane = lax.rem(lane8, 8 * tiles)
        held = jnp.zeros((8, 128), jnp.int32)
        for h in range(4):
            for side in range(2):
                slab = x if side == 0 else 1 - x
                for t in range(tiles):
                    held = jnp.where(
                        lane == (h * 2 + side) * tiles + t, ids_ref[2 * h + slab, t], held)
        held = jnp.concatenate([held] * 16, axis=0)
        column = lax.broadcasted_iota(jnp.int32, (128, 128), 1)
        belongs = (held == line // 8) & (lax.rem(line, 8) == column // (2 * tiles))
        ts_copy.wait_recv()
        all_sums = jnp.concatenate(
            [ts_buf[0].reshape(8, tiles, DH), ts_rx[...].reshape(8, tiles, DH)], axis=1
        ).reshape(16 * tiles, DH)
        clustered = jnp.dot(
            jnp.where(belongs, 1.0, 0.0), all_sums, precision=highest,
            preferred_element_type=jnp.float32)
        cs_buf[...] = clustered.reshape(clus, 8, DH)
        cs_rx[i] = cs_buf[i]
        lax.fori_loop(1, clus, start_cs, 0)

    def cs_copy(k):
        other = lax.rem(i + k, clus)
        return remote(cs_buf.at[other], cs_rx.at[i], cs_send, cs_recv, (x, other))

    def start_cs(k, carry):
        cs_copy(k).start()
        return carry

    def tot_copy(k):
        return remote(red_buf, tot_rx.at[i], tot_send, tot_recv, (x, lax.rem(i + k, clus)))

    def start_tot(k, carry):
        tot_copy(k).start()
        return carry

    def take_all(buf, amount, sem):
        part = buf.at[pl.ds(0, amount)]
        pltpu.make_async_copy(part, part, sem).wait()

    def reduce_sums():
        take_all(cs_rx, clus - 1, cs_recv)
        reduced = jnp.sum(cs_rx[...], axis=0)
        red_buf[...] = reduced
        tot_rx[i] = reduced
        lax.fori_loop(1, clus, start_tot, 0)

    hooks = (
        (0, first_half), (1, tile_sums), (2, second_half), (2, cluster_sums))

    def step(n, carry):
        half, pair = n // 2, lax.rem(n + far, 2)
        for number, work in hooks:
            pl.when(n == number)(work)

        blank = jnp.zeros((16, 128), jnp.float32)
        stats = (blank, blank)
        for hh in range(2):
            stats = attend(half, pair, hh, stats)
        for m in range(2):
            packed = stats[m].astype(jnp.bfloat16)
            for j in range(4):
                o_buf[half * clus + pair * 8 + m * 4 + j, 64:80, :] = packed

        def one_dest(k, inner):
            ship(half, pair * 8 + lax.rem(k + i, 8))
            return inner

        lax.fori_loop(0, 8, one_dest, 0)
        return carry

    lax.fori_loop(0, 4, step, 0)
    reduce_sums()
    take_all(tot_rx, clus - 1, tot_recv)
    block, part = i // 4, lax.rem(i, 4)
    share = pl.ds(pl.multiple_of(part * 32, 32), 32)
    totals = tot_rx[...].reshape(clus * 8, DH)
    approx_parts = []
    for h in range(4):
        taken = q_ref[pl.ds(pl.multiple_of(block * QBLK, QBLK), QBLK), h * wide : (h + 1) * wide]
        queries = regroup(taken).astype(jnp.float32)
        approx = lax.dot_general(
            totals, queries, nt, precision=highest, preferred_element_type=jnp.float32)
        usable = lax.rem(line, 8) == h
        for l in range(listing):
            usable = usable & (line // 8 != listed_ref[h, block, l])
        approx = jnp.where(usable, approx * (log2_scale / count), dead)
        top = jnp.max(approx, axis=0, keepdims=True)
        approx_weight = jnp.where(usable, jnp.exp2(approx - top), 0.0)
        total = count * jnp.sum(approx_weight, axis=0, keepdims=True)
        wt[h] = pltpu.roll(approx_weight, 4, 0).T
        numer = jnp.dot(
            wt[h, share, :], totals, precision=highest, preferred_element_type=jnp.float32)
        approx_parts.append((top, total, numer))

    take_all(o_rx, 2, o_recv)
    for h in range(4):
        p, hh = h // 2, h % 2
        held = o_rx[p, :, 64:80, :].astype(jnp.float32)
        tops, sums = held[:, 3 * hh, :], held[:, 3 * hh + 1, :] + held[:, 3 * hh + 2, :]
        approx_top, approx_total, _ = approx_parts[h]
        top = jnp.maximum(jnp.max(tops, axis=0, keepdims=True), approx_top)
        factor = jnp.exp2(tops - top)
        approx_factor = jnp.exp2(approx_top - top)
        total = jnp.sum(factor * sums, axis=0, keepdims=True) + approx_factor * approx_total
        inverse = 1.0 / total
        mixed = jnp.concatenate(
            [factor * inverse, jnp.broadcast_to(approx_factor * inverse, (8, 128)),
             jnp.zeros((104, 128), jnp.float32)], axis=0)
        wt[4 + h] = mixed.T
    for h in range(4):
        p, hh = h // 2, h % 2
        mine = wt[4 + h, share, :]
        numer = mine[:, 2 * chips : 2 * chips + 1] * approx_parts[h][2]
        for source in range(2 * chips):
            numer = numer + mine[:, source : source + 1] * o_rx[p, source, 32 * hh : 32 * (hh + 1), :].astype(jnp.float32)
        out_ref[h] = numer.astype(jnp.bfloat16)

    for copy in small + far_kv[0] + far_kv[1] + [ts_copy]:
        copy.wait_send()

    take_all(cs_buf, clus - 1, cs_send)
    take_all(tot_rx, clus - 1, tot_send)
    take_all(o_buf, 2 * clus - 1, o_send)


def fast_local(key_cache, value_cache, prompt_queries, tile_cluster, listed_clusters):
    clus = lax.axis_size("clus")
    _, rows, width = key_cache.shape
    tiles = rows // TILE
    query_count = prompt_queries.shape[0]
    heads = prompt_queries.shape[1] // (GROUP * DH)
    blocks = query_count // QBLK
    dma = pltpu.SemaphoreType.DMA
    f32, bf16 = jnp.float32, jnp.bfloat16
    share = query_count * GROUP // clus
    vmem = pl.BlockSpec(memory_space=pltpu.VMEM)
    smem = pl.BlockSpec(memory_space=pltpu.SMEM)
    hbm = pl.BlockSpec(memory_space=pltpu.HBM)
    out = pl.pallas_call(
        fast_kernel,
        out_shape=jax.ShapeDtypeStruct((heads, share, DH), bf16),
        in_specs=[hbm, hbm, vmem, smem, smem],
        out_specs=vmem,
        scratch_shapes=[
            pltpu.VMEM((2, 2, 2 * rows, DH), bf16),
            pltpu.VMEM((2, 2, 2 * rows, DH), bf16),
            pltpu.VMEM((2, 2, rows, DH), bf16),
            pltpu.VMEM((2, 2, rows, DH), bf16),
            pltpu.VMEM((2, 2, query_count * GROUP, DH), bf16),
            pltpu.VMEM((2, 2, 2 * blocks, 128), f32),
            pltpu.VMEM((3, 2 * blocks, 128), f32),
            pltpu.VMEM((2, 2 * blocks, 128), f32),
            pltpu.VMEM((2 * clus, 2 * share + 16, DH), bf16),
            pltpu.VMEM((2, clus, 2 * share + 16, DH), bf16),
            pltpu.VMEM((2, 2, heads, tiles, DH), f32),
            pltpu.VMEM((2, heads, tiles, DH), f32),
            pltpu.VMEM((clus, 8, DH), f32),
            pltpu.VMEM((clus, 8, DH), f32),
            pltpu.VMEM((8, DH), f32),
            pltpu.VMEM((clus, 8, DH), f32),
            pltpu.VMEM((8, 128, 128), f32),
            pltpu.VMEM((2 * rows, 128), bf16),
            dma((2, 8)), dma((8,)), dma((8,)), dma((4,)), dma((4,)),
            dma, dma, dma((2,)), dma, dma, dma, dma,
        ],
        compiler_params=pltpu.CompilerParams(
            collective_id=0, has_side_effects=True, vmem_limit_bytes=56 * 1024 * 1024),
    )(
        key_cache.reshape(rows, width), value_cache.reshape(rows, width),
        prompt_queries, tile_cluster.reshape(2 * heads, tiles), listed_clusters,
    )
    out = out.reshape(heads, query_count // clus, GROUP, DH).transpose(1, 0, 2, 3)
    return out.reshape(query_count // clus, heads * GROUP * DH)


def solution(mesh):
    placed = (
        P("head", "clus", None),
        P("head", "clus", None),
        P(None, "head"),
        P("head", "clus", None, None, None),
        P("head", None, None),
    )
    fits = mesh.shape["head"] == 2 and mesh.shape["clus"] == 16
    return jax.shard_map(
        fast_local if fits else local,
        mesh=mesh,
        in_specs=placed,
        out_specs=P("clus", "head"),
        check_vma=False,
    )
```
